32 devices in a mesh: dp: 4 (over z), ctx: 4 (over x, core), expert: 2 (over y).
Axes of the slice: x: 2, y: 2, z: 4, core: 2. Of those that a mesh axis runs over, the one named last changes fastest.
Arguments:
- tokens: bfloat16 [8, 2048, 768], P(('dp', 'expert'), 'ctx'), may hold values from -6 to 6
- cotangent: bfloat16 [8, 2048, 768], P(('dp', 'expert'), 'ctx'), may hold values from -6 to 6
- routes: int32 [8, 2048, 1], P(('dp', 'expert'), 'ctx'), may hold values from 0 to 3, as said below
- norm1_gain: float32 [768], replicated, may hold values from 0.5 to 1.5
- w_query: bfloat16 [768, 768], replicated, may hold values from -0.21875 to 0.21875
- w_key: bfloat16 [768, 768], replicated, may hold values from -0.21875 to 0.21875
- w_value: bfloat16 [768, 768], replicated, may hold values from -0.21875 to 0.21875
- w_output: bfloat16 [768, 768], replicated, may hold values from -1.75 to 1.75
- norm2_gain: float32 [768], replicated, may hold values from 0.5 to 1.5
- w_router: bfloat16 [768, 4], replicated, may hold values from -0.15625 to 0.15625
- w_in: bfloat16 [4, 768, 3072], P('expert'), may hold values from -0.21875 to 0.21875
- w_out: bfloat16 [4, 3072, 768], P('expert'), may hold values from -0.21875 to 0.21875
Outputs:
- output: bfloat16 [8, 2048, 768], P(('dp', 'expert'), 'ctx')
- grad_tokens: float32 [8, 2048, 768], P(('dp', 'expert'), 'ctx')
- grad_norm1: float32 [768], replicated
- grad_query: float32 [768, 768], replicated
- grad_key: float32 [768, 768], replicated
- grad_value: float32 [768, 768], replicated
- grad_output: float32 [768, 768], replicated
- grad_norm2: float32 [768], replicated
- grad_router: float32 [768, 4], replicated
- grad_in: float32 [4, 768, 3072], P('expert', None, ('dp', 'ctx'))
- grad_out: float32 [4, 3072, 768], P('expert', ('dp', 'ctx'))
- balance: float32 [], replicated
The draws below stay inside these ranges and needn't reach their ends.
Inputs may be any that keep to these rules, and one draw needn't show every extreme that they name: `routes`: among the tokens of one device (an aligned block of 512 positions of one sequence) no expert is chosen more than 256 times, and in every such block some expert is chosen exactly 256 times.
All inputs are finite; a program needn't handle non-finite values.
Results may differ from the reference program's by a relative error of at most 0.024.
Values may be sent and summed in bfloat16 or wider, within the bound.
No kernel may reach another device: no remote copies, remote signals or barrier semaphores. Data moves between devices by JAX's collectives and lax.ppermute only.
A program may use at most 192 MiB of HBM per device.

```python
import jax
import jax.numpy as jnp
from jax import lax

D = 768
HEADS = 12
HEAD_DIM = 64
FF = 3072
LEN_DEV = 512
EXPERTS = 4
SEQS = 8
SEQ_LEN = 2048
TOKENS = 16384
CAP = 256


def draw_routes(key, part):
    key = jax.random.fold_in(key, 11)
    blocks = SEQ_LEN // LEN_DEV
    capacity_position_matrix = 2 * LEN_DEV
    slot_expert = jnp.arange(capacity_position_matrix, dtype=jnp.int32) // CAP
    window = max(EXPERTS // 4, 1)

    def one_block(index):
        sequence = index // blocks
        sub = jax.random.fold_in(key, index)
        first_key, latter_prng_seed, third_key = jax.random.split(sub, 3)
        shift = sequence * EXPERTS // SEQS
        offset = (slot_expert - shift) % EXPERTS
        preferred_specialist = (offset < window).astype(jnp.int32)
        argmax_specialist = (offset == 0).astype(jnp.int32)
        drawn_affinities = jax.random.randint(first_key, (capacity_position_matrix,), 0, 1024, dtype=jnp.int32)
        extra_affinity = jax.random.randint(latter_prng_seed, (capacity_position_matrix,), 0, 2048, dtype=jnp.int32)
        specialist_affinity = drawn_affinities + preferred_specialist * extra_affinity + argmax_specialist * 4096
        distinct = specialist_affinity * capacity_position_matrix + jnp.arange(capacity_position_matrix, dtype=jnp.int32)
        top_values, top_index = lax.top_k(distinct, LEN_DEV)
        chosen = slot_expert[top_index]
        return jax.random.permutation(third_key, chosen)
    rows = jax.vmap(one_block)(jnp.arange(SEQS * blocks, dtype=jnp.int32))
    return rows.reshape(SEQS, SEQ_LEN, 1).astype(jnp.int32)


def level_of(key, shape, shards, least, high):
    def one(position, parts):
        heights = jax.random.uniform(jax.random.fold_in(jax.random.fold_in(key, 6), position), (parts,), jnp.float32, least / len(shards), high / len(shards))
        return jnp.repeat(jnp.exp(heights), shape[position] // parts).reshape((-1,) + (1,) * (len(shape) - position - 1))

    level = one(*shards[0])
    for cut in shards[1:]:
        level = level * one(*cut)
    return level


def normal_values(stream_key, shape, scale, most, pieces=(), held_as=jnp.bfloat16):
    level = level_of(stream_key, shape, pieces, -0.22, 0.18) if pieces else 1.0
    values = jax.random.normal(stream_key, shape, jnp.float32) * scale * level
    return jnp.minimum(jnp.maximum(values, -most), most).astype(held_as)


def setup_inputs(seed: int = 0) -> dict:
    keys = jax.random.split(jax.random.key(seed), 13)
    tokens = normal_values(keys[0], (SEQS, SEQ_LEN, D), 1.0, 6.0, ((0, 8), (1, 4)))
    cotangent = normal_values(keys[1], (SEQS, SEQ_LEN, D), 1.0, 6.0, ((0, 8), (1, 4)))
    routes = draw_routes(jax.random.fold_in(keys[12], 71), 0)
    norm1_gain = jnp.clip(1.0 + 0.1 * jax.random.normal(keys[3], (D,), jnp.float32), 0.5, 1.5)
    w_query = normal_values(keys[4], (D, D), D ** -0.5, 0.21875)
    w_key = normal_values(keys[5], (D, D), D ** -0.5, 0.21875)
    w_value = normal_values(keys[6], (D, D), D ** -0.5, 0.21875)
    w_output = normal_values(keys[7], (D, D), (max(D // 64, 1)) ** -0.5, 1.75)
    norm2_gain = jnp.clip(1.0 + 0.1 * jax.random.normal(keys[8], (D,), jnp.float32), 0.5, 1.5)
    w_router = normal_values(keys[9], (D, EXPERTS), (2 * D) ** -0.5, 0.15625)
    w_in = normal_values(keys[10], (EXPERTS, D, FF), D ** -0.5, 0.21875, ((0, 2),))
    w_out = normal_values(keys[11], (EXPERTS, FF, D), (FF // 4) ** -0.5, 0.21875, ((0, 2),))
    return dict(tokens=tokens, cotangent=cotangent, routes=routes, norm1_gain=norm1_gain, w_query=w_query, w_key=w_key, w_value=w_value, w_output=w_output, norm2_gain=norm2_gain, w_router=w_router, w_in=w_in, w_out=w_out)


@jax.custom_vjp
def low(v):
    return lax.optimization_barrier(v.astype(jnp.bfloat16)).astype(jnp.float32)

@jax.custom_vjp
def low_back(v):
    return v

def low_keep(v):
    return (low(v), None)

def low_pass(kept, grad):
    return (grad,)

def back_keep(v):
    return (v, None)

def back_low(kept, grad):
    return (low(grad),)
low.defvjp(low_keep, low_pass)
low_back.defvjp(back_keep, back_low)
precise = lax.Precision.HIGHEST
balance_weight = 1.0
norm_eps = 1e-05
masked_score = -1e+30

def layer_norm(inputs, scaling):
    centred = inputs - lax.optimization_barrier(jnp.mean(inputs, axis=-1, keepdims=True))
    spread = lax.optimization_barrier(jnp.mean(centred * centred, axis=-1, keepdims=True))
    return centred * lax.rsqrt(spread + norm_eps) * scaling

def matmul(left, right):
    return jnp.dot(left, right, precision=precise, preferred_element_type=jnp.float32)

def attend_sequence(packed_seq):
    queries, key_rows, value_rows = packed_seq
    length = queries.shape[0]
    block_rows = min(512, length)
    blocks = length // block_rows
    score_scale = HEAD_DIM ** (-0.5)
    key_heads = key_rows.reshape(length, HEADS, HEAD_DIM)
    value_heads = value_rows.reshape(length, HEADS, HEAD_DIM)
    key_place = jnp.arange(length, dtype=jnp.int32)

    @jax.checkpoint
    def one_block(packed):
        query_block, first_row = packed
        query_heads = query_block.reshape(block_rows, HEADS, HEAD_DIM)
        scores = jnp.einsum('qhd,khd->hqk', query_heads, key_heads, precision=precise) * score_scale
        scores = low_back(scores)
        query_place = first_row + jnp.arange(block_rows, dtype=jnp.int32)
        allowed = key_place[None, :] <= query_place[:, None]
        scores = jnp.where(allowed[None], scores, masked_score)
        probabilities = low(jax.nn.softmax(scores, axis=-1))
        mixed = jnp.einsum('hqk,khd->qhd', probabilities, value_heads, precision=precise)
        return mixed.reshape(block_rows, HEADS * HEAD_DIM)
    starts = jnp.arange(blocks, dtype=jnp.int32) * block_rows
    outputs = lax.map(one_block, (queries.reshape(blocks, block_rows, -1), starts))
    return outputs.reshape(length, -1)

def run_experts(rows, route_flat, in_weight, out_weight):
    total = rows.shape[0]
    row_bound = CAP * (total // LEN_DEV)

    def one_expert(result, expert):
        chosen = jnp.nonzero(route_flat == expert, size=row_bound, fill_value=0)[0].astype(jnp.int32)
        live_rows = (jnp.arange(row_bound, dtype=jnp.int32) < jnp.sum((route_flat == expert).astype(jnp.int32))).astype(rows.dtype)
        picked = rows[chosen]
        hidden = low_back(matmul(picked, in_weight[expert]))
        active = low(jax.nn.gelu(hidden))
        produced = low(low_back(matmul(active, out_weight[expert])))
        return (result.at[chosen].add(produced * live_rows[:, None]), None)
    result, unused = lax.scan(jax.checkpoint(one_expert), jnp.zeros_like(rows), jnp.arange(EXPERTS, dtype=jnp.int32))
    return result

def reference(tokens, cotangent, routes, norm1_gain, w_query, w_key, w_value, w_output, norm2_gain, w_router, w_in, w_out):
    route_flat = routes.reshape(-1).astype(jnp.int32)
    one_hot = (route_flat[:, None] == jnp.arange(EXPERTS, dtype=jnp.int32)[None, :]).astype(jnp.float32)
    counts = lax.optimization_barrier(jnp.sum(one_hot, axis=0))
    mean_load = TOKENS / EXPERTS

    def forward(inputs, gain_one, q_weight, k_weight, v_weight, o_weight, gain_two, r_weight, in_weight, out_weight):
        flat_in = inputs.reshape(-1, D)
        normed = low(layer_norm(flat_in, gain_one))
        queries = low(low_back(matmul(normed, q_weight)))
        key_rows = low(low_back(matmul(normed, k_weight)))
        value_rows = low(low_back(matmul(normed, v_weight)))
        attended = lax.map(attend_sequence, (queries.reshape(SEQS, SEQ_LEN, D), key_rows.reshape(SEQS, SEQ_LEN, D), value_rows.reshape(SEQS, SEQ_LEN, D)))
        attended = low(low_back(attended.reshape(-1, D)))
        branch = low_back(matmul(attended, o_weight))
        middle = flat_in + branch
        second = low(layer_norm(middle, gain_two))
        logits = low_back(matmul(second, r_weight))
        gating = jax.nn.sigmoid(lax.optimization_barrier(jnp.sum(one_hot * logits, axis=1)))
        expert_out = run_experts(low_back(second), route_flat, in_weight, out_weight)
        result = middle + gating[:, None] * expert_out
        sig_sums = lax.optimization_barrier(jnp.sum(one_hot * gating[:, None], axis=0))
        balance = balance_weight * jnp.sum((counts - mean_load) / mean_load * sig_sums) / mean_load
        return (result.reshape(SEQS, SEQ_LEN, D), balance)
    floats = (tokens.astype(jnp.float32), norm1_gain.astype(jnp.float32), w_query.astype(jnp.float32), w_key.astype(jnp.float32), w_value.astype(jnp.float32), w_output.astype(jnp.float32), norm2_gain.astype(jnp.float32), w_router.astype(jnp.float32), w_in.astype(jnp.float32), w_out.astype(jnp.float32))
    (result, balance), pullback = jax.vjp(forward, *floats)
    gradients = pullback((cotangent.astype(jnp.float32), jnp.ones((), balance.dtype)))
    return (result.astype(jnp.bfloat16), gradients[0], gradients[1], gradients[2], gradients[3], gradients[4], gradients[5], gradients[6], gradients[7], gradients[8], gradients[9], balance)
```

```python
import functools

import jax
import jax.numpy as jnp
from jax import lax
from jax.experimental import pallas as pl
from jax.experimental.pallas import tpu as pltpu
from jax.sharding import Mesh
from jax.sharding import PartitionSpec as P

D = 768
HEADS = 12
HD = 64
norm_eps = 1e-05
balance_weight = 1.0
LOG2E = 1.4426950408889634
MASKED = -1e30
GELU_A = 0.7978845608028654
GELU_B = 0.044715
VMEM = 56 * 1024 * 1024
f32 = jnp.float32
bf16 = jnp.bfloat16


def dg(a, b, ca, cb):
    return lax.dot_general(a, b, (((ca,), (cb,)), ((), ())), preferred_element_type=f32)


def attend_kernel(lane, blk, qT_ref, k_ref, vT_ref, oT_ref, osend_ref, lse_ref):
    length = qT_ref.shape[1]
    per = osend_ref.shape[2]
    c = (HD**-0.5) * LOG2E
    rows = lax.broadcasted_iota(jnp.int32, (blk, blk), 0)
    cols = lax.broadcasted_iota(jnp.int32, (blk, blk), 1)
    keep = rows <= cols
    for i in range(length // blk):
        a, b = i * blk, (i + 1) * blk
        q = qT_ref[:, a:b]
        sd = dg(k_ref[a:b, lane : lane + HD], q, 1, 0)
        sd = jnp.where(keep, sd, MASKED)
        m = jnp.max(sd, axis=0, keepdims=True)
        if i:
            s = dg(k_ref[:a, lane : lane + HD], q, 1, 0)
            m = jnp.maximum(m, jnp.max(s, axis=0, keepdims=True))
        mc = m * c
        pd = jnp.exp2(sd * c - mc)
        total = jnp.sum(pd, axis=0, keepdims=True)
        o = dg(vT_ref[:, a:b], pd.astype(bf16), 1, 0)
        if i:
            p = jnp.exp2(s * c - mc)
            total = total + jnp.sum(p, axis=0, keepdims=True)
            o = o + dg(vT_ref[:, :a], p.astype(bf16), 1, 0)
        o = o / total
        oT_ref[:, a:b] = o
        d, off = a // per, a % per
        osend_ref[d, :, off : off + blk] = o.astype(bf16)
        lse_ref[:, a:b] = mc + jnp.log2(total)


def attend(qkvT, kv, h, dests):
    length = kv.shape[0]
    n = qkvT.shape[0] // (3 * HD)
    blk = length // dests
    return pl.pallas_call(
        functools.partial(attend_kernel, (h % 2) * HD, blk),
        out_shape=(
            jax.ShapeDtypeStruct((HD, length), f32),
            jax.ShapeDtypeStruct((dests, HD, length // dests), bf16),
            jax.ShapeDtypeStruct((1, length), f32),
        ),
        grid=(1,),
        in_specs=[
            pl.BlockSpec((HD, length), lambda i: (h, 0)),
            pl.BlockSpec((length, 2 * HD), lambda i: (0, h // 2)),
            pl.BlockSpec((HD, length), lambda i: (2 * n + h, 0)),
        ],
        out_specs=(
            pl.BlockSpec((HD, length), lambda i: (0, 0)),
            pl.BlockSpec((dests, HD, length // dests), lambda i: (0, 0, 0)),
            pl.BlockSpec((1, length), lambda i: (0, 0)),
        ),
        compiler_params=pltpu.CompilerParams(vmem_limit_bytes=VMEM),
        cost_estimate=pl.CostEstimate(
            flops=8 * length * length * HD, bytes_accessed=length * HD * 14, transcendentals=length * length // 2
        ),
        name=f"attend_head{h}",
    )(qkvT, kv, qkvT)


def attend_back_kernel(
    lk, lv, blk, qT_ref, k_ref, kT_ref, v_ref, do_ref, oT_ref, lse_ref, dT_ref, dsend_ref, dk_acc, dv_acc
):
    length = qT_ref.shape[1]
    per = do_ref.shape[2]
    sc = HD**-0.5
    c = sc * LOG2E
    rows = lax.broadcasted_iota(jnp.int32, (blk, blk), 0)
    cols = lax.broadcasted_iota(jnp.int32, (blk, blk), 1)
    keep = rows <= cols
    n = length // blk
    for i in reversed(range(n)):
        x0, x1 = i * blk, (i + 1) * blk
        d, off = x0 // per, x0 % per
        q = qT_ref[:, x0:x1]
        do = do_ref[d, :, off : off + blk]
        lse = lse_ref[:, x0:x1]
        delta = jnp.sum(do.astype(f32) * oT_ref[:, x0:x1], axis=0, keepdims=True)
        dq = None
        for a, b, diag in ([(0, x0, False)] if i else []) + [(x0, x1, True)]:
            s = dg(k_ref[a:b, lk : lk + HD], q, 1, 0)
            p = jnp.exp2(s * c - lse)
            if diag:
                p = jnp.where(keep, p, 0.0)
            dp = dg(v_ref[a:b, lv : lv + HD], do, 1, 0)
            ds = (p * (dp - delta)).astype(bf16)
            dvn = dg(do, p.astype(bf16), 1, 1)
            dkn = dg(q, ds, 1, 1)
            if i == n - 1:
                dv_acc[:, a:b] = dvn
                dk_acc[:, a:b] = dkn
            else:
                dv_acc[:, a:b] += dvn
                dk_acc[:, a:b] += dkn
            t = dg(kT_ref[:, a:b], ds, 1, 0)
            dq = t if dq is None else dq + t
        dq = (dq * sc).astype(bf16)
        dT_ref[0:HD, x0:x1] = dq
        dsend_ref[d, 0:HD, off : off + blk] = dq
    for d in range(dsend_ref.shape[0]):
        dk = (dk_acc[:, d * per : (d + 1) * per] * sc).astype(bf16)
        dv = dv_acc[:, d * per : (d + 1) * per].astype(bf16)
        dT_ref[HD : 2 * HD, d * per : (d + 1) * per] = dk
        dT_ref[2 * HD : 3 * HD, d * per : (d + 1) * per] = dv
        dsend_ref[d, HD : 2 * HD, :] = dk
        dsend_ref[d, 2 * HD : 3 * HD, :] = dv


def attend_back(qkvT, kv, do, oT, lse, h):
    length = kv.shape[0]
    n = qkvT.shape[0] // (3 * HD)
    dests, _, per = do.shape
    hv = n + h
    blk = min(256, per)
    return pl.pallas_call(
        functools.partial(attend_back_kernel, (h % 2) * HD, (hv % 2) * HD, blk),
        out_shape=(
            jax.ShapeDtypeStruct((3 * HD, length), bf16),
            jax.ShapeDtypeStruct((dests, 3 * HD, per), bf16),
        ),
        grid=(1,),
        in_specs=[
            pl.BlockSpec((HD, length), lambda i: (h, 0)),
            pl.BlockSpec((length, 2 * HD), lambda i: (0, h // 2)),
            pl.BlockSpec((HD, length), lambda i: (n + h, 0)),
            pl.BlockSpec((length, 2 * HD), lambda i: (0, hv // 2)),
            pl.BlockSpec((dests, HD, per), lambda i: (0, 0, 0)),
            pl.BlockSpec((HD, length), lambda i: (0, 0)),
            pl.BlockSpec((1, length), lambda i: (0, 0)),
        ],
        out_specs=(
            pl.BlockSpec((3 * HD, length), lambda i: (0, 0)),
            pl.BlockSpec((dests, 3 * HD, per), lambda i: (0, 0, 0)),
        ),
        scratch_shapes=[pltpu.VMEM((HD, length), f32)] * 2,
        compiler_params=pltpu.CompilerParams(vmem_limit_bytes=VMEM),
        cost_estimate=pl.CostEstimate(
            flops=20 * length * length * HD, bytes_accessed=length * HD * 24, transcendentals=length * length // 2
        ),
        name=f"attend_back_head{h}",
    )(qkvT, kv, qkvT, kv, do, oT, lse)


def up_kernel(pick_ref, dy_ref, wo_ref, u_ref):
    u_ref[...] = dg(dy_ref[...], wo_ref[0], 1, 1).astype(bf16)


def expert_up(pick, dy, w_out, fc=768):
    rows = dy.shape[0]
    ff = w_out.shape[1]
    return pl.pallas_call(
        up_kernel,
        out_shape=jax.ShapeDtypeStruct((rows, ff), bf16),
        grid_spec=pltpu.PrefetchScalarGridSpec(
            num_scalar_prefetch=1,
            grid=(ff // fc,),
            in_specs=[
                pl.BlockSpec((rows, D), lambda f, p: (0, 0)),
                pl.BlockSpec((1, fc, D), lambda f, p: (p[0], f, 0)),
            ],
            out_specs=pl.BlockSpec((rows, fc), lambda f, p: (0, f)),
        ),
        compiler_params=pltpu.CompilerParams(vmem_limit_bytes=VMEM),
        cost_estimate=pl.CostEstimate(
            flops=2 * rows * D * ff, bytes_accessed=2 * (rows * D + ff * D + rows * ff), transcendentals=0
        ),
        name="expert_up",
    )(pick, dy, w_out)


def mid_kernel(
    pick_ref, x_ref, u_ref, wi_ref, wr_ref, load_ref, act_ref, gh_ref, rows_ref, router_ref, gate_ref, acc, gg, gate
):
    f = pl.program_id(0)
    n = pl.num_programs(0)

    @pl.when(f == 0)
    def _():
        logit = jnp.sum(x_ref[...].astype(f32) * wr_ref[...], axis=1, keepdims=True)
        gate[...] = jnp.broadcast_to(jax.nn.sigmoid(logit), gate.shape)

    h = dg(x_ref[...], wi_ref[0], 1, 0)
    h2 = h * h
    t = jnp.tanh(h * (GELU_A + (GELU_A * GELU_B) * h2))
    hp = 0.5 + 0.5 * t
    dgelu = hp + (0.5 * h) * (1.0 - t * t) * (GELU_A + (3.0 * GELU_A * GELU_B) * h2)
    u = u_ref[...].astype(f32)
    act = (h * hp).astype(bf16)
    act_ref[...] = act
    g1 = jnp.sum(act.astype(f32) * u, axis=1, keepdims=True)
    gh = (gate[:, :1] * u * dgelu).astype(bf16)
    gh_ref[...] = gh
    part = dg(gh, wi_ref[0], 1, 1)

    @pl.when(f == 0)
    def _():
        acc[...] = part
        gg[...] = jnp.broadcast_to(g1, gg.shape)

    @pl.when(f > 0)
    def _():
        acc[...] += part
        gg[...] += g1

    @pl.when(f == n - 1)
    def _():
        g = gate[:, :1]
        sel = (g * (1.0 - g) * (gg[:, :1] + load_ref[:, :1])).astype(bf16).astype(f32)
        rows_ref[...] = (acc[...] + sel * wr_ref[...]).astype(bf16)
        router_ref[...] = jnp.sum(x_ref[...].astype(f32) * sel, axis=0, keepdims=True)
        gate_ref[...] = gate[...]


def expert_mid(pick, x, u, w_in, wr, load, fc=768):
    rows = x.shape[0]
    ff = w_in.shape[2]

    def full(s):
        return pl.BlockSpec(s, lambda f, p: (0, 0))

    wide = pl.BlockSpec((rows, fc), lambda f, p: (0, f))
    return pl.pallas_call(
        mid_kernel,
        out_shape=(
            jax.ShapeDtypeStruct((rows, ff), bf16),
            jax.ShapeDtypeStruct((rows, ff), bf16),
            jax.ShapeDtypeStruct((rows, D), bf16),
            jax.ShapeDtypeStruct((1, D), f32),
            jax.ShapeDtypeStruct((rows, 128), f32),
        ),
        grid_spec=pltpu.PrefetchScalarGridSpec(
            num_scalar_prefetch=1,
            grid=(ff // fc,),
            in_specs=[
                full((rows, D)),
                wide,
                pl.BlockSpec((1, D, fc), lambda f, p: (p[0], 0, f)),
                full((1, D)),
                full((1, 128)),
            ],
            out_specs=(wide, wide, full((rows, D)), full((1, D)), full((rows, 128))),
            scratch_shapes=[
                pltpu.VMEM((rows, D), f32),
                pltpu.VMEM((rows, 128), f32),
                pltpu.VMEM((rows, 128), f32),
            ],
        ),
        compiler_params=pltpu.CompilerParams(vmem_limit_bytes=VMEM),
        cost_estimate=pl.CostEstimate(
            flops=4 * rows * D * ff,
            bytes_accessed=2 * (3 * rows * D + ff * D + 3 * rows * ff),
            transcendentals=rows * ff,
        ),
        name="expert_mid",
    )(pick, x, u, w_in, wr, load)


def grads_kernel(
    pick_ref, x_ref, dy_ref, gate_ref, act_ref, gh_ref, wo_ref, keep_ref, send_ref, prod_ref, acc, go, gi, gexp
):
    f = pl.program_id(0)
    n = pl.num_programs(0)

    @pl.when(f == 0)
    def _():
        gexp[...] = (dy_ref[...].astype(f32) * gate_ref[:, :1]).astype(bf16)

    go[...] = dg(act_ref[...], gexp[...], 0, 0).astype(bf16)
    gi[...] = dg(gh_ref[...], x_ref[...], 0, 0).astype(bf16)
    part = dg(act_ref[...], wo_ref[0], 1, 0)

    @pl.when(f == 0)
    def _():
        acc[...] = part

    @pl.when(f > 0)
    def _():
        acc[...] += part

    w = keep_ref.shape[3]
    me = pick_ref[1]
    for xx in range(keep_ref.shape[2]):
        a = pl.multiple_of((2 * xx + me) * w, w)
        b = pl.multiple_of((2 * xx + 1 - me) * w, w)
        keep_ref[0, 0, xx] = gi[pl.ds(a, w)]
        keep_ref[0, 1, xx] = go[pl.ds(a, w)]
        send_ref[0, 0, xx] = gi[pl.ds(b, w)]
        send_ref[0, 1, xx] = go[pl.ds(b, w)]

    @pl.when(f == n - 1)
    def _():
        prod_ref[...] = acc[...].astype(bf16)


def expert_grads(pick, x, dy, gate, act, gh, w_out, dp, nx):
    rows = x.shape[0]
    ff = w_out.shape[1]
    fc = ff // dp
    w = fc // (2 * nx)

    def full(s):
        return pl.BlockSpec(s, lambda f, p: (0, 0))

    wide = pl.BlockSpec((rows, fc), lambda f, p: (0, f))
    part = jax.ShapeDtypeStruct((dp, 2, nx, w, D), bf16)
    part_spec = pl.BlockSpec((1, 2, nx, w, D), lambda f, p: (f, 0, 0, 0, 0))
    return pl.pallas_call(
        grads_kernel,
        out_shape=(part, part, jax.ShapeDtypeStruct((rows, D), bf16)),
        grid_spec=pltpu.PrefetchScalarGridSpec(
            num_scalar_prefetch=1,
            grid=(dp,),
            in_specs=[
                full((rows, D)),
                full((rows, D)),
                full((rows, 128)),
                wide,
                wide,
                pl.BlockSpec((1, fc, D), lambda f, p: (p[0], f, 0)),
            ],
            out_specs=(part_spec, part_spec, full((rows, D))),
            scratch_shapes=[
                pltpu.VMEM((rows, D), f32),
                pltpu.VMEM((fc, D), bf16),
                pltpu.VMEM((fc, D), bf16),
                pltpu.VMEM((rows, D), bf16),
            ],
        ),
        compiler_params=pltpu.CompilerParams(vmem_limit_bytes=VMEM),
        cost_estimate=pl.CostEstimate(
            flops=6 * rows * D * ff,
            bytes_accessed=2 * (3 * rows * D + 3 * ff * D + 2 * rows * ff),
            transcendentals=0,
        ),
        name="expert_grads",
    )(pick, x, dy, gate, act, gh, w_out)


def swap(v, axis):
    return lax.ppermute(v, axis, [(0, 1), (1, 0)])


def shift(v, axis, step):
    n = lax.axis_size(axis)
    return lax.ppermute(v, axis, [(i, (i + step) % n) for i in range(n)])


def at(v, index):
    return lax.dynamic_index_in_dim(v, index, 0, keepdims=False)


def place(pieces, n):
    out = jnp.zeros((n,) + pieces[0][1].shape, pieces[0][1].dtype)
    for index, piece in pieces:
        out = lax.dynamic_update_index_in_dim(out, piece, index, 0)
    return out


def gather_shifts(v, axis):
    n = lax.axis_size(axis)
    me = lax.axis_index(axis)
    return place([(me, v)] + [((me - s) % n, shift(v, axis, s)) for s in range(1, n)], n)


def sum_all(v):
    v = v + swap(v, "core")
    v = v + swap(v, "x")
    v = v + swap(v, "expert") if lax.axis_size("expert") == 2 else lax.psum(v, "expert")
    out = v
    for s in range(1, lax.axis_size("dp")):
        out = out + shift(v, "dp", s)
    return out


def scatter_sum(v):
    e = lax.axis_size("expert")
    if e == 2:
        me = lax.axis_index("expert")
        halves = v.reshape(2, -1, D)
        v = at(halves, me) + swap(at(halves, 1 - me).astype(bf16), "expert").astype(f32)
    else:
        v = lax.psum_scatter(v.astype(bf16), "expert", scatter_dimension=0, tiled=True).astype(f32)
    n = lax.axis_size("dp")
    me = lax.axis_index("dp")
    parts = v.reshape(n, -1, D)
    out = at(parts, me)
    for s in range(1, n):
        out = out + shift(at(parts, (me + s) % n).astype(bf16), "dp", s).astype(f32)
    return out


def gather_back(v):
    v = gather_shifts(v, "dp")
    v = v.reshape((-1,) + v.shape[2:])
    if lax.axis_size("expert") == 2:
        v = gather_shifts(v, "expert")
    else:
        v = lax.all_gather(v, "expert")
    v = v.reshape((-1,) + v.shape[2:])
    v = gather_shifts(v, "x")
    v = gather_shifts(v, "core")
    return jnp.swapaxes(v, 0, 1)


def ring_scatter(parts):
    n = lax.axis_size("dp")
    me = lax.axis_index("dp")
    moving = at(parts, (me - 1) % n)
    for s in range(n - 1):
        moving = shift(moving, "dp", 1)
        moving = moving.astype(f32) + at(parts, (me - 2 - s) % n).astype(f32)
        if s < n - 2:
            moving = moving.astype(bf16)
    return moving


def normal_form(v):
    centred = v - jnp.mean(v, axis=-1, keepdims=True)
    rstd = lax.rsqrt(jnp.mean(centred * centred, axis=-1, keepdims=True) + norm_eps)
    return centred * rstd, rstd


def norm_back(dn, xh, rstd):
    return rstd * (dn - jnp.mean(dn, axis=-1, keepdims=True) - xh * jnp.mean(dn * xh, axis=-1, keepdims=True))


def per_device(
    tokens,
    cotangent,
    routes,
    norm1_gain,
    w_query,
    w_key,
    w_value,
    w_output,
    norm2_gain,
    w_router,
    w_in,
    w_out,
):
    rows = tokens.shape[1]
    nx, owners, dp = lax.axis_size("x"), lax.axis_size("expert"), lax.axis_size("dp")
    xi, ci, ei = lax.axis_index("x"), lax.axis_index("core"), lax.axis_index("expert")
    ctx = 2 * nx
    ctx_i = xi * 2 + ci
    length = ctx * rows
    experts = w_router.shape[1]
    cap = 2 * rows // experts
    mine = D // ctx
    heads = mine // HD
    pick = jnp.stack([xi, ci]).astype(jnp.int32)

    flat = tokens.reshape(rows, D).astype(f32)
    xh1, rstd1 = normal_form(flat)
    normed = (xh1 * norm1_gain).astype(bf16)
    other = swap(normed, "x")
    near, far = swap(normed, "core"), swap(other, "core")
    normed_all = place(
        [(ctx_i, normed), (ctx_i ^ 1, near), (ctx_i ^ 2, other), (ctx_i ^ 3, far)], ctx
    ).reshape(length, D)

    route = routes.reshape(rows)
    hot = (route[:, None] == jnp.arange(experts, dtype=jnp.int32)[None, :]).astype(f32)
    lower = jnp.arange(rows)[:, None] >= jnp.arange(rows)[None, :]
    before = dg(lower.astype(bf16), hot.astype(bf16), 1, 0)
    rank = (jnp.sum(before * hot, axis=1) - 1.0).astype(jnp.int32)
    slot = ((route % nx) * owners + route // nx) * cap + rank
    spread = (jnp.arange(experts * cap, dtype=jnp.int32)[:, None] == slot[None, :]).astype(bf16)

    def dispatch(v):
        out = dg(spread, v, 1, 0).astype(bf16).reshape(nx * owners, cap, D)
        out = lax.all_to_all(out, ("x", "expert"), split_axis=0, concat_axis=0, tiled=True)
        return out.reshape(-1, D)

    def give_back(v):
        v = v.reshape(nx * owners, cap, D)
        v = lax.all_to_all(v, ("x", "expert"), split_axis=0, concat_axis=0, tiled=True)
        return dg(spread, v.reshape(-1, D), 0, 0)

    dy_low = cotangent.reshape(rows, D)
    dy = dy_low.astype(f32)
    dy_rows = dispatch(dy_low)
    counts = sum_all(jnp.sum(hot, axis=0))
    mean_load = rows * ctx * dp * owners / experts
    load_term = balance_weight * (counts - mean_load) / (mean_load * mean_load)
    expert_id = ei * nx + xi
    load = jnp.broadcast_to(lax.dynamic_slice(load_term, (expert_id,), (1,)).reshape(1, 1), (1, 128))
    wr = lax.dynamic_slice(w_router, (0, expert_id), (D, 1)).astype(f32).reshape(1, D)

    def cut(w):
        return lax.dynamic_slice(w, (0, ctx_i * mine), (D, mine))

    wq, wk, wv = cut(w_query), cut(w_key), cut(w_value)
    qkvT = dg(jnp.concatenate([wq, wk, wv], axis=1), normed_all, 0, 1).astype(bf16)
    kv = dg(normed_all, jnp.concatenate([wk, wv], axis=1), 1, 0).astype(bf16)
    kept, arrived = [], []
    for h in range(heads):
        oT, osend, lse = attend(qkvT, kv, h, ctx)
        kept.append((oT, lse))
        arrived.append(lax.all_to_all(osend, ("x", "core"), split_axis=0, concat_axis=0, tiled=True))
    attT = jnp.stack(arrived, axis=1).reshape(D, rows)

    middle = flat + dg(attT, w_output, 0, 0)
    xh2, rstd2 = normal_form(middle)
    second = (xh2 * norm2_gain).astype(bf16)
    gating = jax.nn.sigmoid(jnp.sum(hot * dg(second, w_router, 1, 0), axis=1))

    up = expert_up(pick, dy_rows, w_out)
    x_rows = dispatch(second)
    active, grad_hidden, back_rows, router_row, gate = expert_mid(pick, x_rows, up, w_in, wr, load)
    grad_second = give_back(back_rows)
    keep, send, produced = expert_grads(pick, x_rows, dy_rows, gate, active, grad_hidden, w_out, dp, nx)
    output = (middle + gating[:, None] * give_back(produced)).astype(bf16)

    pair = (keep.astype(f32) + swap(send, "core").astype(f32)).astype(bf16)
    ringed = ring_scatter(pair)
    own = lax.dynamic_index_in_dim(ringed, xi, 1, keepdims=False)
    moved = swap(lax.dynamic_index_in_dim(ringed, 1 - xi, 1, keepdims=False).astype(bf16), "x").astype(f32)
    first, latter = jnp.where(xi == 0, own, moved), jnp.where(xi == 0, moved, own)
    both = jnp.stack([first, latter], axis=1)
    grad_in = jnp.swapaxes(both[0], 1, 2)
    grad_out = both[1]

    grad_middle = dy + norm_back(grad_second * norm2_gain, xh2, rstd2)
    branch = grad_middle.astype(bf16)
    go = dg(attT, branch, 1, 0)
    go = go.reshape(nx, 2, mine, D)
    go_keep = lax.dynamic_index_in_dim(go, ci, 1, keepdims=False)
    go_send = lax.dynamic_index_in_dim(go, 1 - ci, 1, keepdims=False).astype(bf16)
    go = go_keep + swap(go_send, "core").astype(f32)
    go = at(go, xi) + swap(at(go, 1 - xi).astype(bf16), "x").astype(f32)
    attT_grad = dg(w_output, branch, 1, 1).astype(bf16).reshape(ctx, heads, HD, rows)

    grad_normed = 0.0
    weight_rows = []
    for h in range(heads):
        do = lax.all_to_all(attT_grad[:, h], ("x", "core"), split_axis=0, concat_axis=0, tiled=True)
        dT, dsend = attend_back(qkvT, kv, do, kept[h][0], kept[h][1], h)
        got = lax.all_to_all(dsend, ("x", "core"), split_axis=0, concat_axis=0, tiled=True)
        wide = jnp.stack([w.reshape(D, ctx, heads, HD)[:, :, h] for w in (w_query, w_key, w_value)], axis=2)
        grad_normed = grad_normed + dg(got.reshape(-1, rows), wide.reshape(D, -1), 0, 1)
        weight_rows.append(dg(dT, normed_all, 1, 0))
    grad_tokens = grad_middle + norm_back(grad_normed * norm1_gain, xh1, rstd1)

    shared = gather_back(scatter_sum(jnp.concatenate(weight_rows + [go], axis=0)).astype(bf16))
    sides = shared[:, :, : 3 * mine].reshape(nx, 2, heads, 3, HD, D)
    grads = []
    for p in range(3):
        grads.append(jnp.transpose(sides[:, :, :, p].reshape(D, D)).astype(f32))
    grad_output = shared[:, :, 3 * mine :].reshape(D, D).astype(f32)
    grad_norm1 = 0.0
    for g, w in zip(grads, (w_query, w_key, w_value)):
        grad_norm1 = grad_norm1 + jnp.sum(g * w.astype(f32), axis=1)
    grad_norm1 = grad_norm1 / norm1_gain

    router_rows = (jnp.arange(experts) == expert_id).astype(f32)[:, None] * router_row
    sig = jnp.pad(jnp.sum(hot * gating[:, None], axis=0), (0, D - experts))
    small = sum_all(
        jnp.concatenate([router_rows, jnp.sum(grad_second * xh2, axis=0)[None], sig[None]], axis=0)
    )
    grad_router = jnp.transpose(small[:experts])
    grad_norm2 = small[experts]
    total_sig = small[experts + 1, :experts]
    balance = balance_weight * jnp.sum((counts - mean_load) / mean_load * total_sig) / mean_load

    return (
        output.reshape(1, rows, D),
        grad_tokens.reshape(1, rows, D),
        grad_norm1,
        grads[0],
        grads[1],
        grads[2],
        grad_output,
        grad_norm2,
        grad_router,
        grad_in,
        grad_out,
        balance,
    )


def solution(mesh):
    dp, ctx, owners = mesh.shape["dp"], mesh.shape["ctx"], mesh.shape["expert"]
    split = Mesh(mesh.devices.reshape(dp, ctx // 2, 2, owners), ("dp", "x", "core", "expert"))
    token = P(("dp", "expert"), ("x", "core"), None)
    return jax.shard_map(
        per_device,
        mesh=split,
        in_specs=(token, token, token, P(), P(), P(), P(), P(), P(), P(), P("expert"), P("expert")),
        out_specs=(
            token,
            token,
            P(),
            P(),
            P(),
            P(),
            P(),
            P(),
            P(),
            P("expert", None, ("dp", "x", "core")),
            P("expert", ("dp", "x", "core"), None),
            P(),
        ),
        check_vma=False,
    )
```

```python
import functools

import jax
import jax.numpy as jnp
from jax import lax
from jax.experimental import pallas as pl
from jax.experimental.pallas import tpu as pltpu
from jax.sharding import Mesh
from jax.sharding import PartitionSpec as P

D = 768
HEADS = 12
HD = 64
norm_eps = 1e-05
balance_weight = 1.0
LOG2E = 1.4426950408889634
MASKED = -1e30
GELU_A = 0.7978845608028654
GELU_B = 0.044715
VMEM = 56 * 1024 * 1024
f32 = jnp.float32
bf16 = jnp.bfloat16


def dg(a, b, ca, cb):
    return lax.dot_general(a, b, (((ca,), (cb,)), ((), ())), preferred_element_type=f32)


def attend_kernel(heads, blk, qT_ref, k_ref, vT_ref, oT_ref, osend_ref, lse_ref):
    length = qT_ref.shape[1]
    per = osend_ref.shape[3]
    c = (HD**-0.5) * LOG2E
    rows = lax.broadcasted_iota(jnp.int32, (blk, blk), 0)
    cols = lax.broadcasted_iota(jnp.int32, (blk, blk), 1)
    keep = rows <= cols
    for h in range(heads):
        hs = slice(h * HD, (h + 1) * HD)
        for i in range(length // blk):
            a, b = i * blk, (i + 1) * blk
            q = qT_ref[hs, a:b]
            sd = dg(k_ref[a:b, hs], q, 1, 0)
            sd = jnp.where(keep, sd, MASKED)
            m = jnp.max(sd, axis=0, keepdims=True)
            if i:
                s = dg(k_ref[:a, hs], q, 1, 0)
                m = jnp.maximum(m, jnp.max(s, axis=0, keepdims=True))
            mc = m * c
            pd = jnp.exp2(sd * c - mc)
            total = jnp.sum(pd, axis=0, keepdims=True)
            o = dg(vT_ref[hs, a:b], pd.astype(bf16), 1, 0)
            if i:
                p = jnp.exp2(s * c - mc)
                total = total + jnp.sum(p, axis=0, keepdims=True)
                o = o + dg(vT_ref[hs, :a], p.astype(bf16), 1, 0)
            o = o / total
            oT_ref[hs, a:b] = o
            d, off = a // per, a % per
            osend_ref[d, h, :, off : off + blk] = o.astype(bf16)
            lse_ref[h, :, a:b] = mc + jnp.log2(total)


def attend(qkvT, kv, dests):
    length = kv.shape[0]
    heads = qkvT.shape[0] // (3 * HD)
    wide = heads * HD
    per = length // dests
    return pl.pallas_call(
        functools.partial(attend_kernel, heads, per),
        out_shape=(
            jax.ShapeDtypeStruct((wide, length), f32),
            jax.ShapeDtypeStruct((dests, heads, HD, per), bf16),
            jax.ShapeDtypeStruct((heads, 1, length), f32),
        ),
        grid=(1,),
        in_specs=[
            pl.BlockSpec((wide, length), lambda i: (0, 0)),
            pl.BlockSpec(kv.shape, lambda i: (0, 0)),
            pl.BlockSpec((wide, length), lambda i: (2, 0)),
        ],
        out_specs=(
            pl.BlockSpec((wide, length), lambda i: (0, 0)),
            pl.BlockSpec((dests, heads, HD, per), lambda i: (0, 0, 0, 0)),
            pl.BlockSpec((heads, 1, length), lambda i: (0, 0, 0)),
        ),
        compiler_params=pltpu.CompilerParams(vmem_limit_bytes=VMEM),
        cost_estimate=pl.CostEstimate(
            flops=8 * heads * length * length * HD,
            bytes_accessed=length * wide * 14,
            transcendentals=heads * length * length // 2,
        ),
        name="attend",
    )(qkvT, kv, qkvT)


def attend_back_kernel(lk, lv, blk, *refs):
    qT_ref, k_ref, kT_ref, v_ref, do_ref, oT_ref, lse_ref = refs[:7]
    dT_ref, dsend_ref, dk_acc, dv_acc = refs[-4:]
    length = qT_ref.shape[1]
    per = do_ref.shape[3]
    sc = HD**-0.5
    c = sc * LOG2E
    rows = lax.broadcasted_iota(jnp.int32, (blk, blk), 0)
    cols = lax.broadcasted_iota(jnp.int32, (blk, blk), 1)
    keep = rows <= cols
    n = length // blk
    for i in reversed(range(n)):
        x0, x1 = i * blk, (i + 1) * blk
        d, off = x0 // per, x0 % per
        q = qT_ref[:, x0:x1]
        do = do_ref[d, 0, :, off : off + blk]
        lse = lse_ref[0, :, x0:x1]
        delta = jnp.sum(do.astype(f32) * oT_ref[:, x0:x1], axis=0, keepdims=True)
        dq = None
        for a, b, diag in ([(0, x0, False)] if i else []) + [(x0, x1, True)]:
            s = dg(k_ref[a:b, lk : lk + HD], q, 1, 0)
            p = jnp.exp2(s * c - lse)
            if diag:
                p = jnp.where(keep, p, 0.0)
            dp = dg(v_ref[a:b, lv : lv + HD], do, 1, 0)
            ds = (p * (dp - delta)).astype(bf16)
            dvn = dg(do, p.astype(bf16), 1, 1)
            dkn = dg(q, ds, 1, 1)
            if i == n - 1:
                dv_acc[:, a:b] = dvn
                dk_acc[:, a:b] = dkn
            else:
                dv_acc[:, a:b] += dvn
                dk_acc[:, a:b] += dkn
            t = dg(kT_ref[:, a:b], ds, 1, 0)
            dq = t if dq is None else dq + t
        dq = (dq * sc).astype(bf16)
        dT_ref[0, :, x0:x1] = dq
        dsend_ref[d, 0, :, off : off + blk] = dq
    for d in range(dsend_ref.shape[0]):
        at_d = slice(d * per, (d + 1) * per)
        dk = (dk_acc[:, at_d] * sc).astype(bf16)
        dv = dv_acc[:, at_d].astype(bf16)
        dT_ref[1, :, at_d] = dk
        dT_ref[2, :, at_d] = dv
        dsend_ref[d, 1] = dk
        dsend_ref[d, 2] = dv


def attend_back(qkvT, kv, do, slot, oT, lse, h, so_far):
    length = kv.shape[0]
    n = qkvT.shape[0] // (3 * HD)
    dests, _, _, per = do.shape
    hv = n + h
    blk = min(256, per)
    args = [qkvT, kv, qkvT, kv, do, oT, lse]
    specs = [
        pl.BlockSpec((HD, length), lambda i: (h, 0)),
        pl.BlockSpec((length, 2 * HD), lambda i: (0, h // 2)),
        pl.BlockSpec((HD, length), lambda i: (n + h, 0)),
        pl.BlockSpec((length, 2 * HD), lambda i: (0, hv // 2)),
        pl.BlockSpec((dests, 1, HD, per), lambda i: (0, slot, 0, 0)),
        pl.BlockSpec((HD, length), lambda i: (h, 0)),
        pl.BlockSpec((1, 1, length), lambda i: (h, 0, 0)),
    ]
    alias = {}
    if so_far is not None:
        alias = {len(args): 0, len(args) + 1: 1}
        args += list(so_far)
        specs += [pl.BlockSpec(memory_space=pl.ANY)] * 2
    return pl.pallas_call(
        functools.partial(attend_back_kernel, (h % 2) * HD, (hv % 2) * HD, blk),
        out_shape=(
            jax.ShapeDtypeStruct((3, n * HD, length), bf16),
            jax.ShapeDtypeStruct((dests, 3, n * HD, per), bf16),
        ),
        grid=(1,),
        in_specs=specs,
        out_specs=(
            pl.BlockSpec((3, HD, length), lambda i: (0, h, 0)),
            pl.BlockSpec((dests, 3, HD, per), lambda i: (0, 0, h, 0)),
        ),
        scratch_shapes=[pltpu.VMEM((HD, length), f32)] * 2,
        input_output_aliases=alias,
        compiler_params=pltpu.CompilerParams(vmem_limit_bytes=VMEM),
        cost_estimate=pl.CostEstimate(
            flops=20 * length * length * HD, bytes_accessed=length * HD * 24, transcendentals=length * length // 2
        ),
        name=f"attend_back_head{h}",
    )(*args)


def up_kernel(pick_ref, dy_ref, wo_ref, u_ref):
    u_ref[...] = dg(dy_ref[...], wo_ref[0], 1, 1).astype(bf16)


def expert_up(pick, dy, w_out, fc=768):
    rows = dy.shape[0]
    ff = w_out.shape[1]
    return pl.pallas_call(
        up_kernel,
        out_shape=jax.ShapeDtypeStruct((rows, ff), bf16),
        grid_spec=pltpu.PrefetchScalarGridSpec(
            num_scalar_prefetch=1,
            grid=(ff // fc,),
            in_specs=[
                pl.BlockSpec((rows, D), lambda f, p: (0, 0)),
                pl.BlockSpec((1, fc, D), lambda f, p: (p[0], f, 0)),
            ],
            out_specs=pl.BlockSpec((rows, fc), lambda f, p: (0, f)),
        ),
        compiler_params=pltpu.CompilerParams(vmem_limit_bytes=VMEM),
        cost_estimate=pl.CostEstimate(
            flops=2 * rows * D * ff, bytes_accessed=2 * (rows * D + ff * D + rows * ff), transcendentals=0
        ),
        name="expert_up",
    )(pick, dy, w_out)


def mid_kernel(
    pick_ref, x_ref, u_ref, wi_ref, wr_ref, load_ref, act_ref, gh_ref, rows_ref, router_ref, gate_ref, acc, gg, gate
):
    f = pl.program_id(0)
    n = pl.num_programs(0)

    @pl.when(f == 0)
    def _():
        logit = jnp.sum(x_ref[...].astype(f32) * wr_ref[...], axis=1, keepdims=True)
        gate[...] = jnp.broadcast_to(jax.nn.sigmoid(logit), gate.shape)

    h = dg(x_ref[...], wi_ref[0], 1, 0)
    h2 = h * h
    t = jnp.tanh(h * (GELU_A + (GELU_A * GELU_B) * h2))
    hp = 0.5 + 0.5 * t
    dgelu = hp + (0.5 * h) * (1.0 - t * t) * (GELU_A + (3.0 * GELU_A * GELU_B) * h2)
    u = u_ref[...].astype(f32)
    act = (h * hp).astype(bf16)
    act_ref[...] = act
    g1 = jnp.sum(act.astype(f32) * u, axis=1, keepdims=True)
    gh = (gate[:, :1] * u * dgelu).astype(bf16)
    gh_ref[...] = gh
    part = dg(gh, wi_ref[0], 1, 1)

    @pl.when(f == 0)
    def _():
        acc[...] = part
        gg[...] = jnp.broadcast_to(g1, gg.shape)

    @pl.when(f > 0)
    def _():
        acc[...] += part
        gg[...] += g1

    @pl.when(f == n - 1)
    def _():
        g = gate[:, :1]
        sel = (g * (1.0 - g) * (gg[:, :1] + load_ref[:, :1])).astype(bf16).astype(f32)
        rows_ref[...] = (acc[...] + sel * wr_ref[...]).astype(bf16)
        router_ref[...] = jnp.sum(x_ref[...].astype(f32) * sel, axis=0, keepdims=True)
        gate_ref[...] = gate[...]


def expert_mid(pick, x, u, w_in, wr, load, fc=768):
    rows = x.shape[0]
    ff = w_in.shape[2]

    def full(s):
        return pl.BlockSpec(s, lambda f, p: (0, 0))

    wide = pl.BlockSpec((rows, fc), lambda f, p: (0, f))
    return pl.pallas_call(
        mid_kernel,
        out_shape=(
            jax.ShapeDtypeStruct((rows, ff), bf16),
            jax.ShapeDtypeStruct((rows, ff), bf16),
            jax.ShapeDtypeStruct((rows, D), bf16),
            jax.ShapeDtypeStruct((1, D), f32),
            jax.ShapeDtypeStruct((rows, 128), f32),
        ),
        grid_spec=pltpu.PrefetchScalarGridSpec(
            num_scalar_prefetch=1,
            grid=(ff // fc,),
            in_specs=[
                full((rows, D)),
                wide,
                pl.BlockSpec((1, D, fc), lambda f, p: (p[0], 0, f)),
                full((1, D)),
                full((1, 128)),
            ],
            out_specs=(wide, wide, full((rows, D)), full((1, D)), full((rows, 128))),
            scratch_shapes=[
                pltpu.VMEM((rows, D), f32),
                pltpu.VMEM((rows, 128), f32),
                pltpu.VMEM((rows, 128), f32),
            ],
        ),
        compiler_params=pltpu.CompilerParams(vmem_limit_bytes=VMEM),
        cost_estimate=pl.CostEstimate(
            flops=4 * rows * D * ff,
            bytes_accessed=2 * (3 * rows * D + ff * D + 3 * rows * ff),
            transcendentals=rows * ff,
        ),
        name="expert_mid",
    )(pick, x, u, w_in, wr, load)


def grads_kernel(
    pick_ref, x_ref, dy_ref, gate_ref, act_ref, gh_ref, wo_ref, keep_ref, send_ref, prod_ref, acc, go, gi, gexp
):
    f = pl.program_id(0)
    n = pl.num_programs(0)

    @pl.when(f == 0)
    def _():
        gexp[...] = (dy_ref[...].astype(f32) * gate_ref[:, :1]).astype(bf16)

    go[...] = dg(act_ref[...], gexp[...], 0, 0).astype(bf16)
    gi[...] = dg(gh_ref[...], x_ref[...], 0, 0).astype(bf16)
    part = dg(act_ref[...], wo_ref[0], 1, 0)

    @pl.when(f == 0)
    def _():
        acc[...] = part

    @pl.when(f > 0)
    def _():
        acc[...] += part

    w = keep_ref.shape[3]
    me = pick_ref[1]
    for xx in range(keep_ref.shape[2]):
        a = pl.multiple_of((2 * xx + me) * w, w)
        b = pl.multiple_of((2 * xx + 1 - me) * w, w)
        keep_ref[0, 0, xx] = gi[pl.ds(a, w)]
        keep_ref[0, 1, xx] = go[pl.ds(a, w)]
        send_ref[0, 0, xx] = gi[pl.ds(b, w)]
        send_ref[0, 1, xx] = go[pl.ds(b, w)]

    @pl.when(f == n - 1)
    def _():
        prod_ref[...] = acc[...].astype(bf16)


def expert_grads(pick, x, dy, gate, act, gh, w_out, dp, nx):
    rows = x.shape[0]
    ff = w_out.shape[1]
    fc = ff // dp
    w = fc // (2 * nx)

    def full(s):
        return pl.BlockSpec(s, lambda f, p: (0, 0))

    wide = pl.BlockSpec((rows, fc), lambda f, p: (0, f))
    part = jax.ShapeDtypeStruct((dp, 2, nx, w, D), bf16)
    part_spec = pl.BlockSpec((1, 2, nx, w, D), lambda f, p: (f, 0, 0, 0, 0))
    return pl.pallas_call(
        grads_kernel,
        out_shape=(part, part, jax.ShapeDtypeStruct((rows, D), bf16)),
        grid_spec=pltpu.PrefetchScalarGridSpec(
            num_scalar_prefetch=1,
            grid=(dp,),
            in_specs=[
                full((rows, D)),
                full((rows, D)),
                full((rows, 128)),
                wide,
                wide,
                pl.BlockSpec((1, fc, D), lambda f, p: (p[0], f, 0)),
            ],
            out_specs=(part_spec, part_spec, full((rows, D))),
            scratch_shapes=[
                pltpu.VMEM((rows, D), f32),
                pltpu.VMEM((fc, D), bf16),
                pltpu.VMEM((fc, D), bf16),
                pltpu.VMEM((rows, D), bf16),
            ],
        ),
        compiler_params=pltpu.CompilerParams(vmem_limit_bytes=VMEM),
        cost_estimate=pl.CostEstimate(
            flops=6 * rows * D * ff,
            bytes_accessed=2 * (3 * rows * D + 3 * ff * D + 2 * rows * ff),
            transcendentals=0,
        ),
        name="expert_grads",
    )(pick, x, dy, gate, act, gh, w_out)


def swap(v, axis):
    return lax.ppermute(v, axis, [(0, 1), (1, 0)])


def shift(v, axis, step):
    n = lax.axis_size(axis)
    return lax.ppermute(v, axis, [(i, (i + step) % n) for i in range(n)])


def at(v, index):
    return lax.dynamic_index_in_dim(v, index, 0, keepdims=False)


def place(pieces, n):
    out = jnp.zeros((n,) + pieces[0][1].shape, pieces[0][1].dtype)
    for index, piece in pieces:
        out = lax.dynamic_update_index_in_dim(out, piece, index, 0)
    return out


def gather_shifts(v, axis):
    n = lax.axis_size(axis)
    me = lax.axis_index(axis)
    return place([(me, v)] + [((me - s) % n, shift(v, axis, s)) for s in range(1, n)], n)


def sum_all(v):
    return jnp.sum(lax.all_gather(v, ("dp", "x", "core", "expert")), axis=0)


def tie(*arrays):
    return lax.optimization_barrier(arrays)


def scatter_sum(v):
    e = lax.axis_size("expert")
    if e == 2:
        me = lax.axis_index("expert")
        halves = v.reshape(2, -1, D)
        v = at(halves, me) + swap(at(halves, 1 - me).astype(bf16), "expert").astype(f32)
    else:
        v = lax.psum_scatter(v.astype(bf16), "expert", scatter_dimension=0, tiled=True).astype(f32)
    n = lax.axis_size("dp")
    me = lax.axis_index("dp")
    parts = v.reshape(n, -1, D)
    out = at(parts, me)
    for s in range(1, n):
        out = out + shift(at(parts, (me + s) % n).astype(bf16), "dp", s).astype(f32)
    return out


def gather_back(v):
    v = gather_shifts(v, "dp")
    v = v.reshape((-1,) + v.shape[2:])
    if lax.axis_size("expert") == 2:
        v = gather_shifts(v, "expert")
    else:
        v = lax.all_gather(v, "expert")
    v = v.reshape((-1,) + v.shape[2:])
    v = gather_shifts(v, "x")
    v = gather_shifts(v, "core")
    return jnp.swapaxes(v, 0, 1)


def ring_steps(parts):
    n = lax.axis_size("dp")
    me = lax.axis_index("dp")
    moving = at(parts, (me - 1) % n)
    for s in range(n - 1):
        moving = shift(moving, "dp", 1)
        moving = moving.astype(f32) + at(parts, (me - 2 - s) % n).astype(f32)
        if s < n - 2:
            moving = moving.astype(bf16)
        moving = yield moving


def normal_form(v):
    centred = v - jnp.mean(v, axis=-1, keepdims=True)
    rstd = lax.rsqrt(jnp.mean(centred * centred, axis=-1, keepdims=True) + norm_eps)
    return centred * rstd, rstd


def norm_back(dn, xh, rstd):
    return rstd * (dn - jnp.mean(dn, axis=-1, keepdims=True) - xh * jnp.mean(dn * xh, axis=-1, keepdims=True))


def per_device(
    tokens,
    cotangent,
    routes,
    norm1_gain,
    w_query,
    w_key,
    w_value,
    w_output,
    norm2_gain,
    w_router,
    w_in,
    w_out,
):
    rows = tokens.shape[1]
    nx, owners, dp = lax.axis_size("x"), lax.axis_size("expert"), lax.axis_size("dp")
    xi, ci, ei = lax.axis_index("x"), lax.axis_index("core"), lax.axis_index("expert")
    ctx = 2 * nx
    ctx_i = xi * 2 + ci
    length = ctx * rows
    experts = w_router.shape[1]
    cap = 2 * rows // experts
    mine = D // ctx
    heads = mine // HD
    pick = jnp.stack([xi, ci]).astype(jnp.int32)

    flat = tokens.reshape(rows, D).astype(f32)
    xh1, rstd1 = normal_form(flat)
    normed = (xh1 * norm1_gain).astype(bf16)
    other = swap(normed, "x")
    near = swap(normed, "core")
    route = routes.reshape(rows)
    hot = (route[:, None] == jnp.arange(experts, dtype=jnp.int32)[None, :]).astype(f32)
    lower = jnp.arange(rows)[:, None] >= jnp.arange(rows)[None, :]
    before = dg(lower.astype(bf16), hot.astype(bf16), 1, 0)
    rank = (jnp.sum(before * hot, axis=1) - 1.0).astype(jnp.int32)
    slot = ((route % nx) * owners + route // nx) * cap + rank
    spread = (jnp.arange(experts * cap, dtype=jnp.int32)[:, None] == slot[None, :]).astype(bf16)

    def pack(v):
        return dg(spread, v, 1, 0).astype(bf16).reshape(nx * owners, cap, D)

    def trade(v):
        v = lax.all_to_all(v.reshape(nx * owners, cap, D), ("x", "expert"), split_axis=0, concat_axis=0, tiled=True)
        return v.reshape(-1, D)

    def turn(v):
        return lax.all_to_all(v, ("x", "core"), split_axis=0, concat_axis=0, tiled=True)

    dy_low = cotangent.reshape(rows, D)
    dy = dy_low.astype(f32)
    other, dy_packed = tie(other, pack(dy_low))
    dy_rows = trade(dy_packed)
    far = swap(other, "core")
    normed_all = place(
        [(ctx_i, normed), (ctx_i ^ 1, near), (ctx_i ^ 2, other), (ctx_i ^ 3, far)], ctx
    ).reshape(length, D)
    counts = sum_all(jnp.zeros((8, 128), f32).at[0, :experts].set(jnp.sum(hot, axis=0)))[0, :experts]
    mean_load = rows * ctx * dp * owners / experts
    load_term = balance_weight * (counts - mean_load) / (mean_load * mean_load)
    expert_id = ei * nx + xi
    load = jnp.broadcast_to(lax.dynamic_slice(load_term, (expert_id,), (1,)).reshape(1, 1), (1, 128))
    wr = lax.dynamic_slice(w_router, (0, expert_id), (D, 1)).astype(f32).reshape(1, D)

    def cut(w):
        return lax.dynamic_slice(w, (0, ctx_i * mine), (D, mine))

    wq, wk, wv = cut(w_query), cut(w_key), cut(w_value)
    qkvT = dg(jnp.concatenate([wq, wk, wv], axis=1), normed_all, 0, 1).astype(bf16)
    kv = dg(normed_all, jnp.concatenate([wk, wv], axis=1), 1, 0).astype(bf16)
    oT, osend, lse = attend(qkvT, kv, ctx)
    osend, dy_rows = tie(osend, dy_rows)
    attT = turn(osend).reshape(D, rows)

    middle = flat + dg(attT, w_output, 0, 0)
    xh2, rstd2 = normal_form(middle)
    second = (xh2 * norm2_gain).astype(bf16)
    gating = jax.nn.sigmoid(jnp.sum(hot * dg(second, w_router, 1, 0), axis=1))

    up = expert_up(pick, dy_rows, w_out)
    x_rows = trade(pack(second))
    active, grad_hidden, back_rows, router_row, gate = expert_mid(pick, x_rows, up, w_in, wr, load)
    returned = trade(back_rows)
    keep, send, produced = expert_grads(pick, x_rows, dy_rows, gate, active, grad_hidden, w_out, dp, nx)
    returned, keep, send, produced = tie(returned, keep, send, produced)
    pair = (keep.astype(f32) + swap(send, "core").astype(f32)).astype(bf16)

    grad_second = dg(spread, returned, 0, 0)
    grad_middle = dy + norm_back(grad_second * norm2_gain, xh2, rstd2)
    branch = grad_middle.astype(bf16)
    attT_grad = dg(w_output, branch, 1, 1).astype(bf16).reshape(ctx, heads, HD, rows)
    do_first, do_later = turn(attT_grad[:, :1]), turn(attT_grad[:, 1:])
    go = dg(attT, branch, 1, 0)
    go = go.reshape(nx, 2, mine, D)
    go_keep = lax.dynamic_index_in_dim(go, ci, 1, keepdims=False)
    go_send = lax.dynamic_index_in_dim(go, 1 - ci, 1, keepdims=False).astype(bf16)
    go = go_keep + swap(go_send, "core").astype(f32)
    go = at(go, xi) + swap(at(go, 1 - xi).astype(bf16), "x").astype(f32)

    do_first, pair = tie(do_first, pair)
    ring = ring_steps(pair)
    ringed = next(ring)
    so_far = attend_back(qkvT, kv, do_first, 0, oT, lse, 0, None)
    for h in range(1, heads):
        do_later, ringed, *so_far = tie(do_later, ringed, *so_far)
        try:
            ringed = ring.send(ringed)
        except StopIteration:
            pass
        so_far = attend_back(qkvT, kv, do_later, h - 1, oT, lse, h, so_far)
    dT, dsend = so_far
    for more in ring:
        ringed = more
    got, produced = tie(turn(dsend), produced)
    grad_normed = 0.0
    for p, w in enumerate((w_query, w_key, w_value)):
        grad_normed = grad_normed + dg(got[:, p].reshape(D, rows), w, 0, 1)
    grad_tokens = grad_middle + norm_back(grad_normed * norm1_gain, xh1, rstd1)
    output = (middle + gating[:, None] * dg(spread, trade(produced), 0, 0)).astype(bf16)

    weight_rows = dg(dT.reshape(3 * mine, length), normed_all, 1, 0)
    shared = gather_back(scatter_sum(jnp.concatenate([weight_rows, go], axis=0)).astype(bf16))
    grads = [shared[:, :, p * mine : (p + 1) * mine].reshape(D, D).astype(f32) for p in range(4)]
    grads[:3] = [jnp.transpose(g) for g in grads[:3]]
    grad_norm1 = 0.0
    for g, w in zip(grads, (w_query, w_key, w_value)):
        grad_norm1 = grad_norm1 + jnp.sum(g * w.astype(f32), axis=1)
    grad_norm1 = grad_norm1 / norm1_gain

    own = lax.dynamic_index_in_dim(ringed, xi, 1, keepdims=False)
    moved = swap(lax.dynamic_index_in_dim(ringed, 1 - xi, 1, keepdims=False).astype(bf16), "x").astype(f32)
    first, latter = jnp.where(xi == 0, own, moved), jnp.where(xi == 0, moved, own)
    both = jnp.stack([first, latter], axis=1)
    grad_in = jnp.swapaxes(both[0], 1, 2)
    grad_out = both[1]

    router_rows = (jnp.arange(experts) == expert_id).astype(f32)[:, None] * router_row
    sig = jnp.pad(jnp.sum(hot * gating[:, None], axis=0), (0, D - experts))
    small = sum_all(
        jnp.concatenate([router_rows, jnp.sum(grad_second * xh2, axis=0)[None], sig[None]], axis=0)
    )
    grad_router = jnp.transpose(small[:experts])
    grad_norm2 = small[experts]
    total_sig = small[experts + 1, :experts]
    balance = balance_weight * jnp.sum((counts - mean_load) / mean_load * total_sig) / mean_load

    return (
        output.reshape(1, rows, D),
        grad_tokens.reshape(1, rows, D),
        grad_norm1,
        grads[0],
        grads[1],
        grads[2],
        grads[3],
        grad_norm2,
        grad_router,
        grad_in,
        grad_out,
        balance,
    )


def solution(mesh):
    dp, ctx, owners = mesh.shape["dp"], mesh.shape["ctx"], mesh.shape["expert"]
    split = Mesh(mesh.devices.reshape(dp, ctx // 2, 2, owners), ("dp", "x", "core", "expert"))
    token = P(("dp", "expert"), ("x", "core"), None)
    return jax.shard_map(
        per_device,
        mesh=split,
        in_specs=(token, token, token, P(), P(), P(), P(), P(), P(), P(), P("expert"), P("expert")),
        out_specs=(
            token,
            token,
            P(),
            P(),
            P(),
            P(),
            P(),
            P(),
            P(),
            P("expert", None, ("dp", "x", "core")),
            P("expert", ("dp", "x", "core"), None),
            P(),
        ),
        check_vma=False,
    )
```

```python
import functools

import jax
import jax.numpy as jnp
from jax import lax
from jax.experimental import pallas as pl
from jax.experimental.pallas import tpu as pltpu
from jax.sharding import Mesh
from jax.sharding import PartitionSpec as P

D = 768
HEADS = 12
HD = 64
norm_eps = 1e-05
balance_weight = 1.0
LOG2E = 1.4426950408889634
MASKED = -1e30
GELU_A = 0.7978845608028654
GELU_B = 0.044715
VMEM = 56 * 1024 * 1024
f32 = jnp.float32
bf16 = jnp.bfloat16


def dg(a, b, ca, cb):
    return lax.dot_general(a, b, (((ca,), (cb,)), ((), ())), preferred_element_type=f32)


def project_kernel(place_ref, tok_ref, gain_ref, w_ref, *refs):
    normed_ref, qkvT_ref, kv_ref = refs[-3:]
    x = tok_ref[...].astype(f32)
    centred = x - jnp.mean(x, axis=1, keepdims=True)
    rstd = lax.rsqrt(jnp.mean(centred * centred, axis=1, keepdims=True) + norm_eps)
    normed = (centred * rstd * gain_ref[...]).astype(bf16)
    normed_ref[...] = normed
    qkv = dg(normed, w_ref[...], 1, 0).astype(bf16)
    kv_ref[...] = qkv[:, qkv.shape[1] - kv_ref.shape[1] :]
    qkvT_ref[...] = qkv.T


def project(place, tok, gain, w, ctx, so_far):
    rows = tok.shape[0]
    wide = w.shape[1]
    args = [tok, gain, w]
    specs = [pl.BlockSpec(a.shape, lambda i, p: (0, 0)) for a in args]
    alias = {}
    if so_far is not None:
        alias = {4: 0, 5: 1, 6: 2}
        args += list(so_far)
        specs += [pl.BlockSpec(memory_space=pl.ANY)] * 3
    return pl.pallas_call(
        project_kernel,
        out_shape=(
            jax.ShapeDtypeStruct((ctx * rows, D), bf16),
            jax.ShapeDtypeStruct((wide, ctx * rows), bf16),
            jax.ShapeDtypeStruct((ctx * rows, 2 * wide // 3), bf16),
        ),
        grid_spec=pltpu.PrefetchScalarGridSpec(
            num_scalar_prefetch=1,
            grid=(1,),
            in_specs=specs,
            out_specs=(
                pl.BlockSpec((rows, D), lambda i, p: (p[0], 0)),
                pl.BlockSpec((wide, rows), lambda i, p: (0, p[0])),
                pl.BlockSpec((rows, 2 * wide // 3), lambda i, p: (p[0], 0)),
            ),
        ),
        input_output_aliases=alias,
        compiler_params=pltpu.CompilerParams(vmem_limit_bytes=VMEM),
        cost_estimate=pl.CostEstimate(
            flops=4 * rows * D * wide, bytes_accessed=4 * rows * D + 8 * rows * wide, transcendentals=0
        ),
        name="project",
    )(place.astype(jnp.int32).reshape(1), *args)


def attend_kernel(heads, blk, qT_ref, k_ref, vT_ref, oT_ref, osend_ref, lse_ref):
    length = qT_ref.shape[1]
    per = osend_ref.shape[3]
    c = (HD**-0.5) * LOG2E
    rows = lax.broadcasted_iota(jnp.int32, (blk, blk), 0)
    cols = lax.broadcasted_iota(jnp.int32, (blk, blk), 1)
    keep = rows <= cols
    for h in range(heads):
        hs = slice(h * HD, (h + 1) * HD)
        for i in range(length // blk):
            a, b = i * blk, (i + 1) * blk
            q = qT_ref[hs, a:b]
            sd = dg(k_ref[a:b, hs], q, 1, 0)
            sd = jnp.where(keep, sd, MASKED)
            m = jnp.max(sd, axis=0, keepdims=True)
            if i:
                s = dg(k_ref[:a, hs], q, 1, 0)
                m = jnp.maximum(m, jnp.max(s, axis=0, keepdims=True))
            mc = m * c
            pd = jnp.exp2(sd * c - mc)
            total = jnp.sum(pd, axis=0, keepdims=True)
            o = dg(vT_ref[hs, a:b], pd.astype(bf16), 1, 0)
            if i:
                p = jnp.exp2(s * c - mc)
                total = total + jnp.sum(p, axis=0, keepdims=True)
                o = o + dg(vT_ref[hs, :a], p.astype(bf16), 1, 0)
            o = o / total
            oT_ref[hs, a:b] = o
            d, off = a // per, a % per
            osend_ref[d, h, :, off : off + blk] = o.astype(bf16)
            lse_ref[h, :, a:b] = mc + jnp.log2(total)


def attend(qkvT, kv, dests):
    length = kv.shape[0]
    heads = qkvT.shape[0] // (3 * HD)
    wide = heads * HD
    per = length // dests
    return pl.pallas_call(
        functools.partial(attend_kernel, heads, per),
        out_shape=(
            jax.ShapeDtypeStruct((wide, length), f32),
            jax.ShapeDtypeStruct((dests, heads, HD, per), bf16),
            jax.ShapeDtypeStruct((heads, 1, length), f32),
        ),
        grid=(1,),
        in_specs=[
            pl.BlockSpec((wide, length), lambda i: (0, 0)),
            pl.BlockSpec(kv.shape, lambda i: (0, 0)),
            pl.BlockSpec((wide, length), lambda i: (2, 0)),
        ],
        out_specs=(
            pl.BlockSpec((wide, length), lambda i: (0, 0)),
            pl.BlockSpec((dests, heads, HD, per), lambda i: (0, 0, 0, 0)),
            pl.BlockSpec((heads, 1, length), lambda i: (0, 0, 0)),
        ),
        compiler_params=pltpu.CompilerParams(vmem_limit_bytes=VMEM),
        cost_estimate=pl.CostEstimate(
            flops=8 * heads * length * length * HD,
            bytes_accessed=length * wide * 14,
            transcendentals=heads * length * length // 2,
        ),
        name="attend",
    )(qkvT, kv, qkvT)


def attend_back_kernel(lk, lv, blk, *refs):
    qT_ref, k_ref, kT_ref, v_ref, do_ref, oT_ref, lse_ref = refs[:7]
    dT_ref, dsend_ref, dk_acc, dv_acc = refs[-4:]
    length = qT_ref.shape[1]
    per = do_ref.shape[3]
    sc = HD**-0.5
    c = sc * LOG2E
    rows = lax.broadcasted_iota(jnp.int32, (blk, blk), 0)
    cols = lax.broadcasted_iota(jnp.int32, (blk, blk), 1)
    keep = rows <= cols
    n = length // blk
    for i in reversed(range(n)):
        x0, x1 = i * blk, (i + 1) * blk
        d, off = x0 // per, x0 % per
        q = qT_ref[:, x0:x1]
        do = do_ref[d, 0, :, off : off + blk]
        lse = lse_ref[0, :, x0:x1]
        delta = jnp.sum(do.astype(f32) * oT_ref[:, x0:x1], axis=0, keepdims=True)
        dq = None
        for a, b, diag in ([(0, x0, False)] if i else []) + [(x0, x1, True)]:
            s = dg(k_ref[a:b, lk : lk + HD], q, 1, 0)
            p = jnp.exp2(s * c - lse)
            if diag:
                p = jnp.where(keep, p, 0.0)
            dp = dg(v_ref[a:b, lv : lv + HD], do, 1, 0)
            ds = (p * (dp - delta)).astype(bf16)
            dvn = dg(do, p.astype(bf16), 1, 1)
            dkn = dg(q, ds, 1, 1)
            if i == n - 1:
                dv_acc[:, a:b] = dvn
                dk_acc[:, a:b] = dkn
            else:
                dv_acc[:, a:b] += dvn
                dk_acc[:, a:b] += dkn
            t = dg(kT_ref[:, a:b], ds, 1, 0)
            dq = t if dq is None else dq + t
        dq = (dq * sc).astype(bf16)
        dT_ref[0, :, x0:x1] = dq
        dsend_ref[d, 0, :, off : off + blk] = dq
    for d in range(dsend_ref.shape[0]):
        at_d = slice(d * per, (d + 1) * per)
        dk = (dk_acc[:, at_d] * sc).astype(bf16)
        dv = dv_acc[:, at_d].astype(bf16)
        dT_ref[1, :, at_d] = dk
        dT_ref[2, :, at_d] = dv
        dsend_ref[d, 1] = dk
        dsend_ref[d, 2] = dv


def attend_back(qkvT, kv, do, slot, oT, lse, h, so_far):
    length = kv.shape[0]
    n = qkvT.shape[0] // (3 * HD)
    dests, _, _, per = do.shape
    hv = n + h
    blk = min(256, per)
    args = [qkvT, kv, qkvT, kv, do, oT, lse]
    specs = [
        pl.BlockSpec((HD, length), lambda i: (h, 0)),
        pl.BlockSpec((length, 2 * HD), lambda i: (0, h // 2)),
        pl.BlockSpec((HD, length), lambda i: (n + h, 0)),
        pl.BlockSpec((length, 2 * HD), lambda i: (0, hv // 2)),
        pl.BlockSpec((dests, 1, HD, per), lambda i: (0, slot, 0, 0)),
        pl.BlockSpec((HD, length), lambda i: (h, 0)),
        pl.BlockSpec((1, 1, length), lambda i: (h, 0, 0)),
    ]
    alias = {}
    if so_far is not None:
        alias = {len(args): 0, len(args) + 1: 1}
        args += list(so_far)
        specs += [pl.BlockSpec(memory_space=pl.ANY)] * 2
    return pl.pallas_call(
        functools.partial(attend_back_kernel, (h % 2) * HD, (hv % 2) * HD, blk),
        out_shape=(
            jax.ShapeDtypeStruct((3, n * HD, length), bf16),
            jax.ShapeDtypeStruct((dests, 3, n * HD, per), bf16),
        ),
        grid=(1,),
        in_specs=specs,
        out_specs=(
            pl.BlockSpec((3, HD, length), lambda i: (0, h, 0)),
            pl.BlockSpec((dests, 3, HD, per), lambda i: (0, 0, h, 0)),
        ),
        scratch_shapes=[pltpu.VMEM((HD, length), f32)] * 2,
        input_output_aliases=alias,
        compiler_params=pltpu.CompilerParams(vmem_limit_bytes=VMEM),
        cost_estimate=pl.CostEstimate(
            flops=20 * length * length * HD, bytes_accessed=length * HD * 24, transcendentals=length * length // 2
        ),
        name=f"attend_back_head{h}",
    )(*args)


def up_kernel(pick_ref, dy_ref, wo_ref, u_ref):
    u_ref[...] = dg(dy_ref[...], wo_ref[0], 1, 1).astype(bf16)


def expert_up(pick, dy, w_out, fc=768):
    rows = dy.shape[0]
    ff = w_out.shape[1]
    return pl.pallas_call(
        up_kernel,
        out_shape=jax.ShapeDtypeStruct((rows, ff), bf16),
        grid_spec=pltpu.PrefetchScalarGridSpec(
            num_scalar_prefetch=1,
            grid=(ff // fc,),
            in_specs=[
                pl.BlockSpec((rows, D), lambda f, p: (0, 0)),
                pl.BlockSpec((1, fc, D), lambda f, p: (p[0], f, 0)),
            ],
            out_specs=pl.BlockSpec((rows, fc), lambda f, p: (0, f)),
        ),
        compiler_params=pltpu.CompilerParams(vmem_limit_bytes=VMEM),
        cost_estimate=pl.CostEstimate(
            flops=2 * rows * D * ff, bytes_accessed=2 * (rows * D + ff * D + rows * ff), transcendentals=0
        ),
        name="expert_up",
    )(pick, dy, w_out)


def mid_kernel(
    pick_ref, x_ref, u_ref, wi_ref, wr_ref, load_ref, act_ref, gh_ref, rows_ref, router_ref, gate_ref, acc, gg, gate
):
    f = pl.program_id(0)
    n = pl.num_programs(0)

    @pl.when(f == 0)
    def _():
        logit = jnp.sum(x_ref[...].astype(f32) * wr_ref[...], axis=1, keepdims=True)
        gate[...] = jnp.broadcast_to(jax.nn.sigmoid(logit), gate.shape)

    h = dg(x_ref[...], wi_ref[0], 1, 0)
    h2 = h * h
    t = jnp.tanh(h * (GELU_A + (GELU_A * GELU_B) * h2))
    hp = 0.5 + 0.5 * t
    dgelu = hp + (0.5 * h) * (1.0 - t * t) * (GELU_A + (3.0 * GELU_A * GELU_B) * h2)
    u = u_ref[...].astype(f32)
    act = (h * hp).astype(bf16)
    act_ref[...] = act
    g1 = jnp.sum(act.astype(f32) * u, axis=1, keepdims=True)
    gh = (gate[:, :1] * u * dgelu).astype(bf16)
    gh_ref[...] = gh
    part = dg(gh, wi_ref[0], 1, 1)

    @pl.when(f == 0)
    def _():
        acc[...] = part
        gg[...] = jnp.broadcast_to(g1, gg.shape)

    @pl.when(f > 0)
    def _():
        acc[...] += part
        gg[...] += g1

    @pl.when(f == n - 1)
    def _():
        g = gate[:, :1]
        sel = (g * (1.0 - g) * (gg[:, :1] + load_ref[:, :1])).astype(bf16).astype(f32)
        rows_ref[...] = (acc[...] + sel * wr_ref[...]).astype(bf16)
        router_ref[...] = jnp.sum(x_ref[...].astype(f32) * sel, axis=0, keepdims=True)
        gate_ref[...] = gate[...]


def expert_mid(pick, x, u, w_in, wr, load, fc=768):
    rows = x.shape[0]
    ff = w_in.shape[2]

    def full(s):
        return pl.BlockSpec(s, lambda f, p: (0, 0))

    wide = pl.BlockSpec((rows, fc), lambda f, p: (0, f))
    return pl.pallas_call(
        mid_kernel,
        out_shape=(
            jax.ShapeDtypeStruct((rows, ff), bf16),
            jax.ShapeDtypeStruct((rows, ff), bf16),
            jax.ShapeDtypeStruct((rows, D), bf16),
            jax.ShapeDtypeStruct((1, D), f32),
            jax.ShapeDtypeStruct((rows, 128), f32),
        ),
        grid_spec=pltpu.PrefetchScalarGridSpec(
            num_scalar_prefetch=1,
            grid=(ff // fc,),
            in_specs=[
                full((rows, D)),
                wide,
                pl.BlockSpec((1, D, fc), lambda f, p: (p[0], 0, f)),
                full((1, D)),
                full((1, 128)),
            ],
            out_specs=(wide, wide, full((rows, D)), full((1, D)), full((rows, 128))),
            scratch_shapes=[
                pltpu.VMEM((rows, D), f32),
                pltpu.VMEM((rows, 128), f32),
                pltpu.VMEM((rows, 128), f32),
            ],
        ),
        compiler_params=pltpu.CompilerParams(vmem_limit_bytes=VMEM),
        cost_estimate=pl.CostEstimate(
            flops=4 * rows * D * ff,
            bytes_accessed=2 * (3 * rows * D + ff * D + 3 * rows * ff),
            transcendentals=rows * ff,
        ),
        name="expert_mid",
    )(pick, x, u, w_in, wr, load)


def grads_kernel(
    pick_ref, x_ref, dy_ref, gate_ref, act_ref, gh_ref, wo_ref, keep_ref, send_ref, prod_ref, acc, go, gi, gexp
):
    f = pl.program_id(0)
    n = pl.num_programs(0)

    @pl.when(f == 0)
    def _():
        gexp[...] = (dy_ref[...].astype(f32) * gate_ref[:, :1]).astype(bf16)

    go[...] = dg(act_ref[...], gexp[...], 0, 0).astype(bf16)
    gi[...] = dg(gh_ref[...], x_ref[...], 0, 0).astype(bf16)
    part = dg(act_ref[...], wo_ref[0], 1, 0)

    @pl.when(f == 0)
    def _():
        acc[...] = part

    @pl.when(f > 0)
    def _():
        acc[...] += part

    w = keep_ref.shape[3]
    me = pick_ref[1]
    for xx in range(keep_ref.shape[2]):
        a = pl.multiple_of((2 * xx + me) * w, w)
        b = pl.multiple_of((2 * xx + 1 - me) * w, w)
        keep_ref[0, 0, xx] = gi[pl.ds(a, w)]
        keep_ref[0, 1, xx] = go[pl.ds(a, w)]
        send_ref[0, 0, xx] = gi[pl.ds(b, w)]
        send_ref[0, 1, xx] = go[pl.ds(b, w)]

    @pl.when(f == n - 1)
    def _():
        prod_ref[...] = acc[...].astype(bf16)


def expert_grads(pick, x, dy, gate, act, gh, w_out, dp, nx):
    rows = x.shape[0]
    ff = w_out.shape[1]
    fc = ff // dp
    w = fc // (2 * nx)

    def full(s):
        return pl.BlockSpec(s, lambda f, p: (0, 0))

    wide = pl.BlockSpec((rows, fc), lambda f, p: (0, f))
    part = jax.ShapeDtypeStruct((dp, 2, nx, w, D), bf16)
    part_spec = pl.BlockSpec((1, 2, nx, w, D), lambda f, p: (f, 0, 0, 0, 0))
    return pl.pallas_call(
        grads_kernel,
        out_shape=(part, part, jax.ShapeDtypeStruct((rows, D), bf16)),
        grid_spec=pltpu.PrefetchScalarGridSpec(
            num_scalar_prefetch=1,
            grid=(dp,),
            in_specs=[
                full((rows, D)),
                full((rows, D)),
                full((rows, 128)),
                wide,
                wide,
                pl.BlockSpec((1, fc, D), lambda f, p: (p[0], f, 0)),
            ],
            out_specs=(part_spec, part_spec, full((rows, D))),
            scratch_shapes=[
                pltpu.VMEM((rows, D), f32),
                pltpu.VMEM((fc, D), bf16),
                pltpu.VMEM((fc, D), bf16),
                pltpu.VMEM((rows, D), bf16),
            ],
        ),
        compiler_params=pltpu.CompilerParams(vmem_limit_bytes=VMEM),
        cost_estimate=pl.CostEstimate(
            flops=6 * rows * D * ff,
            bytes_accessed=2 * (3 * rows * D + 3 * ff * D + 2 * rows * ff),
            transcendentals=0,
        ),
        name="expert_grads",
    )(pick, x, dy, gate, act, gh, w_out)


def weight_rows_kernel(half_ref, dT_ref, normed_ref, go_ref, small_ref, keep_ref, send_ref, acc):
    n = dT_ref.shape[0]
    half = keep_ref.shape[0]
    acc[:n] = dg(dT_ref[...], normed_ref[...], 1, 0)
    acc[n:] = go_ref[...]
    a = pl.multiple_of(half_ref[0] * half, half)
    b = pl.multiple_of((1 - half_ref[0]) * half, half)
    keep_ref[...] = acc[pl.ds(a, half)]
    send_ref[:half] = acc[pl.ds(b, half)].astype(bf16)
    send_ref[half:] = small_ref[...]


def weight_rows(half, dT, normed, go, small):
    rows = dT.shape[0] + go.shape[0]
    extra = small.shape[0]
    args = (dT, normed, go, small)
    return pl.pallas_call(
        weight_rows_kernel,
        out_shape=(
            jax.ShapeDtypeStruct((rows // 2, D), f32),
            jax.ShapeDtypeStruct((rows // 2 + extra, D), bf16),
        ),
        grid_spec=pltpu.PrefetchScalarGridSpec(
            num_scalar_prefetch=1,
            grid=(1,),
            in_specs=[pl.BlockSpec(a.shape, lambda i, p: (0, 0)) for a in args],
            out_specs=(
                pl.BlockSpec((rows // 2, D), lambda i, p: (0, 0)),
                pl.BlockSpec((rows // 2 + extra, D), lambda i, p: (0, 0)),
            ),
            scratch_shapes=[pltpu.VMEM((rows, D), f32)],
        ),
        compiler_params=pltpu.CompilerParams(vmem_limit_bytes=VMEM),
        cost_estimate=pl.CostEstimate(
            flops=2 * dT.size * D, bytes_accessed=2 * dT.size + 2 * normed.size + 6 * rows * D, transcendentals=0
        ),
        name="weight_rows",
    )(half.astype(jnp.int32).reshape(1), *args)


def finish_kernel(dp, me_ref, *refs):
    pieces = refs[:8]
    weights = refs[8:11]
    outs = refs[11:15]
    gain_ref = refs[15]
    got, wide, in_sem, out_sem = refs[16:]
    z, xi, ci, yi = me_ref[0], me_ref[1], me_ref[2], me_ref[3]
    rows = pieces[0].shape[0] // dp
    per = 4 * 2 // dp
    copies = []
    for n in range(8):
        c, x, y = (n // 4) ^ ci, ((n // 2) % 2) ^ xi, (n % 2) ^ yi
        for r in range(dp):
            j = y * dp + lax.rem(z + dp - r, dp)
            p = lax.div(j * 4, 2 * dp)
            first = (x * 2 + c) * (D // 4) + lax.rem(j, 2 * dp // 4) * rows
            copy = pltpu.make_async_copy(
                pieces[n].at[pl.ds(r * rows, rows)],
                got.at[p, pl.ds(pl.multiple_of(first, rows), rows)],
                in_sem.at[n, r],
            )
            copy.start()
            copies.append(copy)
    for copy in copies:
        copy.wait()
    del per
    gain = jnp.zeros((D, 1), f32)
    backs = []
    for p in range(4):
        if p < 3:
            g = got[p].T.astype(f32)
            gain = gain + jnp.sum(g * weights[p][...].astype(f32), axis=1, keepdims=True)
        else:
            g = got[p].astype(f32)
        wide[p] = g
        back = pltpu.make_async_copy(wide.at[p], outs[p], out_sem.at[p])
        back.start()
        backs.append(back)
    gain_ref[...] = gain
    for back in backs:
        back.wait()


def finish(me, pieces, weights, dp):
    whole = jax.ShapeDtypeStruct((D, D), f32)
    anywhere = pl.BlockSpec(memory_space=pl.ANY)
    return pl.pallas_call(
        functools.partial(finish_kernel, dp),
        out_shape=(whole,) * 4 + (jax.ShapeDtypeStruct((D, 1), f32),),
        grid_spec=pltpu.PrefetchScalarGridSpec(
            num_scalar_prefetch=1,
            grid=(1,),
            in_specs=[anywhere] * 8 + [pl.BlockSpec((D, D), lambda i, p: (0, 0))] * 3,
            out_specs=(anywhere,) * 4 + (pl.BlockSpec((D, 1), lambda i, p: (0, 0)),),
            scratch_shapes=[
                pltpu.VMEM((4, D, D), bf16),
                pltpu.VMEM((4, D, D), f32),
                pltpu.SemaphoreType.DMA((8, dp)),
                pltpu.SemaphoreType.DMA((4,)),
            ],
        ),
        compiler_params=pltpu.CompilerParams(vmem_limit_bytes=VMEM),
        cost_estimate=pl.CostEstimate(flops=8 * D * D, bytes_accessed=32 * D * D, transcendentals=0),
        name="finish",
    )(me, *pieces, *weights)


def swap(v, axis):
    return lax.ppermute(v, axis, [(0, 1), (1, 0)])


def shift(v, axis, step):
    n = lax.axis_size(axis)
    return lax.ppermute(v, axis, [(i, (i + step) % n) for i in range(n)])


def at(v, index):
    return lax.dynamic_index_in_dim(v, index, 0, keepdims=False)


def two(v):
    high = lax.reduce_precision(v, 8, 7)
    return jnp.concatenate([high, v - high], axis=0).astype(bf16)


def one(v):
    v = v.astype(f32)
    n = v.shape[0] // 2
    return v[:n] + v[n:]


def add_pair(v):
    return v + (swap(v, "expert") if lax.axis_size("expert") == 2 else lax.psum(v, "expert") - v)


def add_shifts(v):
    out = v
    for s in range(1, lax.axis_size("dp")):
        out = out + shift(v, "dp", s)
    return out


def tie(*arrays):
    return lax.optimization_barrier(arrays)


def normal_form(v):
    centred = v - jnp.mean(v, axis=-1, keepdims=True)
    rstd = lax.rsqrt(jnp.mean(centred * centred, axis=-1, keepdims=True) + norm_eps)
    return centred * rstd, rstd


def norm_back(dn, xh, rstd):
    return rstd * (dn - jnp.mean(dn, axis=-1, keepdims=True) - xh * jnp.mean(dn * xh, axis=-1, keepdims=True))


def per_device(
    tokens,
    cotangent,
    routes,
    norm1_gain,
    w_query,
    w_key,
    w_value,
    w_output,
    norm2_gain,
    w_router,
    w_in,
    w_out,
):
    rows = tokens.shape[1]
    nx, owners, dp = lax.axis_size("x"), lax.axis_size("expert"), lax.axis_size("dp")
    xi, ci, ei = lax.axis_index("x"), lax.axis_index("core"), lax.axis_index("expert")
    ctx = 2 * nx
    ctx_i = xi * 2 + ci
    length = ctx * rows
    experts = w_router.shape[1]
    cap = 2 * rows // experts
    mine = D // ctx
    heads = mine // HD
    pick = jnp.stack([xi, ci]).astype(jnp.int32)

    tok = tokens.reshape(rows, D)
    other = swap(tok, "x")
    near = swap(tok, "core")

    route = routes.reshape(rows)
    hot = (route[:, None] == jnp.arange(experts, dtype=jnp.int32)[None, :]).astype(f32)
    lower = jnp.arange(rows)[:, None] >= jnp.arange(rows)[None, :]
    before = dg(lower.astype(bf16), hot.astype(bf16), 1, 0)
    rank = (jnp.sum(before * hot, axis=1) - 1.0).astype(jnp.int32)
    slot = ((route % nx) * owners + route // nx) * cap + rank
    spread = (jnp.arange(experts * cap, dtype=jnp.int32)[:, None] == slot[None, :]).astype(bf16)

    def pack(v):
        return dg(spread, v, 1, 0).astype(bf16).reshape(nx * owners, cap, D)

    def trade(v):
        v = lax.all_to_all(v.reshape(nx * owners, cap, D), ("x", "expert"), split_axis=0, concat_axis=0, tiled=True)
        return v.reshape(-1, D)

    def turn(v):
        return lax.all_to_all(v, ("x", "core"), split_axis=0, concat_axis=0, tiled=True)

    def cut(w):
        return lax.dynamic_slice(w, (0, ctx_i * mine), (D, mine))

    w_own = jnp.concatenate([cut(w_query), cut(w_key), cut(w_value)], axis=1)
    gain1 = norm1_gain.reshape(1, D)
    dy_low = cotangent.reshape(rows, D)
    dy = dy_low.astype(f32)
    counts = jnp.sum(hot, axis=0)
    counts = counts + swap(counts, "core")
    counts = counts + swap(counts, "x")
    so_far = project(ctx_i, tok, gain1, w_own, ctx, None)
    so_far = project(ctx_i ^ 1, near, gain1, w_own, ctx, so_far)
    other, dy_packed, counts, *so_far = tie(other, pack(dy_low), counts, *so_far)
    far = swap(other, "core")
    dy_rows = trade(dy_packed)
    counts = add_pair(counts)
    so_far = project(ctx_i ^ 2, other, gain1, w_own, ctx, so_far)
    so_far = project(ctx_i ^ 3, far, gain1, w_own, ctx, so_far)
    counts, normed_all, qkvT, kv = tie(counts, *so_far)
    counts = add_shifts(counts)
    oT, osend, lse = attend(qkvT, kv, ctx)
    osend, dy_rows, counts = tie(osend, dy_rows, counts)
    attT = turn(osend).reshape(D, rows)

    mean_load = rows * ctx * dp * owners / experts
    load_term = balance_weight * (counts - mean_load) / (mean_load * mean_load)
    expert_id = ei * nx + xi
    load = jnp.broadcast_to(lax.dynamic_slice(load_term, (expert_id,), (1,)).reshape(1, 1), (1, 128))
    wr = lax.dynamic_slice(w_router, (0, expert_id), (D, 1)).astype(f32).reshape(1, D)

    flat = tok.astype(f32)
    middle = flat + dg(attT, w_output, 0, 0)
    xh2, rstd2 = normal_form(middle)
    second = (xh2 * norm2_gain).astype(bf16)
    gating = jax.nn.sigmoid(jnp.sum(hot * dg(second, w_router, 1, 0), axis=1))

    up = expert_up(pick, dy_rows, w_out)
    x_rows = trade(pack(second))
    active, grad_hidden, back_rows, router_row, gate = expert_mid(pick, x_rows, up, w_in, wr, load)
    returned = trade(back_rows)
    keep, send, produced = expert_grads(pick, x_rows, dy_rows, gate, active, grad_hidden, w_out, dp, nx)
    returned, keep, send, produced = tie(returned, keep, send, produced)
    taken = swap(send, "core")
    zi = lax.axis_index("dp")

    def chunk(i):
        return at(keep, (i + dp) % dp).astype(f32) + at(taken, (i + dp) % dp).astype(f32)

    def ring(moving, step):
        moving = shift(moving, "dp", 1).astype(f32) + chunk(zi - 2 - step)
        return moving if step == dp - 2 else moving.astype(bf16)

    grad_second = dg(spread, returned, 0, 0)
    grad_middle = dy + norm_back(grad_second * norm2_gain, xh2, rstd2)
    branch = grad_middle.astype(bf16)
    attT_grad = dg(w_output, branch, 1, 1).astype(bf16).reshape(ctx, heads, HD, rows)
    do_first, do_later = turn(attT_grad[:, :1]), turn(attT_grad[:, 1:])

    go = dg(attT, branch, 1, 0).reshape(nx, 2, mine, D)
    router_rows = (jnp.arange(experts) == expert_id).astype(f32)[:, None] * router_row
    sig = jnp.pad(jnp.sum(hot * gating[:, None], axis=0), (0, D - experts))
    small = jnp.concatenate([router_rows, jnp.sum(grad_second * xh2, axis=0)[None], sig[None]], axis=0)
    small = jnp.pad(small, ((0, -small.shape[0] % 8), (0, 0)))
    go_send = lax.dynamic_index_in_dim(go, 1 - ci, 1, keepdims=False).astype(bf16).reshape(-1, D)
    go_send = jnp.concatenate([go_send, two(small)], axis=0)
    go_keep = lax.dynamic_index_in_dim(go, ci, 1, keepdims=False)

    moving = chunk(zi - 1).astype(bf16)
    do_first, moving, go_send = tie(do_first, moving, go_send)
    moving = ring(moving, 0)
    go_got = swap(go_send, "core")
    so_far = attend_back(qkvT, kv, do_first, 0, oT, lse, 0, None)
    do_later, go_got, produced, *so_far = tie(do_later, go_got, produced, *so_far)
    go = go_keep + go_got[: nx * mine].astype(f32).reshape(nx, mine, D)
    small = small + one(go_got[nx * mine :])
    go_got = swap(jnp.concatenate([at(go, 1 - xi).astype(bf16), two(small)], axis=0), "x")
    went_back = trade(produced)
    so_far = attend_back(qkvT, kv, do_later, 0, oT, lse, 1, so_far)
    go_got, moving, *so_far = tie(go_got, moving, *so_far)
    go = at(go, xi) + go_got[:mine].astype(f32)
    small = small + one(go_got[mine:])
    moving = ring(moving, 1)
    for h in range(2, heads):
        so_far = attend_back(qkvT, kv, do_later, h - 1, oT, lse, h, so_far)
    went_back, dT, dsend = tie(went_back, *so_far)
    output = (middle + gating[:, None] * dg(spread, went_back, 0, 0)).astype(bf16)
    got = turn(dsend)

    ei2 = ei if owners == 2 else jnp.zeros_like(ei)
    half, send = weight_rows(ei2, dT.reshape(3 * mine, length), normed_all, go, two(small))
    cut_at = half.shape[0]
    if owners == 2:
        gift = swap(send, "expert")
        gift, moving = tie(gift, moving)
        halves = [half + gift[:cut_at].astype(f32)]
        small = small + one(gift[cut_at:])
    else:
        halves = [lax.psum(half, "expert"), lax.psum(send[:cut_at].astype(f32), "expert")]
        small = lax.psum(small, "expert")
    pieces = []
    for part in halves:
        part = part.reshape(dp, -1, D)
        share = at(part, zi)
        more = small
        for step in range(1, dp):
            gift = jnp.concatenate([at(part, (zi + step) % dp).astype(bf16), two(small)], axis=0)
            gift = shift(gift, "dp", step)
            share = share + gift[: share.shape[0]].astype(f32)
            more = more + one(gift[share.shape[0] :])
        share = share.astype(bf16)
        pieces.append(jnp.concatenate([share] + [shift(share, "dp", step) for step in range(1, dp)], axis=0))
    small = more
    for step in range(2, dp - 1):
        moving = ring(moving, step)

    if owners == 2:
        pieces.append(swap(pieces[0], "expert"))
    pieces += [swap(piece, "x") for piece in pieces]
    pieces += [swap(piece, "core") for piece in pieces]
    me = jnp.stack([zi, xi, ci, ei2]).astype(jnp.int32)
    *grads, grad_norm1 = finish(me, pieces, (w_query, w_key, w_value), dp)
    grad_norm1 = grad_norm1.reshape(D) / norm1_gain

    grad_normed = 0.0
    for p, w in enumerate((w_query, w_key, w_value)):
        grad_normed = grad_normed + dg(got[:, p].reshape(D, rows), w, 0, 1)
    xh1, rstd1 = normal_form(flat)
    grad_tokens = grad_middle + norm_back(grad_normed * norm1_gain, xh1, rstd1)

    own = lax.dynamic_index_in_dim(moving, xi, 1, keepdims=False)
    moved = swap(lax.dynamic_index_in_dim(moving, 1 - xi, 1, keepdims=False).astype(bf16), "x").astype(f32)
    first, latter = jnp.where(xi == 0, own, moved), jnp.where(xi == 0, moved, own)
    both = jnp.stack([first, latter], axis=1)
    grad_in = jnp.swapaxes(both[0], 1, 2)
    grad_out = both[1]

    grad_router = jnp.transpose(small[:experts])
    grad_norm2 = small[experts]
    total_sig = small[experts + 1, :experts]
    balance = balance_weight * jnp.sum((counts - mean_load) / mean_load * total_sig) / mean_load

    return (
        output.reshape(1, rows, D),
        grad_tokens.reshape(1, rows, D),
        grad_norm1,
        grads[0],
        grads[1],
        grads[2],
        grads[3],
        grad_norm2,
        grad_router,
        grad_in,
        grad_out,
        balance,
    )


def solution(mesh):
    dp, ctx, owners = mesh.shape["dp"], mesh.shape["ctx"], mesh.shape["expert"]
    split = Mesh(mesh.devices.reshape(dp, ctx // 2, 2, owners), ("dp", "x", "core", "expert"))
    token = P(("dp", "expert"), ("x", "core"), None)
    return jax.shard_map(
        per_device,
        mesh=split,
        in_specs=(token, token, token, P(), P(), P(), P(), P(), P(), P(), P("expert"), P("expert")),
        out_specs=(
            token,
            token,
            P(),
            P(),
            P(),
            P(),
            P(),
            P(),
            P(),
            P("expert", None, ("dp", "x", "core")),
            P("expert", ("dp", "x", "core"), None),
            P(),
        ),
        check_vma=False,
    )
```

```python
import functools

import jax
import jax.numpy as jnp
from jax import lax
from jax.experimental import pallas as pl
from jax.experimental.pallas import tpu as pltpu
from jax.sharding import Mesh
from jax.sharding import PartitionSpec as P

D = 768
HEADS = 12
HD = 64
norm_eps = 1e-05
balance_weight = 1.0
LOG2E = 1.4426950408889634
MASKED = -1e30
GELU_A = 0.7978845608028654
GELU_B = 0.044715
VMEM = 56 * 1024 * 1024
f32 = jnp.float32
bf16 = jnp.bfloat16


def dg(a, b, ca, cb):
    return lax.dot_general(a, b, (((ca,), (cb,)), ((), ())), preferred_element_type=f32)


def project_kernel(place_ref, tok_ref, gain_ref, w_ref, *refs):
    normed_ref, qkvT_ref, kv_ref = refs[-3:]
    x = tok_ref[...].astype(f32)
    centred = x - jnp.mean(x, axis=1, keepdims=True)
    rstd = lax.rsqrt(jnp.mean(centred * centred, axis=1, keepdims=True) + norm_eps)
    normed = (centred * rstd * gain_ref[...]).astype(bf16)
    normed_ref[...] = normed
    qkv = dg(normed, w_ref[...], 1, 0).astype(bf16)
    kv_ref[...] = qkv[:, qkv.shape[1] - kv_ref.shape[1] :]
    qkvT_ref[...] = qkv.T


def project(place, tok, gain, w, ctx, so_far):
    rows = tok.shape[0]
    wide = w.shape[1]
    args = [tok, gain, w]
    specs = [pl.BlockSpec(a.shape, lambda i, p: (0, 0)) for a in args]
    alias = {}
    if so_far is not None:
        alias = {4: 0, 5: 1, 6: 2}
        args += list(so_far)
        specs += [pl.BlockSpec(memory_space=pl.ANY)] * 3
    return pl.pallas_call(
        project_kernel,
        out_shape=(
            jax.ShapeDtypeStruct((ctx * rows, D), bf16),
            jax.ShapeDtypeStruct((wide, ctx * rows), bf16),
            jax.ShapeDtypeStruct((ctx * rows, 2 * wide // 3), bf16),
        ),
        grid_spec=pltpu.PrefetchScalarGridSpec(
            num_scalar_prefetch=1,
            grid=(1,),
            in_specs=specs,
            out_specs=(
                pl.BlockSpec((rows, D), lambda i, p: (p[0], 0)),
                pl.BlockSpec((wide, rows), lambda i, p: (0, p[0])),
                pl.BlockSpec((rows, 2 * wide // 3), lambda i, p: (p[0], 0)),
            ),
        ),
        input_output_aliases=alias,
        compiler_params=pltpu.CompilerParams(vmem_limit_bytes=VMEM),
        cost_estimate=pl.CostEstimate(
            flops=4 * rows * D * wide, bytes_accessed=4 * rows * D + 8 * rows * wide, transcendentals=0
        ),
        name="project",
    )(place.astype(jnp.int32).reshape(1), *args)


def attend_kernel(heads, blk, qT_ref, k_ref, vT_ref, oT_ref, osend_ref, lse_ref):
    length = qT_ref.shape[1]
    per = osend_ref.shape[3]
    c = (HD**-0.5) * LOG2E
    rows = lax.broadcasted_iota(jnp.int32, (blk, blk), 0)
    cols = lax.broadcasted_iota(jnp.int32, (blk, blk), 1)
    keep = rows <= cols
    for h in range(heads):
        hs = slice(h * HD, (h + 1) * HD)
        for i in range(length // blk):
            a, b = i * blk, (i + 1) * blk
            q = qT_ref[hs, a:b]
            sd = dg(k_ref[a:b, hs], q, 1, 0)
            sd = jnp.where(keep, sd, MASKED)
            m = jnp.max(sd, axis=0, keepdims=True)
            if i:
                s = dg(k_ref[:a, hs], q, 1, 0)
                m = jnp.maximum(m, jnp.max(s, axis=0, keepdims=True))
            mc = m * c
            pd = jnp.exp2(sd * c - mc)
            total = jnp.sum(pd, axis=0, keepdims=True)
            o = dg(vT_ref[hs, a:b], pd.astype(bf16), 1, 0)
            if i:
                p = jnp.exp2(s * c - mc)
                total = total + jnp.sum(p, axis=0, keepdims=True)
                o = o + dg(vT_ref[hs, :a], p.astype(bf16), 1, 0)
            o = o / total
            oT_ref[hs, a:b] = o
            d, off = a // per, a % per
            osend_ref[d, h, :, off : off + blk] = o.astype(bf16)
            lse_ref[h, :, a:b] = mc + jnp.log2(total)


def attend(qkvT, kv, dests):
    length = kv.shape[0]
    heads = qkvT.shape[0] // (3 * HD)
    wide = heads * HD
    per = length // dests
    return pl.pallas_call(
        functools.partial(attend_kernel, heads, per),
        out_shape=(
            jax.ShapeDtypeStruct((wide, length), f32),
            jax.ShapeDtypeStruct((dests, heads, HD, per), bf16),
            jax.ShapeDtypeStruct((heads, 1, length), f32),
        ),
        grid=(1,),
        in_specs=[
            pl.BlockSpec((wide, length), lambda i: (0, 0)),
            pl.BlockSpec(kv.shape, lambda i: (0, 0)),
            pl.BlockSpec((wide, length), lambda i: (2, 0)),
        ],
        out_specs=(
            pl.BlockSpec((wide, length), lambda i: (0, 0)),
            pl.BlockSpec((dests, heads, HD, per), lambda i: (0, 0, 0, 0)),
            pl.BlockSpec((heads, 1, length), lambda i: (0, 0, 0)),
        ),
        compiler_params=pltpu.CompilerParams(vmem_limit_bytes=VMEM),
        cost_estimate=pl.CostEstimate(
            flops=8 * heads * length * length * HD,
            bytes_accessed=length * wide * 14,
            transcendentals=heads * length * length // 2,
        ),
        name="attend",
    )(qkvT, kv, qkvT)


def attend_back_kernel(lk, lv, blk, *refs):
    qT_ref, k_ref, kT_ref, v_ref, do_ref, oT_ref, lse_ref = refs[:7]
    dT_ref, dsend_ref, dk_acc, dv_acc = refs[-4:]
    length = qT_ref.shape[1]
    per = do_ref.shape[3]
    sc = HD**-0.5
    c = sc * LOG2E
    rows = lax.broadcasted_iota(jnp.int32, (blk, blk), 0)
    cols = lax.broadcasted_iota(jnp.int32, (blk, blk), 1)
    keep = rows <= cols
    n = length // blk
    for i in reversed(range(n)):
        x0, x1 = i * blk, (i + 1) * blk
        d, off = x0 // per, x0 % per
        q = qT_ref[:, x0:x1]
        do = do_ref[d, 0, :, off : off + blk]
        lse = lse_ref[0, :, x0:x1]
        delta = jnp.sum(do.astype(f32) * oT_ref[:, x0:x1], axis=0, keepdims=True)
        dq = None
        for a, b, diag in ([(0, x0, False)] if i else []) + [(x0, x1, True)]:
            s = dg(k_ref[a:b, lk : lk + HD], q, 1, 0)
            p = jnp.exp2(s * c - lse)
            if diag:
                p = jnp.where(keep, p, 0.0)
            dp = dg(v_ref[a:b, lv : lv + HD], do, 1, 0)
            ds = (p * (dp - delta)).astype(bf16)
            dvn = dg(do, p.astype(bf16), 1, 1)
            dkn = dg(q, ds, 1, 1)
            if i == n - 1:
                dv_acc[:, a:b] = dvn
                dk_acc[:, a:b] = dkn
            else:
                dv_acc[:, a:b] += dvn
                dk_acc[:, a:b] += dkn
            t = dg(kT_ref[:, a:b], ds, 1, 0)
            dq = t if dq is None else dq + t
        dq = (dq * sc).astype(bf16)
        dT_ref[0, :, x0:x1] = dq
        dsend_ref[d, 0, :, off : off + blk] = dq
    for d in range(dsend_ref.shape[0]):
        at_d = slice(d * per, (d + 1) * per)
        dk = (dk_acc[:, at_d] * sc).astype(bf16)
        dv = dv_acc[:, at_d].astype(bf16)
        dT_ref[1, :, at_d] = dk
        dT_ref[2, :, at_d] = dv
        dsend_ref[d, 1] = dk
        dsend_ref[d, 2] = dv


def attend_back(qkvT, kv, do, slot, oT, lse, h, so_far):
    length = kv.shape[0]
    n = qkvT.shape[0] // (3 * HD)
    dests, _, _, per = do.shape
    hv = n + h
    blk = min(256, per)
    args = [qkvT, kv, qkvT, kv, do, oT, lse]
    specs = [
        pl.BlockSpec((HD, length), lambda i: (h, 0)),
        pl.BlockSpec((length, 2 * HD), lambda i: (0, h // 2)),
        pl.BlockSpec((HD, length), lambda i: (n + h, 0)),
        pl.BlockSpec((length, 2 * HD), lambda i: (0, hv // 2)),
        pl.BlockSpec((dests, 1, HD, per), lambda i: (0, slot, 0, 0)),
        pl.BlockSpec((HD, length), lambda i: (h, 0)),
        pl.BlockSpec((1, 1, length), lambda i: (h, 0, 0)),
    ]
    alias = {}
    if so_far is not None:
        alias = {len(args): 0, len(args) + 1: 1}
        args += list(so_far)
        specs += [pl.BlockSpec(memory_space=pl.ANY)] * 2
    return pl.pallas_call(
        functools.partial(attend_back_kernel, (h % 2) * HD, (hv % 2) * HD, blk),
        out_shape=(
            jax.ShapeDtypeStruct((3, n * HD, length), bf16),
            jax.ShapeDtypeStruct((dests, 3, n * HD, per), bf16),
        ),
        grid=(1,),
        in_specs=specs,
        out_specs=(
            pl.BlockSpec((3, HD, length), lambda i: (0, h, 0)),
            pl.BlockSpec((dests, 3, HD, per), lambda i: (0, 0, h, 0)),
        ),
        scratch_shapes=[pltpu.VMEM((HD, length), f32)] * 2,
        input_output_aliases=alias,
        compiler_params=pltpu.CompilerParams(vmem_limit_bytes=VMEM),
        cost_estimate=pl.CostEstimate(
            flops=20 * length * length * HD, bytes_accessed=length * HD * 24, transcendentals=length * length // 2
        ),
        name=f"attend_back_head{h}",
    )(*args)


def up_kernel(pick_ref, dy_ref, wo_ref, u_ref):
    u_ref[...] = dg(dy_ref[...], wo_ref[0], 1, 1).astype(bf16)


def expert_up(pick, dy, w_out, fc=768):
    rows = dy.shape[0]
    ff = w_out.shape[1]
    return pl.pallas_call(
        up_kernel,
        out_shape=jax.ShapeDtypeStruct((rows, ff), bf16),
        grid_spec=pltpu.PrefetchScalarGridSpec(
            num_scalar_prefetch=1,
            grid=(ff // fc,),
            in_specs=[
                pl.BlockSpec((rows, D), lambda f, p: (0, 0)),
                pl.BlockSpec((1, fc, D), lambda f, p: (p[0], f, 0)),
            ],
            out_specs=pl.BlockSpec((rows, fc), lambda f, p: (0, f)),
        ),
        compiler_params=pltpu.CompilerParams(vmem_limit_bytes=VMEM),
        cost_estimate=pl.CostEstimate(
            flops=2 * rows * D * ff, bytes_accessed=2 * (rows * D + ff * D + rows * ff), transcendentals=0
        ),
        name="expert_up",
    )(pick, dy, w_out)


def mid_kernel(
    pick_ref, x_ref, u_ref, wi_ref, wr_ref, load_ref, act_ref, gh_ref, rows_ref, router_ref, gate_ref, acc, gg, gate
):
    f = pl.program_id(0)
    n = pl.num_programs(0)

    @pl.when(f == 0)
    def _():
        logit = jnp.sum(x_ref[...].astype(f32) * wr_ref[...], axis=1, keepdims=True)
        gate[...] = jnp.broadcast_to(jax.nn.sigmoid(logit), gate.shape)

    h = dg(x_ref[...], wi_ref[0], 1, 0)
    h2 = h * h
    t = jnp.tanh(h * (GELU_A + (GELU_A * GELU_B) * h2))
    hp = 0.5 + 0.5 * t
    dgelu = hp + (0.5 * h) * (1.0 - t * t) * (GELU_A + (3.0 * GELU_A * GELU_B) * h2)
    u = u_ref[...].astype(f32)
    act = (h * hp).astype(bf16)
    act_ref[...] = act
    g1 = jnp.sum(act.astype(f32) * u, axis=1, keepdims=True)
    gh = (gate[:, :1] * u * dgelu).astype(bf16)
    gh_ref[...] = gh
    part = dg(gh, wi_ref[0], 1, 1)

    @pl.when(f == 0)
    def _():
        acc[...] = part
        gg[...] = jnp.broadcast_to(g1, gg.shape)

    @pl.when(f > 0)
    def _():
        acc[...] += part
        gg[...] += g1

    @pl.when(f == n - 1)
    def _():
        g = gate[:, :1]
        sel = (g * (1.0 - g) * (gg[:, :1] + load_ref[:, :1])).astype(bf16).astype(f32)
        rows_ref[...] = (acc[...] + sel * wr_ref[...]).astype(bf16)
        router_ref[...] = jnp.sum(x_ref[...].astype(f32) * sel, axis=0, keepdims=True)
        gate_ref[...] = gate[...]


def expert_mid(pick, x, u, w_in, wr, load, fc=768):
    rows = x.shape[0]
    ff = w_in.shape[2]

    def full(s):
        return pl.BlockSpec(s, lambda f, p: (0, 0))

    wide = pl.BlockSpec((rows, fc), lambda f, p: (0, f))
    return pl.pallas_call(
        mid_kernel,
        out_shape=(
            jax.ShapeDtypeStruct((rows, ff), bf16),
            jax.ShapeDtypeStruct((rows, ff), bf16),
            jax.ShapeDtypeStruct((rows, D), bf16),
            jax.ShapeDtypeStruct((1, D), f32),
            jax.ShapeDtypeStruct((rows, 128), f32),
        ),
        grid_spec=pltpu.PrefetchScalarGridSpec(
            num_scalar_prefetch=1,
            grid=(ff // fc,),
            in_specs=[
                full((rows, D)),
                wide,
                pl.BlockSpec((1, D, fc), lambda f, p: (p[0], 0, f)),
                full((1, D)),
                full((1, 128)),
            ],
            out_specs=(wide, wide, full((rows, D)), full((1, D)), full((rows, 128))),
            scratch_shapes=[
                pltpu.VMEM((rows, D), f32),
                pltpu.VMEM((rows, 128), f32),
                pltpu.VMEM((rows, 128), f32),
            ],
        ),
        compiler_params=pltpu.CompilerParams(vmem_limit_bytes=VMEM),
        cost_estimate=pl.CostEstimate(
            flops=4 * rows * D * ff,
            bytes_accessed=2 * (3 * rows * D + ff * D + 3 * rows * ff),
            transcendentals=rows * ff,
        ),
        name="expert_mid",
    )(pick, x, u, w_in, wr, load)


def grads_kernel(
    pick_ref, x_ref, dy_ref, gate_ref, act_ref, gh_ref, wo_ref, keep_ref, send_ref, prod_ref, acc, go, gi, gexp
):
    f = pl.program_id(0)
    n = pl.num_programs(0)

    @pl.when(f == 0)
    def _():
        gexp[...] = (dy_ref[...].astype(f32) * gate_ref[:, :1]).astype(bf16)

    go[...] = dg(act_ref[...], gexp[...], 0, 0).astype(bf16)
    gi[...] = dg(gh_ref[...], x_ref[...], 0, 0).astype(bf16)
    part = dg(act_ref[...], wo_ref[0], 1, 0)

    @pl.when(f == 0)
    def _():
        acc[...] = part

    @pl.when(f > 0)
    def _():
        acc[...] += part

    w = keep_ref.shape[3]
    me = pick_ref[1]
    for xx in range(keep_ref.shape[2]):
        a = pl.multiple_of((2 * xx + me) * w, w)
        b = pl.multiple_of((2 * xx + 1 - me) * w, w)
        keep_ref[0, 0, xx] = gi[pl.ds(a, w)]
        keep_ref[0, 1, xx] = go[pl.ds(a, w)]
        send_ref[0, 0, xx] = gi[pl.ds(b, w)]
        send_ref[0, 1, xx] = go[pl.ds(b, w)]

    @pl.when(f == n - 1)
    def _():
        prod_ref[...] = acc[...].astype(bf16)


def expert_grads(pick, x, dy, gate, act, gh, w_out, dp, nx):
    rows = x.shape[0]
    ff = w_out.shape[1]
    fc = ff // dp
    w = fc // (2 * nx)

    def full(s):
        return pl.BlockSpec(s, lambda f, p: (0, 0))

    wide = pl.BlockSpec((rows, fc), lambda f, p: (0, f))
    part = jax.ShapeDtypeStruct((dp, 2, nx, w, D), bf16)
    part_spec = pl.BlockSpec((1, 2, nx, w, D), lambda f, p: (f, 0, 0, 0, 0))
    return pl.pallas_call(
        grads_kernel,
        out_shape=(part, part, jax.ShapeDtypeStruct((rows, D), bf16)),
        grid_spec=pltpu.PrefetchScalarGridSpec(
            num_scalar_prefetch=1,
            grid=(dp,),
            in_specs=[
                full((rows, D)),
                full((rows, D)),
                full((rows, 128)),
                wide,
                wide,
                pl.BlockSpec((1, fc, D), lambda f, p: (p[0], f, 0)),
            ],
            out_specs=(part_spec, part_spec, full((rows, D))),
            scratch_shapes=[
                pltpu.VMEM((rows, D), f32),
                pltpu.VMEM((fc, D), bf16),
                pltpu.VMEM((fc, D), bf16),
                pltpu.VMEM((rows, D), bf16),
            ],
        ),
        compiler_params=pltpu.CompilerParams(vmem_limit_bytes=VMEM),
        cost_estimate=pl.CostEstimate(
            flops=6 * rows * D * ff,
            bytes_accessed=2 * (3 * rows * D + 3 * ff * D + 2 * rows * ff),
            transcendentals=0,
        ),
        name="expert_grads",
    )(pick, x, dy, gate, act, gh, w_out)


def one_hot_slots(slot, slots):
    return (lax.broadcasted_iota(jnp.int32, (slots, slot.shape[1]), 0) == slot).astype(f32).astype(bf16)


def halves_of(v):
    high = v.astype(bf16)
    return jnp.concatenate([high, (v - high.astype(f32)).astype(bf16)], axis=0)


def sum_halves(v):
    v = v.astype(f32)
    n = v.shape[0] // 2
    return v[:n] + v[n:]


def branch_kernel(
    norm_row,
    me_ref,
    back_ref,
    slot_ref,
    dy_ref,
    middle_ref,
    gain_ref,
    w_ref,
    att_ref,
    early_ref,
    grad_ref,
    heads_ref,
    keep_ref,
    send_ref,
    small_ref,
    acc,
):
    g = dg(one_hot_slots(slot_ref[...], back_ref.shape[0]), back_ref[...], 0, 0)
    v = middle_ref[...]
    centred = v - jnp.mean(v, axis=1, keepdims=True)
    rstd = lax.rsqrt(jnp.mean(centred * centred, axis=1, keepdims=True) + norm_eps)
    xh = centred * rstd
    dn = g * gain_ref[...]
    grad = rstd * (dn - jnp.mean(dn, axis=1, keepdims=True) - xh * jnp.mean(dn * xh, axis=1, keepdims=True))
    grad = dy_ref[...].astype(f32) + grad
    grad_ref[...] = grad
    low = grad.astype(bf16)
    heads_ref[...] = dg(w_ref[...], low, 1, 1).astype(bf16).reshape(heads_ref.shape)
    row = lax.broadcasted_iota(jnp.int32, small_ref.shape, 0)
    small = early_ref[...] + jnp.where(row == norm_row, jnp.sum(g * xh, axis=0, keepdims=True), 0.0)
    small_ref[...] = small
    acc[...] = dg(att_ref[...], low, 1, 0)
    nx, w, _ = keep_ref.shape
    for x in range(nx):
        keep_ref[x] = acc[pl.ds(pl.multiple_of((2 * x + me_ref[0]) * w, w), w)]
        send_ref[x * w : (x + 1) * w] = acc[pl.ds(pl.multiple_of((2 * x + 1 - me_ref[0]) * w, w), w)].astype(bf16)
    send_ref[nx * w :] = halves_of(small)


def whole_block(shape):
    return pl.BlockSpec(shape, lambda i, p: (0,) * len(shape))


def one_step(kernel, name, outs, args, scratch, flops):
    return pl.pallas_call(
        kernel,
        out_shape=tuple(jax.ShapeDtypeStruct(shape, dtype) for shape, dtype in outs),
        grid_spec=pltpu.PrefetchScalarGridSpec(
            num_scalar_prefetch=1,
            grid=(1,),
            in_specs=[whole_block(a.shape) for a in args[1:]],
            out_specs=tuple(whole_block(shape) for shape, _ in outs),
            scratch_shapes=scratch,
        ),
        compiler_params=pltpu.CompilerParams(vmem_limit_bytes=VMEM),
        cost_estimate=pl.CostEstimate(
            flops=flops, bytes_accessed=4 * sum(a.size for a in args), transcendentals=0
        ),
        name=name,
    )(*args)


def branch_back(ci, back, slot, dy, middle, gain, w, attT, early, norm_row, ctx):
    rows = dy.shape[0]
    mine = D // ctx
    outs = (
        ((rows, D), f32),
        ((ctx, HEADS // ctx, HD, rows), bf16),
        ((ctx // 2, mine, D), f32),
        ((ctx // 2 * mine + 2 * early.shape[0], D), bf16),
        (early.shape, f32),
    )
    return one_step(
        functools.partial(branch_kernel, norm_row),
        "branch_back",
        outs,
        (ci, back, slot, dy, middle, gain, w, attT, early),
        [pltpu.VMEM((D, D), f32)],
        2 * rows * D * (back.shape[0] + 2 * D),
    )


def go_kernel(me_ref, keep_ref, got_ref, small_ref, own_ref, send_ref, sum_ref, acc):
    nx, w, _ = keep_ref.shape
    for x in range(nx):
        acc[x] = keep_ref[x] + got_ref[x * w : (x + 1) * w].astype(f32)
    small = small_ref[...] + sum_halves(got_ref[nx * w :])
    sum_ref[...] = small
    own_ref[...] = acc[me_ref[0]]
    send_ref[:w] = acc[1 - me_ref[0]].astype(bf16)
    send_ref[w:] = halves_of(small)


def go_step(xi, keep, got, small):
    w = keep.shape[1]
    outs = (((w, D), f32), ((w + 2 * small.shape[0], D), bf16), (small.shape, f32))
    return one_step(go_kernel, "go_step", outs, (xi, keep, got, small), [pltpu.VMEM(keep.shape, f32)], 0)


def weight_rows_kernel(half_ref, dT_ref, normed_ref, go_ref, got_ref, early_ref, keep_ref, send_ref, small_ref, acc):
    n = dT_ref.shape[0]
    w = go_ref.shape[0]
    half = keep_ref.shape[0]
    acc[:n] = dg(dT_ref[...], normed_ref[...], 1, 0)
    acc[n:] = go_ref[...] + got_ref[:w].astype(f32)
    small = early_ref[...] + sum_halves(got_ref[w:])
    small_ref[...] = small
    a = pl.multiple_of(half_ref[0] * half, half)
    b = pl.multiple_of((1 - half_ref[0]) * half, half)
    keep_ref[...] = acc[pl.ds(a, half)]
    send_ref[:half] = acc[pl.ds(b, half)].astype(bf16)
    send_ref[half:] = halves_of(small)


def weight_rows(half, dT, normed, go, got, small):
    rows = dT.shape[0] + go.shape[0]
    outs = (((rows // 2, D), f32), ((rows // 2 + 2 * small.shape[0], D), bf16), (small.shape, f32))
    return one_step(
        weight_rows_kernel,
        "weight_rows",
        outs,
        (half, dT, normed, go, got, small),
        [pltpu.VMEM((rows, D), f32)],
        2 * dT.size * D,
    )


def share_kernel(me_ref, half_ref, got_ref, early_ref, own_ref, *refs):
    dp = len(refs) - 1
    sends, small_ref, acc = refs[: dp - 1], refs[dp - 1], refs[dp]
    half = half_ref.shape[0]
    w = half // dp
    acc[...] = half_ref[...] + got_ref[:half].astype(f32)
    small = early_ref[...] + sum_halves(got_ref[half:])
    small_ref[...] = small

    def share(step):
        return acc[pl.ds(pl.multiple_of(lax.rem(me_ref[0] + step, dp) * w, w), w)]

    own_ref[...] = share(0)
    for step in range(1, dp):
        sends[step - 1][:w] = share(step).astype(bf16)
        sends[step - 1][w:] = halves_of(small)


def share_step(zi, half, got, small, dp):
    w = half.shape[0] // dp
    outs = (((w, D), f32),) + (((w + 2 * small.shape[0], D), bf16),) * (dp - 1) + ((small.shape, f32),)
    return one_step(
        functools.partial(share_kernel),
        "share_step",
        outs,
        (zi, half, got, small),
        [pltpu.VMEM(half.shape, f32)],
        0,
    )


def finish_kernel(dp, me_ref, *refs):
    pieces = refs[:8]
    weights = refs[8:11]
    outs = refs[11:15]
    gain_ref = refs[15]
    got, wide, in_sem, out_sem = refs[16:]
    z, xi, ci, yi = me_ref[0], me_ref[1], me_ref[2], me_ref[3]
    rows = pieces[0].shape[0] // dp
    per = 4 * 2 // dp
    copies = []
    for n in range(8):
        c, x, y = (n // 4) ^ ci, ((n // 2) % 2) ^ xi, (n % 2) ^ yi
        for r in range(dp):
            j = y * dp + lax.rem(z + dp - r, dp)
            p = lax.div(j * 4, 2 * dp)
            first = (x * 2 + c) * (D // 4) + lax.rem(j, 2 * dp // 4) * rows
            copy = pltpu.make_async_copy(
                pieces[n].at[pl.ds(r * rows, rows)],
                got.at[p, pl.ds(pl.multiple_of(first, rows), rows)],
                in_sem.at[n, r],
            )
            copy.start()
            copies.append(copy)
    for copy in copies:
        copy.wait()
    del per
    gain = jnp.zeros((D, 1), f32)
    backs = []
    for p in range(4):
        if p < 3:
            g = got[p].T.astype(f32)
            gain = gain + jnp.sum(g * weights[p][...].astype(f32), axis=1, keepdims=True)
        else:
            g = got[p].astype(f32)
        wide[p] = g
        back = pltpu.make_async_copy(wide.at[p], outs[p], out_sem.at[p])
        back.start()
        backs.append(back)
    gain_ref[...] = gain
    for back in backs:
        back.wait()


def finish(me, pieces, weights, dp):
    whole = jax.ShapeDtypeStruct((D, D), f32)
    anywhere = pl.BlockSpec(memory_space=pl.ANY)
    return pl.pallas_call(
        functools.partial(finish_kernel, dp),
        out_shape=(whole,) * 4 + (jax.ShapeDtypeStruct((D, 1), f32),),
        grid_spec=pltpu.PrefetchScalarGridSpec(
            num_scalar_prefetch=1,
            grid=(1,),
            in_specs=[anywhere] * 8 + [pl.BlockSpec((D, D), lambda i, p: (0, 0))] * 3,
            out_specs=(anywhere,) * 4 + (pl.BlockSpec((D, 1), lambda i, p: (0, 0)),),
            scratch_shapes=[
                pltpu.VMEM((4, D, D), bf16),
                pltpu.VMEM((4, D, D), f32),
                pltpu.SemaphoreType.DMA((8, dp)),
                pltpu.SemaphoreType.DMA((4,)),
            ],
        ),
        compiler_params=pltpu.CompilerParams(vmem_limit_bytes=VMEM),
        cost_estimate=pl.CostEstimate(flops=8 * D * D, bytes_accessed=32 * D * D, transcendentals=0),
        name="finish",
    )(me, *pieces, *weights)


def swap(v, axis):
    return lax.ppermute(v, axis, [(0, 1), (1, 0)])


def shift(v, axis, step):
    n = lax.axis_size(axis)
    return lax.ppermute(v, axis, [(i, (i + step) % n) for i in range(n)])


def at(v, index):
    return lax.dynamic_index_in_dim(v, index, 0, keepdims=False)


def one(v):
    v = v.astype(f32)
    n = v.shape[0] // 2
    return v[:n] + v[n:]


def add_pair(v):
    return v + (swap(v, "expert") if lax.axis_size("expert") == 2 else lax.psum(v, "expert") - v)


def add_shifts(v):
    out = v
    for s in range(1, lax.axis_size("dp")):
        out = out + shift(v, "dp", s)
    return out


def index(i):
    return i.astype(jnp.int32).reshape(1)


def tie(*arrays):
    return lax.optimization_barrier(arrays)


def normal_form(v):
    centred = v - jnp.mean(v, axis=-1, keepdims=True)
    rstd = lax.rsqrt(jnp.mean(centred * centred, axis=-1, keepdims=True) + norm_eps)
    return centred * rstd, rstd


def norm_back(dn, xh, rstd):
    return rstd * (dn - jnp.mean(dn, axis=-1, keepdims=True) - xh * jnp.mean(dn * xh, axis=-1, keepdims=True))


def per_device(
    tokens,
    cotangent,
    routes,
    norm1_gain,
    w_query,
    w_key,
    w_value,
    w_output,
    norm2_gain,
    w_router,
    w_in,
    w_out,
):
    rows = tokens.shape[1]
    nx, owners, dp = lax.axis_size("x"), lax.axis_size("expert"), lax.axis_size("dp")
    xi, ci, ei = lax.axis_index("x"), lax.axis_index("core"), lax.axis_index("expert")
    ctx = 2 * nx
    ctx_i = xi * 2 + ci
    length = ctx * rows
    experts = w_router.shape[1]
    cap = 2 * rows // experts
    mine = D // ctx
    heads = mine // HD
    pick = jnp.stack([xi, ci]).astype(jnp.int32)

    tok = tokens.reshape(rows, D)
    other = swap(tok, "x")
    near = swap(tok, "core")

    route = routes.reshape(rows)
    hot = (route[:, None] == jnp.arange(experts, dtype=jnp.int32)[None, :]).astype(f32)
    lower = jnp.arange(rows)[:, None] >= jnp.arange(rows)[None, :]
    before = dg(lower.astype(bf16), hot.astype(bf16), 1, 0)
    rank = (jnp.sum(before * hot, axis=1) - 1.0).astype(jnp.int32)
    slot = ((route % nx) * owners + route // nx) * cap + rank
    spread = (jnp.arange(experts * cap, dtype=jnp.int32)[:, None] == slot[None, :]).astype(bf16)

    def pack(v):
        return dg(spread, v, 1, 0).astype(bf16).reshape(nx * owners, cap, D)

    def trade(v):
        v = lax.all_to_all(v.reshape(nx * owners, cap, D), ("x", "expert"), split_axis=0, concat_axis=0, tiled=True)
        return v.reshape(-1, D)

    def turn(v):
        return lax.all_to_all(v, ("x", "core"), split_axis=0, concat_axis=0, tiled=True)

    def cut(w):
        return lax.dynamic_slice(w, (0, ctx_i * mine), (D, mine))

    w_own = jnp.concatenate([cut(w_query), cut(w_key), cut(w_value)], axis=1)
    gain1 = norm1_gain.reshape(1, D)
    dy_low = cotangent.reshape(rows, D)
    dy = dy_low.astype(f32)
    counts = jnp.sum(hot, axis=0)
    counts = add_shifts(add_pair(counts))
    counts = counts + swap(counts, "core")
    so_far = project(ctx_i, tok, gain1, w_own, ctx, None)
    so_far = project(ctx_i ^ 1, near, gain1, w_own, ctx, so_far)
    dy_packed, counts, *so_far = tie(pack(dy_low), counts, *so_far)
    dy_rows = trade(dy_packed)
    other, *so_far = tie(other, *so_far)
    far = swap(other, "core")
    counts = counts + swap(tie(counts, other)[0], "x")
    so_far = project(ctx_i ^ 2, other, gain1, w_own, ctx, so_far)
    normed_all, qkvT, kv = project(ctx_i ^ 3, far, gain1, w_own, ctx, so_far)
    oT, osend, lse = attend(qkvT, kv, ctx)
    osend, dy_rows, counts = tie(osend, dy_rows, counts)
    attT = turn(osend).reshape(D, rows)

    mean_load = rows * ctx * dp * owners / experts
    load_term = balance_weight * (counts - mean_load) / (mean_load * mean_load)
    expert_id = ei * nx + xi
    load = jnp.broadcast_to(lax.dynamic_slice(load_term, (expert_id,), (1,)).reshape(1, 1), (1, 128))
    wr = lax.dynamic_slice(w_router, (0, expert_id), (D, 1)).astype(f32).reshape(1, D)

    flat = tok.astype(f32)
    middle = flat + dg(attT, w_output, 0, 0)
    xh2, rstd2 = normal_form(middle)
    second = (xh2 * norm2_gain).astype(bf16)
    gating = jax.nn.sigmoid(jnp.sum(hot * dg(second, w_router, 1, 0), axis=1))

    up = expert_up(pick, dy_rows, w_out)
    sig = jnp.pad(jnp.sum(hot * gating[:, None], axis=0), (0, D - experts))
    x_rows = trade(pack(second))
    x_rows, gating, sig = tie(x_rows, gating, sig)
    active, grad_hidden, back_rows, router_row, gate = expert_mid(pick, x_rows, up, w_in, wr, load)
    returned = trade(back_rows)
    keep, send, produced = expert_grads(pick, x_rows, dy_rows, gate, active, grad_hidden, w_out, dp, nx)
    returned, keep, send, produced = tie(returned, keep, send, produced)
    taken = swap(send, "core")
    zi = lax.axis_index("dp")

    def chunk(i):
        return at(keep, (i + dp) % dp).astype(f32) + at(taken, (i + dp) % dp).astype(f32)

    def ring(moving, step):
        moving = shift(moving, "dp", 1).astype(f32) + chunk(zi - 2 - step)
        return moving if step == dp - 2 else moving.astype(bf16)

    router_rows = (jnp.arange(experts) == expert_id).astype(f32)[:, None] * router_row
    small = jnp.concatenate([router_rows, jnp.zeros((1, D), f32), sig[None]], axis=0)
    small = jnp.pad(small, ((0, -small.shape[0] % 8), (0, 0)))
    grad_middle, heads_grad, go, go_send, small = branch_back(
        index(ci), returned, slot[None], dy_low, middle, norm2_gain.reshape(1, D), w_output, attT, small, experts, ctx
    )
    do = turn(heads_grad)

    go_got = swap(go_send, "core")
    moving = chunk(zi - 1).astype(bf16)
    go, go_send, small = go_step(index(xi), go, go_got, small)
    do, moving, go_send = tie(do, moving, go_send)
    moving = ring(moving, 0)
    go_got = swap(go_send, "x")

    so_far = attend_back(qkvT, kv, do, 0, oT, lse, 0, None)
    go_got, produced, *so_far = tie(go_got, produced, *so_far)
    went_back = trade(produced)
    so_far = attend_back(qkvT, kv, do, 1, oT, lse, 1, so_far)
    moving, *so_far = tie(moving, *so_far)
    moving = ring(moving, 1)
    for h in range(2, heads):
        so_far = attend_back(qkvT, kv, do, h, oT, lse, h, so_far)
    went_back, dT, dsend = tie(went_back, *so_far)
    output = (middle + gating[:, None] * dg(spread, went_back, 0, 0)).astype(bf16)
    got = turn(dsend)

    ei2 = ei if owners == 2 else jnp.zeros_like(ei)
    half, send, small = weight_rows(index(ei2), dT.reshape(3 * mine, length), normed_all, go, go_got, small)
    if owners == 2:
        gift = swap(send, "expert")
        gift, moving = tie(gift, moving)
        halves = [(half, gift)]
    else:
        cut_at = half.shape[0]
        small = lax.psum(small, "expert")
        nothing = jnp.zeros_like(send)
        halves = [(lax.psum(half, "expert"), nothing), (lax.psum(send[:cut_at].astype(f32), "expert"), nothing)]
    pieces = []
    for part, gift in halves:
        share, *gifts, more = share_step(index(zi), part, gift, small, dp)
        gifts = [shift(gift, "dp", step + 1) for step, gift in enumerate(gifts)]
        for gift in gifts:
            more = more + one(gift[share.shape[0] :])
            share = share + gift[: share.shape[0]].astype(f32)
        share = share.astype(bf16)
        pieces.append(jnp.concatenate([share] + [shift(share, "dp", step) for step in range(1, dp)], axis=0))
    small = more
    moving, *pieces = tie(moving, *pieces)
    for step in range(2, dp - 1):
        moving = ring(moving, step)

    if owners == 2:
        pieces.append(swap(pieces[0], "expert"))
    pieces += [swap(piece, "x") for piece in pieces]
    pieces += [swap(piece, "core") for piece in pieces]
    me = jnp.stack([zi, xi, ci, ei2]).astype(jnp.int32)
    *grads, grad_norm1 = finish(me, pieces, (w_query, w_key, w_value), dp)
    grad_norm1 = grad_norm1.reshape(D) / norm1_gain

    grad_normed = 0.0
    for p, w in enumerate((w_query, w_key, w_value)):
        grad_normed = grad_normed + dg(got[:, p].reshape(D, rows), w, 0, 1)
    xh1, rstd1 = normal_form(flat)
    grad_tokens = grad_middle + norm_back(grad_normed * norm1_gain, xh1, rstd1)

    own = lax.dynamic_index_in_dim(moving, xi, 1, keepdims=False)
    moved = swap(lax.dynamic_index_in_dim(moving, 1 - xi, 1, keepdims=False).astype(bf16), "x").astype(f32)
    first, latter = jnp.where(xi == 0, own, moved), jnp.where(xi == 0, moved, own)
    both = jnp.stack([first, latter], axis=1)
    grad_in = jnp.swapaxes(both[0], 1, 2)
    grad_out = both[1]

    grad_router = jnp.transpose(small[:experts])
    grad_norm2 = small[experts]
    total_sig = small[experts + 1, :experts]
    balance = balance_weight * jnp.sum((counts - mean_load) / mean_load * total_sig) / mean_load

    return (
        output.reshape(1, rows, D),
        grad_tokens.reshape(1, rows, D),
        grad_norm1,
        grads[0],
        grads[1],
        grads[2],
        grads[3],
        grad_norm2,
        grad_router,
        grad_in,
        grad_out,
        balance,
    )


def solution(mesh):
    dp, ctx, owners = mesh.shape["dp"], mesh.shape["ctx"], mesh.shape["expert"]
    split = Mesh(mesh.devices.reshape(dp, ctx // 2, 2, owners), ("dp", "x", "core", "expert"))
    token = P(("dp", "expert"), ("x", "core"), None)
    return jax.shard_map(
        per_device,
        mesh=split,
        in_specs=(token, token, token, P(), P(), P(), P(), P(), P(), P(), P("expert"), P("expert")),
        out_specs=(
            token,
            token,
            P(),
            P(),
            P(),
            P(),
            P(),
            P(),
            P(),
            P("expert", None, ("dp", "x", "core")),
            P("expert", ("dp", "x", "core"), None),
            P(),
        ),
        check_vma=False,
    )
```

```python
import functools

import jax
import jax.numpy as jnp
from jax import lax
from jax.experimental import pallas as pl
from jax.experimental.pallas import tpu as pltpu
from jax.sharding import Mesh
from jax.sharding import PartitionSpec as P

D = 768
HEADS = 12
HD = 64
norm_eps = 1e-05
balance_weight = 1.0
LOG2E = 1.4426950408889634
MASKED = -1e30
GELU_A = 0.7978845608028654
GELU_B = 0.044715
VMEM = 56 * 1024 * 1024
f32 = jnp.float32
bf16 = jnp.bfloat16


def dg(a, b, ca, cb):
    return lax.dot_general(a, b, (((ca,), (cb,)), ((), ())), preferred_element_type=f32)


def project_kernel(place_ref, tok_ref, gain_ref, w_ref, *refs):
    normed_ref, qkvT_ref, kv_ref = refs[-3:]
    x = tok_ref[...].astype(f32)
    centred = x - jnp.mean(x, axis=1, keepdims=True)
    rstd = lax.rsqrt(jnp.mean(centred * centred, axis=1, keepdims=True) + norm_eps)
    normed = (centred * rstd * gain_ref[...]).astype(bf16)
    normed_ref[...] = normed
    qkv = dg(normed, w_ref[...], 1, 0).astype(bf16)
    kv_ref[...] = qkv[:, qkv.shape[1] - kv_ref.shape[1] :]
    qkvT_ref[...] = qkv.T


def project(place, tok, gain, w, ctx, so_far):
    rows = tok.shape[0]
    wide = w.shape[1]
    args = [tok, gain, w]
    specs = [pl.BlockSpec(a.shape, lambda i, p: (0, 0)) for a in args]
    alias = {}
    if so_far is not None:
        alias = {4: 0, 5: 1, 6: 2}
        args += list(so_far)
        specs += [pl.BlockSpec(memory_space=pl.ANY)] * 3
    return pl.pallas_call(
        project_kernel,
        out_shape=(
            jax.ShapeDtypeStruct((ctx * rows, D), bf16),
            jax.ShapeDtypeStruct((wide, ctx * rows), bf16),
            jax.ShapeDtypeStruct((ctx * rows, 2 * wide // 3), bf16),
        ),
        grid_spec=pltpu.PrefetchScalarGridSpec(
            num_scalar_prefetch=1,
            grid=(1,),
            in_specs=specs,
            out_specs=(
                pl.BlockSpec((rows, D), lambda i, p: (p[0], 0)),
                pl.BlockSpec((wide, rows), lambda i, p: (0, p[0])),
                pl.BlockSpec((rows, 2 * wide // 3), lambda i, p: (p[0], 0)),
            ),
        ),
        input_output_aliases=alias,
        compiler_params=pltpu.CompilerParams(vmem_limit_bytes=VMEM),
        cost_estimate=pl.CostEstimate(
            flops=4 * rows * D * wide, bytes_accessed=4 * rows * D + 8 * rows * wide, transcendentals=0
        ),
        name="project",
    )(place.astype(jnp.int32).reshape(1), *args)


def attend_kernel(heads, blk, qT_ref, k_ref, vT_ref, oT_ref, osend_ref, lse_ref):
    length = qT_ref.shape[1]
    per = osend_ref.shape[3]
    c = (HD**-0.5) * LOG2E
    rows = lax.broadcasted_iota(jnp.int32, (blk, blk), 0)
    cols = lax.broadcasted_iota(jnp.int32, (blk, blk), 1)
    keep = rows <= cols
    for h in range(heads):
        hs = slice(h * HD, (h + 1) * HD)
        for i in range(length // blk):
            a, b = i * blk, (i + 1) * blk
            q = qT_ref[hs, a:b]
            sd = dg(k_ref[a:b, hs], q, 1, 0)
            sd = jnp.where(keep, sd, MASKED)
            m = jnp.max(sd, axis=0, keepdims=True)
            if i:
                s = dg(k_ref[:a, hs], q, 1, 0)
                m = jnp.maximum(m, jnp.max(s, axis=0, keepdims=True))
            mc = m * c
            pd = jnp.exp2(sd * c - mc)
            total = jnp.sum(pd, axis=0, keepdims=True)
            o = dg(vT_ref[hs, a:b], pd.astype(bf16), 1, 0)
            if i:
                p = jnp.exp2(s * c - mc)
                total = total + jnp.sum(p, axis=0, keepdims=True)
                o = o + dg(vT_ref[hs, :a], p.astype(bf16), 1, 0)
            o = o / total
            oT_ref[hs, a:b] = o
            d, off = a // per, a % per
            osend_ref[d, h, :, off : off + blk] = o.astype(bf16)
            lse_ref[h, :, a:b] = mc + jnp.log2(total)


def attend(qkvT, kv, dests):
    length = kv.shape[0]
    heads = qkvT.shape[0] // (3 * HD)
    wide = heads * HD
    per = length // dests
    return pl.pallas_call(
        functools.partial(attend_kernel, heads, per),
        out_shape=(
            jax.ShapeDtypeStruct((wide, length), f32),
            jax.ShapeDtypeStruct((dests, heads, HD, per), bf16),
            jax.ShapeDtypeStruct((heads, 1, length), f32),
        ),
        grid=(1,),
        in_specs=[
            pl.BlockSpec((wide, length), lambda i: (0, 0)),
            pl.BlockSpec(kv.shape, lambda i: (0, 0)),
            pl.BlockSpec((wide, length), lambda i: (2, 0)),
        ],
        out_specs=(
            pl.BlockSpec((wide, length), lambda i: (0, 0)),
            pl.BlockSpec((dests, heads, HD, per), lambda i: (0, 0, 0, 0)),
            pl.BlockSpec((heads, 1, length), lambda i: (0, 0, 0)),
        ),
        compiler_params=pltpu.CompilerParams(vmem_limit_bytes=VMEM),
        cost_estimate=pl.CostEstimate(
            flops=8 * heads * length * length * HD,
            bytes_accessed=length * wide * 14,
            transcendentals=heads * length * length // 2,
        ),
        name="attend",
    )(qkvT, kv, qkvT)


def attend_back_kernel(lk, lv, blk, *refs):
    qT_ref, k_ref, kT_ref, v_ref, do_ref, oT_ref, lse_ref = refs[:7]
    dT_ref, dsend_ref, dk_acc, dv_acc = refs[-4:]
    length = qT_ref.shape[1]
    per = do_ref.shape[3]
    sc = HD**-0.5
    c = sc * LOG2E
    rows = lax.broadcasted_iota(jnp.int32, (blk, blk), 0)
    cols = lax.broadcasted_iota(jnp.int32, (blk, blk), 1)
    keep = rows <= cols
    n = length // blk
    for i in reversed(range(n)):
        x0, x1 = i * blk, (i + 1) * blk
        d, off = x0 // per, x0 % per
        q = qT_ref[:, x0:x1]
        do = do_ref[d, 0, :, off : off + blk]
        lse = lse_ref[0, :, x0:x1]
        delta = jnp.sum(do.astype(f32) * oT_ref[:, x0:x1], axis=0, keepdims=True)
        dq = None
        for a, b, diag in ([(0, x0, False)] if i else []) + [(x0, x1, True)]:
            s = dg(k_ref[a:b, lk : lk + HD], q, 1, 0)
            p = jnp.exp2(s * c - lse)
            if diag:
                p = jnp.where(keep, p, 0.0)
            dp = dg(v_ref[a:b, lv : lv + HD], do, 1, 0)
            ds = (p * (dp - delta)).astype(bf16)
            dvn = dg(do, p.astype(bf16), 1, 1)
            dkn = dg(q, ds, 1, 1)
            if i == n - 1:
                dv_acc[:, a:b] = dvn
                dk_acc[:, a:b] = dkn
            else:
                dv_acc[:, a:b] += dvn
                dk_acc[:, a:b] += dkn
            t = dg(kT_ref[:, a:b], ds, 1, 0)
            dq = t if dq is None else dq + t
        dq = (dq * sc).astype(bf16)
        dT_ref[0, :, x0:x1] = dq
        dsend_ref[d, 0, :, off : off + blk] = dq
    for d in range(dsend_ref.shape[0]):
        at_d = slice(d * per, (d + 1) * per)
        dk = (dk_acc[:, at_d] * sc).astype(bf16)
        dv = dv_acc[:, at_d].astype(bf16)
        dT_ref[1, :, at_d] = dk
        dT_ref[2, :, at_d] = dv
        dsend_ref[d, 1] = dk
        dsend_ref[d, 2] = dv


def attend_back(qkvT, kv, do, slot, oT, lse, h, so_far):
    length = kv.shape[0]
    n = qkvT.shape[0] // (3 * HD)
    dests, _, _, per = do.shape
    hv = n + h
    blk = min(256, per)
    args = [qkvT, kv, qkvT, kv, do, oT, lse]
    specs = [
        pl.BlockSpec((HD, length), lambda i: (h, 0)),
        pl.BlockSpec((length, 2 * HD), lambda i: (0, h // 2)),
        pl.BlockSpec((HD, length), lambda i: (n + h, 0)),
        pl.BlockSpec((length, 2 * HD), lambda i: (0, hv // 2)),
        pl.BlockSpec((dests, 1, HD, per), lambda i: (0, slot, 0, 0)),
        pl.BlockSpec((HD, length), lambda i: (h, 0)),
        pl.BlockSpec((1, 1, length), lambda i: (h, 0, 0)),
    ]
    alias = {}
    if so_far is not None:
        alias = {len(args): 0, len(args) + 1: 1}
        args += list(so_far)
        specs += [pl.BlockSpec(memory_space=pl.ANY)] * 2
    return pl.pallas_call(
        functools.partial(attend_back_kernel, (h % 2) * HD, (hv % 2) * HD, blk),
        out_shape=(
            jax.ShapeDtypeStruct((3, n * HD, length), bf16),
            jax.ShapeDtypeStruct((dests, 3, n * HD, per), bf16),
        ),
        grid=(1,),
        in_specs=specs,
        out_specs=(
            pl.BlockSpec((3, HD, length), lambda i: (0, h, 0)),
            pl.BlockSpec((dests, 3, HD, per), lambda i: (0, 0, h, 0)),
        ),
        scratch_shapes=[pltpu.VMEM((HD, length), f32)] * 2,
        input_output_aliases=alias,
        compiler_params=pltpu.CompilerParams(vmem_limit_bytes=VMEM),
        cost_estimate=pl.CostEstimate(
            flops=20 * length * length * HD, bytes_accessed=length * HD * 24, transcendentals=length * length // 2
        ),
        name=f"attend_back_head{h}",
    )(*args)


def up_kernel(pick_ref, dy_ref, wo_ref, u_ref):
    u_ref[...] = dg(dy_ref[...], wo_ref[0], 1, 1).astype(bf16)


def expert_up(pick, dy, w_out, fc=768):
    rows = dy.shape[0]
    ff = w_out.shape[1]
    return pl.pallas_call(
        up_kernel,
        out_shape=jax.ShapeDtypeStruct((rows, ff), bf16),
        grid_spec=pltpu.PrefetchScalarGridSpec(
            num_scalar_prefetch=1,
            grid=(ff // fc,),
            in_specs=[
                pl.BlockSpec((rows, D), lambda f, p: (0, 0)),
                pl.BlockSpec((1, fc, D), lambda f, p: (p[0], f, 0)),
            ],
            out_specs=pl.BlockSpec((rows, fc), lambda f, p: (0, f)),
        ),
        compiler_params=pltpu.CompilerParams(vmem_limit_bytes=VMEM),
        cost_estimate=pl.CostEstimate(
            flops=2 * rows * D * ff, bytes_accessed=2 * (rows * D + ff * D + rows * ff), transcendentals=0
        ),
        name="expert_up",
    )(pick, dy, w_out)


def mid_kernel(
    pick_ref, x_ref, u_ref, wi_ref, wr_ref, load_ref, act_ref, gh_ref, rows_ref, router_ref, gate_ref, acc, gg, gate
):
    f = pl.program_id(0)
    n = pl.num_programs(0)

    @pl.when(f == 0)
    def _():
        logit = jnp.sum(x_ref[...].astype(f32) * wr_ref[...], axis=1, keepdims=True)
        gate[...] = jnp.broadcast_to(jax.nn.sigmoid(logit), gate.shape)
        acc[...] = jnp.zeros_like(acc)
        gg[...] = jnp.zeros_like(gg)

    step = 256
    for r in range(0, x_ref.shape[0], step):
        rs = slice(r, r + step)
        for c in range(0, wi_ref.shape[2], step):
            cs = slice(c, c + step)
            h = dg(x_ref[rs], wi_ref[0, :, cs], 1, 0)
            h2 = h * h
            t = jnp.tanh(h * (GELU_A + (GELU_A * GELU_B) * h2))
            hp = 0.5 + 0.5 * t
            dgelu = hp + (h * (hp - hp * hp)) * (2.0 * GELU_A + (6.0 * GELU_A * GELU_B) * h2)
            u = u_ref[rs, cs].astype(f32)
            active = h * hp
            act_ref[rs, cs] = active.astype(bf16)
            au = active * u
            lanes = au[:, :128]
            for j in range(128, step, 128):
                lanes = lanes + au[:, j : j + 128]
            gg[rs] += lanes
            gh = (gate[rs, :1] * (u * dgelu)).astype(bf16)
            gh_ref[rs, cs] = gh
            acc[rs] += dg(gh, wi_ref[0, :, cs], 1, 1)

    @pl.when(f == n - 1)
    def _():
        g = gate[:, :1]
        got = jnp.sum(gg[...], axis=1, keepdims=True)
        sel = (g * (1.0 - g) * (got + load_ref[:, :1])).astype(bf16).astype(f32)
        rows_ref[...] = (acc[...] + sel * wr_ref[...]).astype(bf16)
        router_ref[...] = jnp.sum(x_ref[...].astype(f32) * sel, axis=0, keepdims=True)
        gate_ref[...] = gate[...]


def expert_mid(pick, x, u, w_in, wr, load, fc=768):
    rows = x.shape[0]
    ff = w_in.shape[2]

    def full(s):
        return pl.BlockSpec(s, lambda f, p: (0, 0))

    wide = pl.BlockSpec((rows, fc), lambda f, p: (0, f))
    return pl.pallas_call(
        mid_kernel,
        out_shape=(
            jax.ShapeDtypeStruct((rows, ff), bf16),
            jax.ShapeDtypeStruct((rows, ff), bf16),
            jax.ShapeDtypeStruct((rows, D), bf16),
            jax.ShapeDtypeStruct((1, D), f32),
            jax.ShapeDtypeStruct((rows, 128), f32),
        ),
        grid_spec=pltpu.PrefetchScalarGridSpec(
            num_scalar_prefetch=1,
            grid=(ff // fc,),
            in_specs=[
                full((rows, D)),
                wide,
                pl.BlockSpec((1, D, fc), lambda f, p: (p[0], 0, f)),
                full((1, D)),
                full((1, 128)),
            ],
            out_specs=(wide, wide, full((rows, D)), full((1, D)), full((rows, 128))),
            scratch_shapes=[
                pltpu.VMEM((rows, D), f32),
                pltpu.VMEM((rows, 128), f32),
                pltpu.VMEM((rows, 128), f32),
            ],
        ),
        compiler_params=pltpu.CompilerParams(vmem_limit_bytes=VMEM),
        cost_estimate=pl.CostEstimate(
            flops=4 * rows * D * ff,
            bytes_accessed=2 * (3 * rows * D + ff * D + 3 * rows * ff),
            transcendentals=rows * ff,
        ),
        name="expert_mid",
    )(pick, x, u, w_in, wr, load)


def grads_kernel(
    pick_ref, x_ref, dy_ref, gate_ref, act_ref, gh_ref, keep_ref, send_ref, go, gi, gexp
):
    f = pl.program_id(0)

    @pl.when(f == 0)
    def _():
        gexp[...] = (dy_ref[...].astype(f32) * gate_ref[:, :1]).astype(bf16)

    go[...] = dg(act_ref[...], gexp[...], 0, 0).astype(bf16)
    gi[...] = dg(gh_ref[...], x_ref[...], 0, 0).astype(bf16)
    w = keep_ref.shape[3]
    me = pick_ref[1]
    for xx in range(keep_ref.shape[2]):
        a = pl.multiple_of((2 * xx + me) * w, w)
        b = pl.multiple_of((2 * xx + 1 - me) * w, w)
        keep_ref[0, 0, xx] = gi[pl.ds(a, w)]
        keep_ref[0, 1, xx] = go[pl.ds(a, w)]
        send_ref[0, 0, xx] = gi[pl.ds(b, w)]
        send_ref[0, 1, xx] = go[pl.ds(b, w)]


def expert_grads(pick, x, dy, gate, act, gh, dp, nx):
    rows = x.shape[0]
    ff = act.shape[1]
    fc = ff // dp
    w = fc // (2 * nx)

    def full(s):
        return pl.BlockSpec(s, lambda f, p: (0, 0))

    wide = pl.BlockSpec((rows, fc), lambda f, p: (0, f))
    part = jax.ShapeDtypeStruct((dp, 2, nx, w, D), bf16)
    part_spec = pl.BlockSpec((1, 2, nx, w, D), lambda f, p: (f, 0, 0, 0, 0))
    return pl.pallas_call(
        grads_kernel,
        out_shape=(part, part),
        grid_spec=pltpu.PrefetchScalarGridSpec(
            num_scalar_prefetch=1,
            grid=(dp,),
            in_specs=[full((rows, D)), full((rows, D)), full((rows, 128)), wide, wide],
            out_specs=(part_spec, part_spec),
            scratch_shapes=[
                pltpu.VMEM((fc, D), bf16),
                pltpu.VMEM((fc, D), bf16),
                pltpu.VMEM((rows, D), bf16),
            ],
        ),
        compiler_params=pltpu.CompilerParams(vmem_limit_bytes=VMEM),
        cost_estimate=pl.CostEstimate(
            flops=4 * rows * D * ff,
            bytes_accessed=2 * (2 * rows * D + 2 * ff * D + 2 * rows * ff),
            transcendentals=0,
        ),
        name="expert_grads",
    )(pick, x, dy, gate, act, gh)


def out_kernel(pick_ref, act_ref, wo_ref, out_ref, acc):
    f = pl.program_id(0)
    part = dg(act_ref[...], wo_ref[0], 1, 0)

    @pl.when(f == 0)
    def _():
        acc[...] = part

    @pl.when(f > 0)
    def _():
        acc[...] += part

    @pl.when(f == pl.num_programs(0) - 1)
    def _():
        out_ref[...] = acc[...].astype(bf16)


def expert_out(pick, act, w_out, fc=768):
    rows, ff = act.shape
    return pl.pallas_call(
        out_kernel,
        out_shape=jax.ShapeDtypeStruct((rows, D), bf16),
        grid_spec=pltpu.PrefetchScalarGridSpec(
            num_scalar_prefetch=1,
            grid=(ff // fc,),
            in_specs=[
                pl.BlockSpec((rows, fc), lambda f, p: (0, f)),
                pl.BlockSpec((1, fc, D), lambda f, p: (p[0], f, 0)),
            ],
            out_specs=pl.BlockSpec((rows, D), lambda f, p: (0, 0)),
            scratch_shapes=[pltpu.VMEM((rows, D), f32)],
        ),
        compiler_params=pltpu.CompilerParams(vmem_limit_bytes=VMEM),
        cost_estimate=pl.CostEstimate(
            flops=2 * rows * D * ff, bytes_accessed=2 * (rows * D + ff * D + rows * ff), transcendentals=0
        ),
        name="expert_out",
    )(pick, act, w_out)


def one_hot_slots(slot, slots):
    return (lax.broadcasted_iota(jnp.int32, (slots, slot.shape[1]), 0) == slot).astype(f32).astype(bf16)


def halves_of(v):
    high = v.astype(bf16)
    return jnp.concatenate([high, (v - high.astype(f32)).astype(bf16)], axis=0)


def sum_halves(v):
    v = v.astype(f32)
    n = v.shape[0] // 2
    return v[:n] + v[n:]


def branch_kernel(
    norm_row,
    me_ref,
    back_ref,
    slot_ref,
    dy_ref,
    middle_ref,
    gain_ref,
    w_ref,
    att_ref,
    early_ref,
    grad_ref,
    heads_ref,
    keep_ref,
    send_ref,
    small_ref,
    acc,
):
    g = dg(one_hot_slots(slot_ref[...], back_ref.shape[0]), back_ref[...], 0, 0)
    v = middle_ref[...]
    centred = v - jnp.mean(v, axis=1, keepdims=True)
    rstd = lax.rsqrt(jnp.mean(centred * centred, axis=1, keepdims=True) + norm_eps)
    xh = centred * rstd
    dn = g * gain_ref[...]
    grad = rstd * (dn - jnp.mean(dn, axis=1, keepdims=True) - xh * jnp.mean(dn * xh, axis=1, keepdims=True))
    grad = dy_ref[...].astype(f32) + grad
    grad_ref[...] = grad
    low = grad.astype(bf16)
    heads_ref[...] = dg(w_ref[...], low, 1, 1).astype(bf16).reshape(heads_ref.shape)
    row = lax.broadcasted_iota(jnp.int32, small_ref.shape, 0)
    small = early_ref[...] + jnp.where(row == norm_row, jnp.sum(g * xh, axis=0, keepdims=True), 0.0)
    small_ref[...] = small
    acc[...] = dg(att_ref[...], low, 1, 0)
    nx, w, _ = keep_ref.shape
    for x in range(nx):
        keep_ref[x] = acc[pl.ds(pl.multiple_of((2 * x + me_ref[0]) * w, w), w)]
        send_ref[x * w : (x + 1) * w] = acc[pl.ds(pl.multiple_of((2 * x + 1 - me_ref[0]) * w, w), w)].astype(bf16)
    send_ref[nx * w :] = halves_of(small)


def whole_block(shape):
    return pl.BlockSpec(shape, lambda i, p: (0,) * len(shape))


def one_step(kernel, name, outs, args, scratch, flops):
    return pl.pallas_call(
        kernel,
        out_shape=tuple(jax.ShapeDtypeStruct(shape, dtype) for shape, dtype in outs),
        grid_spec=pltpu.PrefetchScalarGridSpec(
            num_scalar_prefetch=1,
            grid=(1,),
            in_specs=[whole_block(a.shape) for a in args[1:]],
            out_specs=tuple(whole_block(shape) for shape, _ in outs),
            scratch_shapes=scratch,
        ),
        compiler_params=pltpu.CompilerParams(vmem_limit_bytes=VMEM),
        cost_estimate=pl.CostEstimate(
            flops=flops, bytes_accessed=4 * sum(a.size for a in args), transcendentals=0
        ),
        name=name,
    )(*args)


def branch_back(ci, back, slot, dy, middle, gain, w, attT, early, norm_row, ctx):
    rows = dy.shape[0]
    mine = D // ctx
    outs = (
        ((rows, D), f32),
        ((ctx, HEADS // ctx, HD, rows), bf16),
        ((ctx // 2, mine, D), f32),
        ((ctx // 2 * mine + 2 * early.shape[0], D), bf16),
        (early.shape, f32),
    )
    return one_step(
        functools.partial(branch_kernel, norm_row),
        "branch_back",
        outs,
        (ci, back, slot, dy, middle, gain, w, attT, early),
        [pltpu.VMEM((D, D), f32)],
        2 * rows * D * (back.shape[0] + 2 * D),
    )


def go_kernel(me_ref, keep_ref, got_ref, small_ref, own_ref, send_ref, sum_ref, acc):
    nx, w, _ = keep_ref.shape
    for x in range(nx):
        acc[x] = keep_ref[x] + got_ref[x * w : (x + 1) * w].astype(f32)
    small = small_ref[...] + sum_halves(got_ref[nx * w :])
    sum_ref[...] = small
    own_ref[...] = acc[me_ref[0]]
    send_ref[:w] = acc[1 - me_ref[0]].astype(bf16)
    send_ref[w:] = halves_of(small)


def go_step(xi, keep, got, small):
    w = keep.shape[1]
    outs = (((w, D), f32), ((w + 2 * small.shape[0], D), bf16), (small.shape, f32))
    return one_step(go_kernel, "go_step", outs, (xi, keep, got, small), [pltpu.VMEM(keep.shape, f32)], 0)


def weight_rows_kernel(half_ref, dT_ref, normed_ref, go_ref, got_ref, early_ref, keep_ref, send_ref, small_ref, acc):
    n = dT_ref.shape[0]
    w = go_ref.shape[0]
    half = keep_ref.shape[0]
    acc[:n] = dg(dT_ref[...], normed_ref[...], 1, 0)
    acc[n:] = go_ref[...] + got_ref[:w].astype(f32)
    small = early_ref[...] + sum_halves(got_ref[w:])
    small_ref[...] = small
    a = pl.multiple_of(half_ref[0] * half, half)
    b = pl.multiple_of((1 - half_ref[0]) * half, half)
    keep_ref[...] = acc[pl.ds(a, half)]
    send_ref[:half] = acc[pl.ds(b, half)].astype(bf16)
    send_ref[half:] = halves_of(small)


def weight_rows(half, dT, normed, go, got, small):
    rows = dT.shape[0] + go.shape[0]
    outs = (((rows // 2, D), f32), ((rows // 2 + 2 * small.shape[0], D), bf16), (small.shape, f32))
    return one_step(
        weight_rows_kernel,
        "weight_rows",
        outs,
        (half, dT, normed, go, got, small),
        [pltpu.VMEM((rows, D), f32)],
        2 * dT.size * D,
    )


def share_kernel(me_ref, half_ref, got_ref, early_ref, own_ref, *refs):
    dp = len(refs) - 1
    sends, small_ref, acc = refs[: dp - 1], refs[dp - 1], refs[dp]
    half = half_ref.shape[0]
    w = half // dp
    acc[...] = half_ref[...] + got_ref[:half].astype(f32)
    small = early_ref[...] + sum_halves(got_ref[half:])
    small_ref[...] = small

    def share(step):
        return acc[pl.ds(pl.multiple_of(lax.rem(me_ref[0] + step, dp) * w, w), w)]

    own_ref[...] = share(0)
    for step in range(1, dp):
        sends[step - 1][:w] = share(step).astype(bf16)
        sends[step - 1][w:] = halves_of(small)


def share_step(zi, half, got, small, dp):
    w = half.shape[0] // dp
    outs = (((w, D), f32),) + (((w + 2 * small.shape[0], D), bf16),) * (dp - 1) + ((small.shape, f32),)
    return one_step(
        functools.partial(share_kernel),
        "share_step",
        outs,
        (zi, half, got, small),
        [pltpu.VMEM(half.shape, f32)],
        0,
    )


def finish_kernel(dp, me_ref, *refs):
    pieces = refs[:8]
    weights = refs[8:11]
    outs = refs[11:15]
    gain_ref = refs[15]
    got, wide, in_sem, out_sem = refs[16:]
    z, xi, ci, yi = me_ref[0], me_ref[1], me_ref[2], me_ref[3]
    rows = pieces[0].shape[0] // dp
    per = 4 * 2 // dp
    copies = []
    for n in range(8):
        c, x, y = (n // 4) ^ ci, ((n // 2) % 2) ^ xi, (n % 2) ^ yi
        for r in range(dp):
            j = y * dp + lax.rem(z + dp - r, dp)
            p = lax.div(j * 4, 2 * dp)
            first = (x * 2 + c) * (D // 4) + lax.rem(j, 2 * dp // 4) * rows
            copy = pltpu.make_async_copy(
                pieces[n].at[pl.ds(r * rows, rows)],
                got.at[p, pl.ds(pl.multiple_of(first, rows), rows)],
                in_sem.at[n, r],
            )
            copy.start()
            copies.append(copy)
    for copy in copies:
        copy.wait()
    del per
    gain = jnp.zeros((D, 1), f32)
    backs = []
    for p in range(4):
        if p < 3:
            g = got[p].T.astype(f32)
            gain = gain + jnp.sum(g * weights[p][...].astype(f32), axis=1, keepdims=True)
        else:
            g = got[p].astype(f32)
        wide[p] = g
        back = pltpu.make_async_copy(wide.at[p], outs[p], out_sem.at[p])
        back.start()
        backs.append(back)
    gain_ref[...] = gain
    for back in backs:
        back.wait()


def finish(me, pieces, weights, dp):
    whole = jax.ShapeDtypeStruct((D, D), f32)
    anywhere = pl.BlockSpec(memory_space=pl.ANY)
    return pl.pallas_call(
        functools.partial(finish_kernel, dp),
        out_shape=(whole,) * 4 + (jax.ShapeDtypeStruct((D, 1), f32),),
        grid_spec=pltpu.PrefetchScalarGridSpec(
            num_scalar_prefetch=1,
            grid=(1,),
            in_specs=[anywhere] * 8 + [pl.BlockSpec((D, D), lambda i, p: (0, 0))] * 3,
            out_specs=(anywhere,) * 4 + (pl.BlockSpec((D, 1), lambda i, p: (0, 0)),),
            scratch_shapes=[
                pltpu.VMEM((4, D, D), bf16),
                pltpu.VMEM((4, D, D), f32),
                pltpu.SemaphoreType.DMA((8, dp)),
                pltpu.SemaphoreType.DMA((4,)),
            ],
        ),
        compiler_params=pltpu.CompilerParams(vmem_limit_bytes=VMEM),
        cost_estimate=pl.CostEstimate(flops=8 * D * D, bytes_accessed=32 * D * D, transcendentals=0),
        name="finish",
    )(me, *pieces, *weights)


def swap(v, axis):
    return lax.ppermute(v, axis, [(0, 1), (1, 0)])


def shift(v, axis, step):
    n = lax.axis_size(axis)
    return lax.ppermute(v, axis, [(i, (i + step) % n) for i in range(n)])


def at(v, index):
    return lax.dynamic_index_in_dim(v, index, 0, keepdims=False)


def one(v):
    v = v.astype(f32)
    n = v.shape[0] // 2
    return v[:n] + v[n:]


def add_pair(v):
    return v + (swap(v, "expert") if lax.axis_size("expert") == 2 else lax.psum(v, "expert") - v)


def add_shifts(v):
    out = v
    for s in range(1, lax.axis_size("dp")):
        out = out + shift(v, "dp", s)
    return out


def index(i):
    return i.astype(jnp.int32).reshape(1)


def tie(*arrays):
    return lax.optimization_barrier(arrays)


def normal_form(v):
    centred = v - jnp.mean(v, axis=-1, keepdims=True)
    rstd = lax.rsqrt(jnp.mean(centred * centred, axis=-1, keepdims=True) + norm_eps)
    return centred * rstd, rstd


def norm_back(dn, xh, rstd):
    return rstd * (dn - jnp.mean(dn, axis=-1, keepdims=True) - xh * jnp.mean(dn * xh, axis=-1, keepdims=True))


def per_device(
    tokens,
    cotangent,
    routes,
    norm1_gain,
    w_query,
    w_key,
    w_value,
    w_output,
    norm2_gain,
    w_router,
    w_in,
    w_out,
):
    rows = tokens.shape[1]
    nx, owners, dp = lax.axis_size("x"), lax.axis_size("expert"), lax.axis_size("dp")
    xi, ci, ei = lax.axis_index("x"), lax.axis_index("core"), lax.axis_index("expert")
    ctx = 2 * nx
    ctx_i = xi * 2 + ci
    length = ctx * rows
    experts = w_router.shape[1]
    cap = 2 * rows // experts
    mine = D // ctx
    heads = mine // HD
    pick = jnp.stack([xi, ci]).astype(jnp.int32)

    tok = tokens.reshape(rows, D)
    flat = tok.astype(f32)
    other = swap(tok, "x")
    near = swap(tok, "core")

    route = routes.reshape(rows)
    hot = (route[:, None] == jnp.arange(experts, dtype=jnp.int32)[None, :]).astype(f32)
    lower = jnp.arange(rows)[:, None] >= jnp.arange(rows)[None, :]
    before = dg(lower.astype(bf16), hot.astype(bf16), 1, 0)
    rank = (jnp.sum(before * hot, axis=1) - 1.0).astype(jnp.int32)
    slot = ((route % nx) * owners + route // nx) * cap + rank
    spread = (jnp.arange(experts * cap, dtype=jnp.int32)[:, None] == slot[None, :]).astype(bf16)

    def pack(v):
        return dg(spread, v, 1, 0).astype(bf16).reshape(nx * owners, cap, D)

    def trade(v):
        v = lax.all_to_all(v.reshape(nx * owners, cap, D), ("x", "expert"), split_axis=0, concat_axis=0, tiled=True)
        return v.reshape(-1, D)

    def turn(v):
        return lax.all_to_all(v, ("x", "core"), split_axis=0, concat_axis=0, tiled=True)

    def cut(w):
        return lax.dynamic_slice(w, (0, ctx_i * mine), (D, mine))

    w_own = jnp.concatenate([cut(w_query), cut(w_key), cut(w_value)], axis=1)
    gain1 = norm1_gain.reshape(1, D)
    dy_low = cotangent.reshape(rows, D)
    dy = dy_low.astype(f32)
    expert_id = ei * nx + xi
    wr = lax.dynamic_slice(w_router, (0, expert_id), (D, 1)).astype(f32).reshape(1, D)
    counts = jnp.sum(hot, axis=0)
    counts = counts + swap(counts, "core")
    counts = add_pair(counts)
    so_far = project(ctx_i, tok, gain1, w_own, ctx, None)
    counts, dy_packed, *so_far = tie(counts, pack(dy_low), *so_far)
    so_far = project(ctx_i ^ 1, near, gain1, w_own, ctx, so_far)
    other, dy_packed, *so_far = tie(other, dy_packed, *so_far)
    far = swap(other, "core")
    dy_rows = trade(dy_packed)
    so_far = project(ctx_i ^ 2, other, gain1, w_own, ctx, so_far)
    normed_all, qkvT, kv = project(ctx_i ^ 3, far, gain1, w_own, ctx, so_far)
    oT, osend, lse = attend(qkvT, kv, ctx)
    osend, dy_rows, counts = tie(osend, dy_rows, counts)
    attT = turn(osend)
    counts = add_shifts(counts)
    attT, counts = tie(attT, counts)
    counts = counts + swap(counts, "x")
    attT = attT.reshape(D, rows)
    mean_load = rows * ctx * dp * owners / experts
    load_term = balance_weight * (counts - mean_load) / (mean_load * mean_load)
    load = jnp.broadcast_to(lax.dynamic_slice(load_term, (expert_id,), (1,)).reshape(1, 1), (1, 128))

    middle = flat + dg(attT, w_output, 0, 0)
    xh2, rstd2 = normal_form(middle)
    second = (xh2 * norm2_gain).astype(bf16)
    gating = jax.nn.sigmoid(jnp.sum(hot * dg(second, w_router, 1, 0), axis=1))

    up = expert_up(pick, dy_rows, w_out)
    sig = jnp.pad(jnp.sum(hot * gating[:, None], axis=0), (0, D - experts))
    x_rows = trade(pack(second))
    x_rows, gating, sig, slot, gain2 = tie(x_rows, gating, sig, slot[None], norm2_gain.reshape(1, D))
    active, grad_hidden, back_rows, router_row, gate = expert_mid(pick, x_rows, up, w_in, wr, load)
    returned = trade(back_rows)
    keep, send = expert_grads(pick, x_rows, dy_rows, gate, active, grad_hidden, dp, nx)
    produced = expert_out(pick, tie(active, keep)[0], w_out)
    returned, keep, send, produced = tie(returned, keep, send, produced)
    taken = swap(send, "core")
    zi = lax.axis_index("dp")

    def chunk(i):
        return at(keep, (i + dp) % dp).astype(f32) + at(taken, (i + dp) % dp).astype(f32)

    def ring(moving, step):
        moving = shift(moving, "dp", 1).astype(f32) + chunk(zi - 2 - step)
        return moving if step == dp - 2 else moving.astype(bf16)

    router_rows = (jnp.arange(experts) == expert_id).astype(f32)[:, None] * router_row
    small = jnp.concatenate([router_rows, jnp.zeros((1, D), f32), sig[None]], axis=0)
    small = jnp.pad(small, ((0, -small.shape[0] % 8), (0, 0)))
    grad_middle, heads_grad, go, go_send, small = branch_back(
        index(ci), returned, slot, dy_low, middle, gain2, w_output, attT, small, experts, ctx
    )
    do = turn(heads_grad)

    moving = ring(chunk(zi - 1).astype(bf16), 0)
    go_got = swap(go_send, "core")
    go, go_send, small = go_step(index(xi), go, go_got, small)
    do, go_send = tie(do, go_send)
    go_got = swap(go_send, "x")

    so_far = attend_back(qkvT, kv, do, 0, oT, lse, 0, None)
    produced, *so_far = tie(produced, *so_far)
    went_back = trade(produced)
    so_far = attend_back(qkvT, kv, do, 1, oT, lse, 1, so_far)
    moving, *so_far = tie(moving, *so_far)
    moving = ring(moving, 1)
    for h in range(2, heads):
        so_far = attend_back(qkvT, kv, do, h, oT, lse, h, so_far)
    go_got, *so_far = tie(go_got, *so_far)
    went_back, dT, dsend = tie(went_back, *so_far)
    output = (middle + gating[:, None] * dg(spread, went_back, 0, 0)).astype(bf16)
    got = turn(dsend)

    ei2 = ei if owners == 2 else jnp.zeros_like(ei)
    half, send, small = weight_rows(index(ei2), dT.reshape(3 * mine, length), normed_all, go, go_got, small)
    if owners == 2:
        gift = swap(send, "expert")
        gift, moving = tie(gift, moving)
        halves = [(half, gift)]
    else:
        cut_at = half.shape[0]
        small = lax.psum(small, "expert")
        nothing = jnp.zeros_like(send)
        halves = [(lax.psum(half, "expert"), nothing), (lax.psum(send[:cut_at].astype(f32), "expert"), nothing)]
    pieces = []
    for part, gift in halves:
        share, *gifts, more = share_step(index(zi), part, gift, small, dp)
        gifts = [shift(gift, "dp", step + 1) for step, gift in enumerate(gifts)]
        for gift in gifts:
            more = more + one(gift[share.shape[0] :])
            share = share + gift[: share.shape[0]].astype(f32)
        share = share.astype(bf16)
        pieces.append(jnp.concatenate([share] + [shift(share, "dp", step) for step in range(1, dp)], axis=0))
    small = more
    moving, *pieces = tie(moving, *pieces)
    for step in range(2, dp - 1):
        moving = ring(moving, step)

    if owners == 2:
        pieces.append(swap(pieces[0], "expert"))
    pieces += [swap(piece, "x") for piece in pieces]
    pieces += [swap(piece, "core") for piece in pieces]
    me = jnp.stack([zi, xi, ci, ei2]).astype(jnp.int32)
    *grads, grad_norm1 = finish(me, pieces, (w_query, w_key, w_value), dp)
    grad_norm1 = grad_norm1.reshape(D) / norm1_gain

    grad_normed = 0.0
    for p, w in enumerate((w_query, w_key, w_value)):
        grad_normed = grad_normed + dg(got[:, p].reshape(D, rows), w, 0, 1)
    xh1, rstd1 = normal_form(flat)
    grad_tokens = grad_middle + norm_back(grad_normed * norm1_gain, xh1, rstd1)

    own = lax.dynamic_index_in_dim(moving, xi, 1, keepdims=False)
    moved = swap(lax.dynamic_index_in_dim(moving, 1 - xi, 1, keepdims=False).astype(bf16), "x").astype(f32)
    first, latter = jnp.where(xi == 0, own, moved), jnp.where(xi == 0, moved, own)
    both = jnp.stack([first, latter], axis=1)
    grad_in = jnp.swapaxes(both[0], 1, 2)
    grad_out = both[1]

    grad_router = jnp.transpose(small[:experts])
    grad_norm2 = small[experts]
    total_sig = small[experts + 1, :experts]
    balance = balance_weight * jnp.sum((counts - mean_load) / mean_load * total_sig) / mean_load

    return (
        output.reshape(1, rows, D),
        grad_tokens.reshape(1, rows, D),
        grad_norm1,
        grads[0],
        grads[1],
        grads[2],
        grads[3],
        grad_norm2,
        grad_router,
        grad_in,
        grad_out,
        balance,
    )


def solution(mesh):
    dp, ctx, owners = mesh.shape["dp"], mesh.shape["ctx"], mesh.shape["expert"]
    split = Mesh(mesh.devices.reshape(dp, ctx // 2, 2, owners), ("dp", "x", "core", "expert"))
    token = P(("dp", "expert"), ("x", "core"), None)
    return jax.shard_map(
        per_device,
        mesh=split,
        in_specs=(token, token, token, P(), P(), P(), P(), P(), P(), P(), P("expert"), P("expert")),
        out_specs=(
            token,
            token,
            P(),
            P(),
            P(),
            P(),
            P(),
            P(),
            P(),
            P("expert", None, ("dp", "x", "core")),
            P("expert", ("dp", "x", "core"), None),
            P(),
        ),
        check_vma=False,
    )
```

```python
import functools

import jax
import jax.numpy as jnp
from jax import lax
from jax.experimental import pallas as pl
from jax.experimental.pallas import tpu as pltpu
from jax.sharding import Mesh
from jax.sharding import PartitionSpec as P

D = 768
HEADS = 12
HD = 64
norm_eps = 1e-05
balance_weight = 1.0
LOG2E = 1.4426950408889634
MASKED = -1e30
GELU_A = 0.7978845608028654
GELU_B = 0.044715
VMEM = 56 * 1024 * 1024
f32 = jnp.float32
bf16 = jnp.bfloat16


def dg(a, b, ca, cb):
    return lax.dot_general(a, b, (((ca,), (cb,)), ((), ())), preferred_element_type=f32)


def project_kernel(place_ref, tok_ref, gain_ref, w_ref, *refs):
    normed_ref, qkvT_ref, kv_ref = refs[-3:]
    x = tok_ref[...].astype(f32)
    centred = x - jnp.mean(x, axis=1, keepdims=True)
    rstd = lax.rsqrt(jnp.mean(centred * centred, axis=1, keepdims=True) + norm_eps)
    normed = (centred * rstd * gain_ref[...]).astype(bf16)
    normed_ref[...] = normed
    qkv = dg(normed, w_ref[...], 1, 0).astype(bf16)
    kv_ref[...] = qkv[:, qkv.shape[1] - kv_ref.shape[1] :]
    qkvT_ref[...] = qkv.T


def project(place, tok, gain, w, ctx, so_far):
    rows = tok.shape[0]
    wide = w.shape[1]
    args = [tok, gain, w]
    specs = [pl.BlockSpec(a.shape, lambda i, p: (0, 0)) for a in args]
    alias = {}
    if so_far is not None:
        alias = {4: 0, 5: 1, 6: 2}
        args += list(so_far)
        specs += [pl.BlockSpec(memory_space=pl.ANY)] * 3
    return pl.pallas_call(
        project_kernel,
        out_shape=(
            jax.ShapeDtypeStruct((ctx * rows, D), bf16),
            jax.ShapeDtypeStruct((wide, ctx * rows), bf16),
            jax.ShapeDtypeStruct((ctx * rows, 2 * wide // 3), bf16),
        ),
        grid_spec=pltpu.PrefetchScalarGridSpec(
            num_scalar_prefetch=1,
            grid=(1,),
            in_specs=specs,
            out_specs=(
                pl.BlockSpec((rows, D), lambda i, p: (p[0], 0)),
                pl.BlockSpec((wide, rows), lambda i, p: (0, p[0])),
                pl.BlockSpec((rows, 2 * wide // 3), lambda i, p: (p[0], 0)),
            ),
        ),
        input_output_aliases=alias,
        compiler_params=pltpu.CompilerParams(vmem_limit_bytes=VMEM),
        cost_estimate=pl.CostEstimate(
            flops=4 * rows * D * wide, bytes_accessed=4 * rows * D + 8 * rows * wide, transcendentals=0
        ),
        name="project",
    )(place.astype(jnp.int32).reshape(1), *args)


def attend_kernel(heads, blk, qT_ref, k_ref, vT_ref, oT_ref, osend_ref, lse_ref):
    length = qT_ref.shape[1]
    per = osend_ref.shape[3]
    c = (HD**-0.5) * LOG2E
    rows = lax.broadcasted_iota(jnp.int32, (blk, blk), 0)
    cols = lax.broadcasted_iota(jnp.int32, (blk, blk), 1)
    keep = rows <= cols
    for h in range(heads):
        hs = slice(h * HD, (h + 1) * HD)
        for i in range(length // blk):
            a, b = i * blk, (i + 1) * blk
            q = qT_ref[hs, a:b]
            sd = dg(k_ref[a:b, hs], q, 1, 0)
            sd = jnp.where(keep, sd, MASKED)
            m = jnp.max(sd, axis=0, keepdims=True)
            if i:
                s = dg(k_ref[:a, hs], q, 1, 0)
                m = jnp.maximum(m, jnp.max(s, axis=0, keepdims=True))
            mc = m * c
            pd = jnp.exp2(sd * c - mc)
            total = jnp.sum(pd, axis=0, keepdims=True)
            o = dg(vT_ref[hs, a:b], pd.astype(bf16), 1, 0)
            if i:
                p = jnp.exp2(s * c - mc)
                total = total + jnp.sum(p, axis=0, keepdims=True)
                o = o + dg(vT_ref[hs, :a], p.astype(bf16), 1, 0)
            o = o / total
            oT_ref[hs, a:b] = o
            d, off = a // per, a % per
            osend_ref[d, h, :, off : off + blk] = o.astype(bf16)
            lse_ref[h, :, a:b] = mc + jnp.log2(total)


def attend(qkvT, kv, dests):
    length = kv.shape[0]
    heads = qkvT.shape[0] // (3 * HD)
    wide = heads * HD
    per = length // dests
    return pl.pallas_call(
        functools.partial(attend_kernel, heads, per),
        out_shape=(
            jax.ShapeDtypeStruct((wide, length), f32),
            jax.ShapeDtypeStruct((dests, heads, HD, per), bf16),
            jax.ShapeDtypeStruct((heads, 1, length), f32),
        ),
        grid=(1,),
        in_specs=[
            pl.BlockSpec((wide, length), lambda i: (0, 0)),
            pl.BlockSpec(kv.shape, lambda i: (0, 0)),
            pl.BlockSpec((wide, length), lambda i: (2, 0)),
        ],
        out_specs=(
            pl.BlockSpec((wide, length), lambda i: (0, 0)),
            pl.BlockSpec((dests, heads, HD, per), lambda i: (0, 0, 0, 0)),
            pl.BlockSpec((heads, 1, length), lambda i: (0, 0, 0)),
        ),
        compiler_params=pltpu.CompilerParams(vmem_limit_bytes=VMEM),
        cost_estimate=pl.CostEstimate(
            flops=8 * heads * length * length * HD,
            bytes_accessed=length * wide * 14,
            transcendentals=heads * length * length // 2,
        ),
        name="attend",
    )(qkvT, kv, qkvT)


def attend_back_kernel(lk, lv, blk, *refs):
    qT_ref, k_ref, kT_ref, v_ref, do_ref, oT_ref, lse_ref = refs[:7]
    dT_ref, dsend_ref, dk_acc, dv_acc = refs[-4:]
    length = qT_ref.shape[1]
    per = do_ref.shape[3]
    sc = HD**-0.5
    c = sc * LOG2E
    rows = lax.broadcasted_iota(jnp.int32, (blk, blk), 0)
    cols = lax.broadcasted_iota(jnp.int32, (blk, blk), 1)
    keep = rows <= cols
    n = length // blk
    for i in reversed(range(n)):
        x0, x1 = i * blk, (i + 1) * blk
        d, off = x0 // per, x0 % per
        q = qT_ref[:, x0:x1]
        do = do_ref[d, 0, :, off : off + blk]
        lse = lse_ref[0, :, x0:x1]
        delta = jnp.sum(do.astype(f32) * oT_ref[:, x0:x1], axis=0, keepdims=True)
        dq = None
        for a, b, diag in ([(0, x0, False)] if i else []) + [(x0, x1, True)]:
            s = dg(k_ref[a:b, lk : lk + HD], q, 1, 0)
            p = jnp.exp2(s * c - lse)
            if diag:
                p = jnp.where(keep, p, 0.0)
            dp = dg(v_ref[a:b, lv : lv + HD], do, 1, 0)
            ds = (p * (dp - delta)).astype(bf16)
            dvn = dg(do, p.astype(bf16), 1, 1)
            dkn = dg(q, ds, 1, 1)
            if i == n - 1:
                dv_acc[:, a:b] = dvn
                dk_acc[:, a:b] = dkn
            else:
                dv_acc[:, a:b] += dvn
                dk_acc[:, a:b] += dkn
            t = dg(kT_ref[:, a:b], ds, 1, 0)
            dq = t if dq is None else dq + t
        dq = (dq * sc).astype(bf16)
        dT_ref[0, :, x0:x1] = dq
        dsend_ref[d, 0, :, off : off + blk] = dq
    for d in range(dsend_ref.shape[0]):
        at_d = slice(d * per, (d + 1) * per)
        dk = (dk_acc[:, at_d] * sc).astype(bf16)
        dv = dv_acc[:, at_d].astype(bf16)
        dT_ref[1, :, at_d] = dk
        dT_ref[2, :, at_d] = dv
        dsend_ref[d, 1] = dk
        dsend_ref[d, 2] = dv


def attend_back(qkvT, kv, do, slot, oT, lse, h, so_far):
    length = kv.shape[0]
    n = qkvT.shape[0] // (3 * HD)
    dests, _, _, per = do.shape
    hv = n + h
    blk = min(256, per)
    args = [qkvT, kv, qkvT, kv, do, oT, lse]
    specs = [
        pl.BlockSpec((HD, length), lambda i: (h, 0)),
        pl.BlockSpec((length, 2 * HD), lambda i: (0, h // 2)),
        pl.BlockSpec((HD, length), lambda i: (n + h, 0)),
        pl.BlockSpec((length, 2 * HD), lambda i: (0, hv // 2)),
        pl.BlockSpec((dests, 1, HD, per), lambda i: (0, slot, 0, 0)),
        pl.BlockSpec((HD, length), lambda i: (h, 0)),
        pl.BlockSpec((1, 1, length), lambda i: (h, 0, 0)),
    ]
    alias = {}
    if so_far is not None:
        alias = {len(args): 0, len(args) + 1: 1}
        args += list(so_far)
        specs += [pl.BlockSpec(memory_space=pl.ANY)] * 2
    return pl.pallas_call(
        functools.partial(attend_back_kernel, (h % 2) * HD, (hv % 2) * HD, blk),
        out_shape=(
            jax.ShapeDtypeStruct((3, n * HD, length), bf16),
            jax.ShapeDtypeStruct((dests, 3, n * HD, per), bf16),
        ),
        grid=(1,),
        in_specs=specs,
        out_specs=(
            pl.BlockSpec((3, HD, length), lambda i: (0, h, 0)),
            pl.BlockSpec((dests, 3, HD, per), lambda i: (0, 0, h, 0)),
        ),
        scratch_shapes=[pltpu.VMEM((HD, length), f32)] * 2,
        input_output_aliases=alias,
        compiler_params=pltpu.CompilerParams(vmem_limit_bytes=VMEM),
        cost_estimate=pl.CostEstimate(
            flops=20 * length * length * HD, bytes_accessed=length * HD * 24, transcendentals=length * length // 2
        ),
        name=f"attend_back_head{h}",
    )(*args)


def up_kernel(pick_ref, dy_ref, wo_ref, u_ref):
    u_ref[...] = dg(dy_ref[...], wo_ref[0], 1, 1).astype(bf16)


def expert_up(pick, dy, w_out, fc=768):
    rows = dy.shape[0]
    ff = w_out.shape[1]
    return pl.pallas_call(
        up_kernel,
        out_shape=jax.ShapeDtypeStruct((rows, ff), bf16),
        grid_spec=pltpu.PrefetchScalarGridSpec(
            num_scalar_prefetch=1,
            grid=(ff // fc,),
            in_specs=[
                pl.BlockSpec((rows, D), lambda f, p: (0, 0)),
                pl.BlockSpec((1, fc, D), lambda f, p: (p[0], f, 0)),
            ],
            out_specs=pl.BlockSpec((rows, fc), lambda f, p: (0, f)),
        ),
        compiler_params=pltpu.CompilerParams(vmem_limit_bytes=VMEM),
        cost_estimate=pl.CostEstimate(
            flops=2 * rows * D * ff, bytes_accessed=2 * (rows * D + ff * D + rows * ff), transcendentals=0
        ),
        name="expert_up",
    )(pick, dy, w_out)


def mid_kernel(
    mean, pick_ref, x_ref, u_ref, wi_ref, wr_ref, count_ref, act_ref, gh_ref, rows_ref, router_ref, gate_ref, acc, gg, gate
):
    f = pl.program_id(0)
    n = pl.num_programs(0)

    @pl.when(f == 0)
    def _():
        logit = jnp.sum(x_ref[...].astype(f32) * wr_ref[...], axis=1, keepdims=True)
        gate[...] = jnp.broadcast_to(jax.nn.sigmoid(logit), gate.shape)
        acc[...] = jnp.zeros_like(acc)
        gg[...] = jnp.zeros_like(gg)

    step = 256
    for r in range(0, x_ref.shape[0], step):
        rs = slice(r, r + step)
        for c in range(0, wi_ref.shape[2], step):
            cs = slice(c, c + step)
            h = dg(x_ref[rs], wi_ref[0, :, cs], 1, 0)
            h2 = h * h
            t = jnp.tanh(h * (GELU_A + (GELU_A * GELU_B) * h2))
            hp = 0.5 + 0.5 * t
            dgelu = hp + (h * (hp - hp * hp)) * (2.0 * GELU_A + (6.0 * GELU_A * GELU_B) * h2)
            u = u_ref[rs, cs].astype(f32)
            active = h * hp
            act_ref[rs, cs] = active.astype(bf16)
            au = active * u
            lanes = au[:, :128]
            for j in range(128, step, 128):
                lanes = lanes + au[:, j : j + 128]
            gg[rs] += lanes
            gh = (gate[rs, :1] * (u * dgelu)).astype(bf16)
            gh_ref[rs, cs] = gh
            acc[rs] += dg(gh, wi_ref[0, :, cs], 1, 1)

    @pl.when(f == n - 1)
    def _():
        g = gate[:, :1]
        got = jnp.sum(gg[...], axis=1, keepdims=True)
        lane = lax.broadcasted_iota(jnp.int32, count_ref.shape, 1)
        count = jnp.sum(jnp.where(lane == pick_ref[2], count_ref[...], 0.0), axis=1, keepdims=True)
        load = balance_weight * (count - mean) / (mean * mean)
        sel = (g * (1.0 - g) * (got + load)).astype(bf16).astype(f32)
        rows_ref[...] = (acc[...] + sel * wr_ref[...]).astype(bf16)
        router_ref[...] = jnp.sum(x_ref[...].astype(f32) * sel, axis=0, keepdims=True)
        gate_ref[...] = gate[...]


def expert_mid(pick, x, u, w_in, wr, counts, mean, fc=768):
    rows = x.shape[0]
    ff = w_in.shape[2]

    def full(s):
        return pl.BlockSpec(s, lambda f, p: (0, 0))

    wide = pl.BlockSpec((rows, fc), lambda f, p: (0, f))
    return pl.pallas_call(
        functools.partial(mid_kernel, mean),
        out_shape=(
            jax.ShapeDtypeStruct((rows, ff), bf16),
            jax.ShapeDtypeStruct((rows, ff), bf16),
            jax.ShapeDtypeStruct((rows, D), bf16),
            jax.ShapeDtypeStruct((1, D), f32),
            jax.ShapeDtypeStruct((rows, 128), f32),
        ),
        grid_spec=pltpu.PrefetchScalarGridSpec(
            num_scalar_prefetch=1,
            grid=(ff // fc,),
            in_specs=[
                full((rows, D)),
                wide,
                pl.BlockSpec((1, D, fc), lambda f, p: (p[0], 0, f)),
                full((1, D)),
                full((1, 128)),
            ],
            out_specs=(wide, wide, full((rows, D)), full((1, D)), full((rows, 128))),
            scratch_shapes=[
                pltpu.VMEM((rows, D), f32),
                pltpu.VMEM((rows, 128), f32),
                pltpu.VMEM((rows, 128), f32),
            ],
        ),
        compiler_params=pltpu.CompilerParams(vmem_limit_bytes=VMEM),
        cost_estimate=pl.CostEstimate(
            flops=4 * rows * D * ff,
            bytes_accessed=2 * (3 * rows * D + ff * D + 3 * rows * ff),
            transcendentals=rows * ff,
        ),
        name="expert_mid",
    )(pick, x, u, w_in, wr, counts)


def grads_kernel(
    pick_ref, x_ref, dy_ref, gate_ref, act_ref, gh_ref, keep_ref, send_ref, go, gi, gexp
):
    f = pl.program_id(0)

    @pl.when(f == 0)
    def _():
        gexp[...] = (dy_ref[...].astype(f32) * gate_ref[:, :1]).astype(bf16)

    go[...] = dg(act_ref[...], gexp[...], 0, 0).astype(bf16)
    gi[...] = dg(gh_ref[...], x_ref[...], 0, 0).astype(bf16)
    w = keep_ref.shape[3]
    me = pick_ref[1]
    for xx in range(keep_ref.shape[2]):
        a = pl.multiple_of((2 * xx + me) * w, w)
        b = pl.multiple_of((2 * xx + 1 - me) * w, w)
        keep_ref[0, 0, xx] = gi[pl.ds(a, w)]
        keep_ref[0, 1, xx] = go[pl.ds(a, w)]
        send_ref[0, 0, xx] = gi[pl.ds(b, w)]
        send_ref[0, 1, xx] = go[pl.ds(b, w)]


def expert_grads(pick, x, dy, gate, act, gh, dp, nx):
    rows = x.shape[0]
    ff = act.shape[1]
    fc = ff // dp
    w = fc // (2 * nx)

    def full(s):
        return pl.BlockSpec(s, lambda f, p: (0, 0))

    wide = pl.BlockSpec((rows, fc), lambda f, p: (0, f))
    part = jax.ShapeDtypeStruct((dp, 2, nx, w, D), bf16)
    part_spec = pl.BlockSpec((1, 2, nx, w, D), lambda f, p: (f, 0, 0, 0, 0))
    return pl.pallas_call(
        grads_kernel,
        out_shape=(part, part),
        grid_spec=pltpu.PrefetchScalarGridSpec(
            num_scalar_prefetch=1,
            grid=(dp,),
            in_specs=[full((rows, D)), full((rows, D)), full((rows, 128)), wide, wide],
            out_specs=(part_spec, part_spec),
            scratch_shapes=[
                pltpu.VMEM((fc, D), bf16),
                pltpu.VMEM((fc, D), bf16),
                pltpu.VMEM((rows, D), bf16),
            ],
        ),
        compiler_params=pltpu.CompilerParams(vmem_limit_bytes=VMEM),
        cost_estimate=pl.CostEstimate(
            flops=4 * rows * D * ff,
            bytes_accessed=2 * (2 * rows * D + 2 * ff * D + 2 * rows * ff),
            transcendentals=0,
        ),
        name="expert_grads",
    )(pick, x, dy, gate, act, gh)


def out_kernel(pick_ref, act_ref, wo_ref, out_ref, acc):
    f = pl.program_id(0)
    part = dg(act_ref[...], wo_ref[0], 1, 0)

    @pl.when(f == 0)
    def _():
        acc[...] = part

    @pl.when(f > 0)
    def _():
        acc[...] += part

    @pl.when(f == pl.num_programs(0) - 1)
    def _():
        out_ref[...] = acc[...].astype(bf16)


def expert_out(pick, act, w_out, fc=768):
    rows, ff = act.shape
    return pl.pallas_call(
        out_kernel,
        out_shape=jax.ShapeDtypeStruct((rows, D), bf16),
        grid_spec=pltpu.PrefetchScalarGridSpec(
            num_scalar_prefetch=1,
            grid=(ff // fc,),
            in_specs=[
                pl.BlockSpec((rows, fc), lambda f, p: (0, f)),
                pl.BlockSpec((1, fc, D), lambda f, p: (p[0], f, 0)),
            ],
            out_specs=pl.BlockSpec((rows, D), lambda f, p: (0, 0)),
            scratch_shapes=[pltpu.VMEM((rows, D), f32)],
        ),
        compiler_params=pltpu.CompilerParams(vmem_limit_bytes=VMEM),
        cost_estimate=pl.CostEstimate(
            flops=2 * rows * D * ff, bytes_accessed=2 * (rows * D + ff * D + rows * ff), transcendentals=0
        ),
        name="expert_out",
    )(pick, act, w_out)


def one_hot_slots(slot, slots):
    return (lax.broadcasted_iota(jnp.int32, (slots, slot.shape[1]), 0) == slot).astype(f32).astype(bf16)


def halves_of(v):
    high = v.astype(bf16)
    return jnp.concatenate([high, (v - high.astype(f32)).astype(bf16)], axis=0)


def sum_halves(v):
    v = v.astype(f32)
    n = v.shape[0] // 2
    return v[:n] + v[n:]


def branch_kernel(
    norm_row,
    me_ref,
    back_ref,
    slot_ref,
    dy_ref,
    middle_ref,
    gain_ref,
    w_ref,
    att_ref,
    early_ref,
    grad_ref,
    heads_ref,
    keep_ref,
    send_ref,
    small_ref,
    acc,
):
    g = dg(one_hot_slots(slot_ref[...], back_ref.shape[0]), back_ref[...], 0, 0)
    v = middle_ref[...]
    centred = v - jnp.mean(v, axis=1, keepdims=True)
    rstd = lax.rsqrt(jnp.mean(centred * centred, axis=1, keepdims=True) + norm_eps)
    xh = centred * rstd
    dn = g * gain_ref[...]
    grad = rstd * (dn - jnp.mean(dn, axis=1, keepdims=True) - xh * jnp.mean(dn * xh, axis=1, keepdims=True))
    grad = dy_ref[...].astype(f32) + grad
    grad_ref[...] = grad
    low = grad.astype(bf16)
    heads_ref[...] = dg(w_ref[...], low, 1, 1).astype(bf16).reshape(heads_ref.shape)
    row = lax.broadcasted_iota(jnp.int32, small_ref.shape, 0)
    small = early_ref[...] + jnp.where(row == norm_row, jnp.sum(g * xh, axis=0, keepdims=True), 0.0)
    small_ref[...] = small
    acc[...] = dg(att_ref[...], low, 1, 0)
    nx, w, _ = keep_ref.shape
    for x in range(nx):
        keep_ref[x] = acc[pl.ds(pl.multiple_of((2 * x + me_ref[0]) * w, w), w)]
        send_ref[x * w : (x + 1) * w] = acc[pl.ds(pl.multiple_of((2 * x + 1 - me_ref[0]) * w, w), w)].astype(bf16)
    send_ref[nx * w :] = halves_of(small)


def whole_block(shape):
    return pl.BlockSpec(shape, lambda i, p: (0,) * len(shape))


def one_step(kernel, name, outs, args, scratch, flops):
    return pl.pallas_call(
        kernel,
        out_shape=tuple(jax.ShapeDtypeStruct(shape, dtype) for shape, dtype in outs),
        grid_spec=pltpu.PrefetchScalarGridSpec(
            num_scalar_prefetch=1,
            grid=(1,),
            in_specs=[whole_block(a.shape) for a in args[1:]],
            out_specs=tuple(whole_block(shape) for shape, _ in outs),
            scratch_shapes=scratch,
        ),
        compiler_params=pltpu.CompilerParams(vmem_limit_bytes=VMEM),
        cost_estimate=pl.CostEstimate(
            flops=flops, bytes_accessed=4 * sum(a.size for a in args), transcendentals=0
        ),
        name=name,
    )(*args)


def branch_back(ci, back, slot, dy, middle, gain, w, attT, early, norm_row, ctx):
    rows = dy.shape[0]
    mine = D // ctx
    outs = (
        ((rows, D), f32),
        ((ctx, HEADS // ctx, HD, rows), bf16),
        ((ctx // 2, mine, D), f32),
        ((ctx // 2 * mine + 2 * early.shape[0], D), bf16),
        (early.shape, f32),
    )
    return one_step(
        functools.partial(branch_kernel, norm_row),
        "branch_back",
        outs,
        (ci, back, slot, dy, middle, gain, w, attT, early),
        [pltpu.VMEM((D, D), f32)],
        2 * rows * D * (back.shape[0] + 2 * D),
    )


def go_kernel(me_ref, keep_ref, got_ref, small_ref, own_ref, send_ref, sum_ref, acc):
    nx, w, _ = keep_ref.shape
    for x in range(nx):
        acc[x] = keep_ref[x] + got_ref[x * w : (x + 1) * w].astype(f32)
    small = small_ref[...] + sum_halves(got_ref[nx * w :])
    sum_ref[...] = small
    own_ref[...] = acc[me_ref[0]]
    send_ref[:w] = acc[1 - me_ref[0]].astype(bf16)
    send_ref[w:] = halves_of(small)


def go_step(xi, keep, got, small):
    w = keep.shape[1]
    outs = (((w, D), f32), ((w + 2 * small.shape[0], D), bf16), (small.shape, f32))
    return one_step(go_kernel, "go_step", outs, (xi, keep, got, small), [pltpu.VMEM(keep.shape, f32)], 0)


def weight_rows_kernel(half_ref, dT_ref, normed_ref, go_ref, got_ref, early_ref, keep_ref, send_ref, small_ref, acc):
    n = dT_ref.shape[0]
    w = go_ref.shape[0]
    half = keep_ref.shape[0]
    acc[:n] = dg(dT_ref[...], normed_ref[...], 1, 0)
    acc[n:] = go_ref[...] + got_ref[:w].astype(f32)
    small = early_ref[...] + sum_halves(got_ref[w:])
    small_ref[...] = small
    a = pl.multiple_of(half_ref[0] * half, half)
    b = pl.multiple_of((1 - half_ref[0]) * half, half)
    keep_ref[...] = acc[pl.ds(a, half)]
    send_ref[:half] = acc[pl.ds(b, half)].astype(bf16)
    send_ref[half:] = halves_of(small)


def weight_rows(half, dT, normed, go, got, small):
    rows = dT.shape[0] + go.shape[0]
    outs = (((rows // 2, D), f32), ((rows // 2 + 2 * small.shape[0], D), bf16), (small.shape, f32))
    return one_step(
        weight_rows_kernel,
        "weight_rows",
        outs,
        (half, dT, normed, go, got, small),
        [pltpu.VMEM((rows, D), f32)],
        2 * dT.size * D,
    )


def share_kernel(me_ref, half_ref, got_ref, early_ref, own_ref, *refs):
    dp = len(refs) - 1
    sends, small_ref, acc = refs[: dp - 1], refs[dp - 1], refs[dp]
    half = half_ref.shape[0]
    w = half // dp
    acc[...] = half_ref[...] + got_ref[:half].astype(f32)
    small = early_ref[...] + sum_halves(got_ref[half:])
    small_ref[...] = small

    def share(step):
        return acc[pl.ds(pl.multiple_of(lax.rem(me_ref[0] + step, dp) * w, w), w)]

    own_ref[...] = share(0)
    for step in range(1, dp):
        sends[step - 1][:w] = share(step).astype(bf16)
        sends[step - 1][w:] = halves_of(small)


def share_step(zi, half, got, small, dp):
    w = half.shape[0] // dp
    outs = (((w, D), f32),) + (((w + 2 * small.shape[0], D), bf16),) * (dp - 1) + ((small.shape, f32),)
    return one_step(
        functools.partial(share_kernel),
        "share_step",
        outs,
        (zi, half, got, small),
        [pltpu.VMEM(half.shape, f32)],
        0,
    )


def finish_kernel(dp, me_ref, *refs):
    pieces = refs[:10]
    weights = refs[10:13]
    scale_ref = refs[13]
    outs = refs[14:18]
    gain_ref = refs[18]
    got, wide, held, in_sem, out_sem, w_sem = refs[19:]
    z, xi, ci, yi = me_ref[0], me_ref[1], me_ref[2], me_ref[3]
    rows = pieces[0].shape[0] // dp
    copies = [pltpu.make_async_copy(weights[p], held.at[p], w_sem.at[p]) for p in range(3)]
    for n in range(10):
        k = n % 5
        c, x, y = (n // 5) ^ ci, int(k > 1) ^ xi, int(k != 0 and k != 2) ^ yi
        for i in range(pieces[n].shape[0] // rows):
            r = i + dp // 2 if k == 4 else i
            j = y * dp + lax.rem(z + dp - r, dp)
            p = lax.div(j * 4, 2 * dp)
            first = (x * 2 + c) * (D // 4) + lax.rem(j, 2 * dp // 4) * rows
            copy = pltpu.make_async_copy(
                pieces[n].at[pl.ds(i * rows, rows)],
                got.at[p, pl.ds(pl.multiple_of(first, rows), rows)],
                in_sem.at[n, i],
            )
            copies.append(copy)
    for copy in copies[3:] + copies[:3]:
        copy.start()
    for copy in copies:
        copy.wait()
    gain = jnp.zeros((D, 1), f32)
    backs = []
    for p in (3, 0, 1, 2):
        if p < 3:
            g = got[p].T.astype(f32)
            gain = gain + jnp.sum(g * held[p].astype(f32), axis=1, keepdims=True)
        else:
            g = got[p].astype(f32)
        wide[p] = g
        back = pltpu.make_async_copy(wide.at[p], outs[p], out_sem.at[p])
        back.start()
        backs.append(back)
    gain_ref[...] = jnp.broadcast_to(gain, (D, 128)).T[:8] / scale_ref[...]
    for back in backs:
        back.wait()


def finish(me, pieces, weights, scale, dp):
    whole = jax.ShapeDtypeStruct((D, D), f32)
    anywhere = pl.BlockSpec(memory_space=pl.ANY)
    return pl.pallas_call(
        functools.partial(finish_kernel, dp),
        out_shape=(whole,) * 4 + (jax.ShapeDtypeStruct((8, D), f32),),
        grid_spec=pltpu.PrefetchScalarGridSpec(
            num_scalar_prefetch=1,
            grid=(1,),
            in_specs=[anywhere] * 13
            + [pl.BlockSpec((1, D), lambda i, p: (0, 0))],
            out_specs=(anywhere,) * 4 + (pl.BlockSpec((8, D), lambda i, p: (0, 0)),),
            scratch_shapes=[
                pltpu.VMEM((4, D, D), bf16),
                pltpu.VMEM((4, D, D), f32),
                pltpu.VMEM((3, D, D), bf16),
                pltpu.SemaphoreType.DMA((10, dp)),
                pltpu.SemaphoreType.DMA((4,)),
                pltpu.SemaphoreType.DMA((3,)),
            ],
        ),
        compiler_params=pltpu.CompilerParams(vmem_limit_bytes=VMEM),
        cost_estimate=pl.CostEstimate(flops=8 * D * D, bytes_accessed=32 * D * D, transcendentals=0),
        name="finish",
    )(me, *pieces, *weights, scale)


def swap(v, axis):
    return lax.ppermute(v, axis, [(0, 1), (1, 0)])


def shift(v, axis, step):
    n = lax.axis_size(axis)
    return lax.ppermute(v, axis, [(i, (i + step) % n) for i in range(n)])


def at(v, index):
    return lax.dynamic_index_in_dim(v, index, 0, keepdims=False)


def one(v):
    v = v.astype(f32)
    n = v.shape[0] // 2
    return v[:n] + v[n:]


def add_pair(v):
    return v + (swap(v, "expert") if lax.axis_size("expert") == 2 else lax.psum(v, "expert") - v)


def add_shifts(v):
    out = v
    for s in range(1, lax.axis_size("dp")):
        out = out + shift(v, "dp", s)
    return out


def index(i):
    return i.astype(jnp.int32).reshape(1)


def tie(*arrays):
    return lax.optimization_barrier(arrays)


def normal_form(v):
    centred = v - jnp.mean(v, axis=-1, keepdims=True)
    rstd = lax.rsqrt(jnp.mean(centred * centred, axis=-1, keepdims=True) + norm_eps)
    return centred * rstd, rstd


def norm_back(dn, xh, rstd):
    return rstd * (dn - jnp.mean(dn, axis=-1, keepdims=True) - xh * jnp.mean(dn * xh, axis=-1, keepdims=True))


def per_device(
    tokens,
    cotangent,
    routes,
    norm1_gain,
    w_query,
    w_key,
    w_value,
    w_output,
    norm2_gain,
    w_router,
    w_in,
    w_out,
):
    rows = tokens.shape[1]
    nx, owners, dp = lax.axis_size("x"), lax.axis_size("expert"), lax.axis_size("dp")
    xi, ci, ei = lax.axis_index("x"), lax.axis_index("core"), lax.axis_index("expert")
    ctx = 2 * nx
    ctx_i = xi * 2 + ci
    length = ctx * rows
    experts = w_router.shape[1]
    cap = 2 * rows // experts
    mine = D // ctx
    heads = mine // HD
    expert_id = ei * nx + xi
    pick = jnp.stack([xi, ci, expert_id]).astype(jnp.int32)

    tok = tokens.reshape(rows, D)
    flat = tok.astype(f32)
    other = swap(tok, "x")
    near = swap(tok, "core")

    route = routes.reshape(rows)
    hot = (route[:, None] == jnp.arange(128, dtype=jnp.int32)[None, :]).astype(f32)
    lower = jnp.arange(rows)[:, None] >= jnp.arange(rows)[None, :]
    before = dg(lower.astype(bf16), hot.astype(bf16), 1, 0)
    rank = (jnp.sum(before * hot, axis=1) - 1.0).astype(jnp.int32)
    slot = ((route % nx) * owners + route // nx) * cap + rank
    spread = (jnp.arange(experts * cap, dtype=jnp.int32)[:, None] == slot[None, :]).astype(bf16)

    def pack(v):
        return dg(spread, v, 1, 0).astype(bf16).reshape(nx * owners, cap, D)

    def trade(v):
        v = lax.all_to_all(v.reshape(nx * owners, cap, D), ("x", "expert"), split_axis=0, concat_axis=0, tiled=True)
        return v.reshape(-1, D)

    def turn(v):
        return lax.all_to_all(v, ("x", "core"), split_axis=0, concat_axis=0, tiled=True)

    def cut(w):
        return lax.dynamic_slice(w, (0, ctx_i * mine), (D, mine))

    w_own = jnp.concatenate([cut(w_query), cut(w_key), cut(w_value)], axis=1)
    gain1 = norm1_gain.reshape(1, D)
    dy_low = cotangent.reshape(rows, D)
    dy = dy_low.astype(f32)
    wr = lax.dynamic_slice(w_router, (0, expert_id), (D, 1)).astype(f32).reshape(1, D)
    counts = jnp.sum(hot, axis=0, keepdims=True)
    counts = counts + swap(counts, "core")
    counts = add_pair(counts)
    so_far = project(ctx_i, tok, gain1, w_own, ctx, None)
    counts, dy_packed, *so_far = tie(counts, pack(dy_low), *so_far)
    so_far = project(ctx_i ^ 1, near, gain1, w_own, ctx, so_far)
    other, dy_packed, *so_far = tie(other, dy_packed, *so_far)
    far = swap(other, "core")
    dy_rows = trade(dy_packed)
    so_far = project(ctx_i ^ 2, other, gain1, w_own, ctx, so_far)
    normed_all, qkvT, kv = project(ctx_i ^ 3, far, gain1, w_own, ctx, so_far)
    oT, osend, lse = attend(qkvT, kv, ctx)
    osend, dy_rows, counts = tie(osend, dy_rows, counts)
    attT = turn(osend)
    counts = add_shifts(counts)
    attT, counts = tie(attT, counts)
    counts = counts + swap(counts, "x")
    attT = attT.reshape(D, rows)
    mean_load = rows * ctx * dp * owners / experts
    middle = flat + dg(attT, w_output, 0, 0)
    xh2, rstd2 = normal_form(middle)
    second = (xh2 * norm2_gain).astype(bf16)
    gating = jax.nn.sigmoid(jnp.sum(hot[:, :experts] * dg(second, w_router, 1, 0), axis=1))

    up = expert_up(pick, dy_rows, w_out)
    sig = jnp.pad(jnp.sum(hot[:, :experts] * gating[:, None], axis=0), (0, D - experts))
    counts, packed = tie(counts, pack(second))
    x_rows = trade(packed)
    x_rows, gating, sig, slot, gain2 = tie(x_rows, gating, sig, slot[None], norm2_gain.reshape(1, D))
    active, grad_hidden, back_rows, router_row, gate = expert_mid(pick, x_rows, up, w_in, wr, counts, mean_load)
    returned = trade(back_rows)
    keep, send = expert_grads(pick, x_rows, dy_rows, gate, active, grad_hidden, dp, nx)
    produced = expert_out(pick, tie(active, keep)[0], w_out)
    returned, keep, send, produced = tie(returned, keep, send, produced)
    taken = swap(send, "core")
    zi = lax.axis_index("dp")

    def chunk(i):
        return at(keep, (i + dp) % dp).astype(f32) + at(taken, (i + dp) % dp).astype(f32)

    def ring(moving, step):
        return (shift(moving, "dp", 1).astype(f32) + chunk(zi - 2 - step)).astype(bf16)

    def side(v, x):
        return lax.dynamic_index_in_dim(v, x, 1, keepdims=False)

    router_rows = (jnp.arange(experts) == expert_id).astype(f32)[:, None] * router_row
    small = jnp.concatenate([router_rows, jnp.zeros((1, D), f32), sig[None]], axis=0)
    small = jnp.pad(small, ((0, -small.shape[0] % 8), (0, 0)))
    grad_middle, heads_grad, go, go_send, small = branch_back(
        index(ci), returned, slot, dy_low, middle, gain2, w_output, attT, small, experts, ctx
    )
    do = turn(heads_grad)

    moving = ring(chunk(zi - 1).astype(bf16), 0)
    go_got = swap(go_send, "core")
    go, go_send, small = go_step(index(xi), go, go_got, small)
    do, go_send = tie(do, go_send)
    go_got = swap(go_send, "x")

    so_far = attend_back(qkvT, kv, do, 0, oT, lse, 0, None)
    produced, go_got, *so_far = tie(produced, go_got, *so_far)
    went_back = trade(produced)
    so_far = attend_back(qkvT, kv, do, 1, oT, lse, 1, so_far)
    moving, *so_far = tie(moving, *so_far)
    moving = ring(moving, 1)
    for h in range(2, heads):
        so_far = attend_back(qkvT, kv, do, h, oT, lse, h, so_far)
    went_back, dT, dsend = tie(went_back, *so_far)
    output = (middle + gating[:, None] * dg(spread, went_back, 0, 0)).astype(bf16)

    ei2 = ei if owners == 2 else jnp.zeros_like(ei)
    half, send, small = weight_rows(index(ei2), dT.reshape(3 * mine, length), normed_all, go, go_got, small)
    dsend, send = tie(dsend, send)
    got = turn(dsend)
    if owners == 2:
        gift = swap(send, "expert")
        gift, moving = tie(gift, moving)
        halves = [(half, gift)]
    else:
        cut_at = half.shape[0]
        small = lax.psum(small, "expert")
        nothing = jnp.zeros_like(send)
        halves = [(lax.psum(half, "expert"), nothing), (lax.psum(send[:cut_at].astype(f32), "expert"), nothing)]
    pieces = []
    for part, gift in halves:
        share, *gifts, more = share_step(index(zi), part, gift, small, dp)
        gifts = [shift(gift, "dp", step + 1) for step, gift in enumerate(gifts)]
        for gift in gifts:
            more = more + one(gift[share.shape[0] :])
            share = share + gift[: share.shape[0]].astype(f32)
        share = share.astype(bf16)
        pieces.append(jnp.concatenate([share] + [shift(share, "dp", step) for step in range(1, dp)], axis=0))
    small = more
    output, keep, taken = tie(output, keep, taken)
    crossed = swap(side(chunk(zi), 1 - xi).astype(bf16), "x")
    for step in range(2, dp - 2):
        moving = ring(moving, step)
    moving, crossed, *pieces = tie(moving, crossed, *pieces)
    own = shift(side(moving, xi), "dp", 1)
    route_on = [(z * nx + x, (z + 1) % dp * nx + 1 - x) for z in range(dp) for x in range(nx)]
    theirs = side(moving, 1 - xi)

    grad_normed = 0.0
    for p, w in enumerate((w_query, w_key, w_value)):
        grad_normed = grad_normed + dg(got[:, p].reshape(D, rows), w, 0, 1)
    xh1, rstd1 = normal_form(flat)
    grad_tokens = grad_middle + norm_back(grad_normed * norm1_gain, xh1, rstd1)

    if owners == 2:
        pieces.append(swap(pieces[0], "expert"))
    beyond = swap(pieces[0], "x")
    pieces[1], beyond, theirs, grad_tokens = tie(pieces[1], beyond, theirs, grad_tokens)
    moved = lax.ppermute(theirs, ("dp", "x"), route_on)
    rest = pieces[0].shape[0] // 2
    if owners == 2:
        corner = [swap(pieces[1][:rest], "x"), swap(beyond[rest:], "expert")]
    else:
        corner = [swap(pieces[1][:rest], "x"), swap(pieces[1][rest:], "x")]
    own, *corner = tie(own, *corner)
    pieces += [beyond, *corner]
    pieces += [swap(piece, "core") for piece in pieces]
    me = jnp.stack([zi, xi, ci, ei2]).astype(jnp.int32)
    *grads, grad_norm1 = finish(me, pieces, (w_query, w_key, w_value), gain1, dp)
    grad_norm1 = grad_norm1[0]

    own = own.astype(f32) + side(chunk(zi), xi)
    moved = moved.astype(f32) + crossed.astype(f32)
    first, latter = jnp.where(xi == 0, own, moved), jnp.where(xi == 0, moved, own)
    both = jnp.stack([first, latter], axis=1)
    grad_in = jnp.swapaxes(both[0], 1, 2)
    grad_out = both[1]

    grad_router = jnp.transpose(small[:experts])
    grad_norm2 = small[experts]
    total_sig = small[experts + 1, :experts]
    counts = counts[0, :experts]
    balance = balance_weight * jnp.sum((counts - mean_load) / mean_load * total_sig) / mean_load

    return (
        output.reshape(1, rows, D),
        grad_tokens.reshape(1, rows, D),
        grad_norm1,
        grads[0],
        grads[1],
        grads[2],
        grads[3],
        grad_norm2,
        grad_router,
        grad_in,
        grad_out,
        balance,
    )


def solution(mesh):
    dp, ctx, owners = mesh.shape["dp"], mesh.shape["ctx"], mesh.shape["expert"]
    split = Mesh(mesh.devices.reshape(dp, ctx // 2, 2, owners), ("dp", "x", "core", "expert"))
    token = P(("dp", "expert"), ("x", "core"), None)
    return jax.shard_map(
        per_device,
        mesh=split,
        in_specs=(token, token, token, P(), P(), P(), P(), P(), P(), P(), P("expert"), P("expert")),
        out_specs=(
            token,
            token,
            P(),
            P(),
            P(),
            P(),
            P(),
            P(),
            P(),
            P("expert", None, ("dp", "x", "core")),
            P("expert", ("dp", "x", "core"), None),
            P(),
        ),
        check_vma=False,
    )
```

```python
import functools

import jax
import jax.numpy as jnp
from jax import lax
from jax.experimental import pallas as pl
from jax.experimental.pallas import tpu as pltpu
from jax.sharding import Mesh
from jax.sharding import PartitionSpec as P

D = 768
HEADS = 12
HD = 64
norm_eps = 1e-05
balance_weight = 1.0
LOG2E = 1.4426950408889634
MASKED = -1e30
GELU_A = 0.7978845608028654
GELU_B = 0.044715
VMEM = 56 * 1024 * 1024
f32 = jnp.float32
bf16 = jnp.bfloat16


def dg(a, b, ca, cb):
    return lax.dot_general(a, b, (((ca,), (cb,)), ((), ())), preferred_element_type=f32)


def project_kernel(place_ref, *refs):
    normed_ref, qkvT_ref, kv_ref = refs[-3:]
    blocks = place_ref.shape[0]
    gain_ref, w_ref = refs[blocks : blocks + 2]

    def work(tok_ref):
        x = tok_ref[...].astype(f32)
        centred = x - jnp.mean(x, axis=1, keepdims=True)
        rstd = lax.rsqrt(jnp.mean(centred * centred, axis=1, keepdims=True) + norm_eps)
        normed = (centred * rstd * gain_ref[...]).astype(bf16)
        normed_ref[...] = normed
        qkv = dg(normed, w_ref[...], 1, 0).astype(bf16)
        kv_ref[...] = qkv[:, qkv.shape[1] - kv_ref.shape[1] :]
        qkvT_ref[...] = qkv.T

    for k in range(blocks):

        @pl.when(pl.program_id(0) == k)
        def _():
            work(refs[k])


def project(places, toks, gain, w, ctx, so_far):
    rows = toks[0].shape[0]
    wide = w.shape[1]
    args = [*toks, gain, w]
    specs = [pl.BlockSpec(a.shape, lambda i, p: (0, 0)) for a in args]
    alias = {}
    if so_far is not None:
        alias = {1 + len(args) + k: k for k in range(3)}
        args += list(so_far)
        specs += [pl.BlockSpec(memory_space=pl.ANY)] * 3
    return pl.pallas_call(
        project_kernel,
        out_shape=(
            jax.ShapeDtypeStruct((ctx * rows, D), bf16),
            jax.ShapeDtypeStruct((wide, ctx * rows), bf16),
            jax.ShapeDtypeStruct((ctx * rows, 2 * wide // 3), bf16),
        ),
        grid_spec=pltpu.PrefetchScalarGridSpec(
            num_scalar_prefetch=1,
            grid=(len(toks),),
            in_specs=specs,
            out_specs=(
                pl.BlockSpec((rows, D), lambda i, p: (p[i], 0)),
                pl.BlockSpec((wide, rows), lambda i, p: (0, p[i])),
                pl.BlockSpec((rows, 2 * wide // 3), lambda i, p: (p[i], 0)),
            ),
        ),
        input_output_aliases=alias,
        compiler_params=pltpu.CompilerParams(vmem_limit_bytes=VMEM),
        cost_estimate=pl.CostEstimate(
            flops=4 * len(toks) * rows * D * wide, bytes_accessed=4 * rows * D + 8 * rows * wide, transcendentals=0
        ),
        name="project",
    )(jnp.stack(places).astype(jnp.int32), *args)


def attend_kernel(heads, blk, qT_ref, k_ref, vT_ref, oT_ref, osend_ref, lse_ref):
    length = qT_ref.shape[1]
    per = osend_ref.shape[3]
    c = (HD**-0.5) * LOG2E
    rows = lax.broadcasted_iota(jnp.int32, (blk, blk), 0)
    cols = lax.broadcasted_iota(jnp.int32, (blk, blk), 1)
    keep = rows <= cols
    for h in range(heads):
        hs = slice(h * HD, (h + 1) * HD)
        for i in range(length // blk):
            a, b = i * blk, (i + 1) * blk
            q = qT_ref[hs, a:b]
            sd = dg(k_ref[a:b, hs], q, 1, 0)
            sd = jnp.where(keep, sd, MASKED)
            m = jnp.max(sd, axis=0, keepdims=True)
            if i:
                s = dg(k_ref[:a, hs], q, 1, 0)
                m = jnp.maximum(m, jnp.max(s, axis=0, keepdims=True))
            mc = m * c
            pd = jnp.exp2(sd * c - mc)
            total = jnp.sum(pd, axis=0, keepdims=True)
            o = dg(vT_ref[hs, a:b], pd.astype(bf16), 1, 0)
            if i:
                p = jnp.exp2(s * c - mc)
                total = total + jnp.sum(p, axis=0, keepdims=True)
                o = o + dg(vT_ref[hs, :a], p.astype(bf16), 1, 0)
            o = o / total
            oT_ref[hs, a:b] = o
            d, off = a // per, a % per
            osend_ref[d, h, :, off : off + blk] = o.astype(bf16)
            lse_ref[h, :, a:b] = mc + jnp.log2(total)


def attend(qkvT, kv, dests):
    length = kv.shape[0]
    heads = qkvT.shape[0] // (3 * HD)
    wide = heads * HD
    per = length // dests
    return pl.pallas_call(
        functools.partial(attend_kernel, heads, per),
        out_shape=(
            jax.ShapeDtypeStruct((wide, length), f32),
            jax.ShapeDtypeStruct((dests, heads, HD, per), bf16),
            jax.ShapeDtypeStruct((heads, 1, length), f32),
        ),
        grid=(1,),
        in_specs=[
            pl.BlockSpec((wide, length), lambda i: (0, 0)),
            pl.BlockSpec(kv.shape, lambda i: (0, 0)),
            pl.BlockSpec((wide, length), lambda i: (2, 0)),
        ],
        out_specs=(
            pl.BlockSpec((wide, length), lambda i: (0, 0)),
            pl.BlockSpec((dests, heads, HD, per), lambda i: (0, 0, 0, 0)),
            pl.BlockSpec((heads, 1, length), lambda i: (0, 0, 0)),
        ),
        compiler_params=pltpu.CompilerParams(vmem_limit_bytes=VMEM),
        cost_estimate=pl.CostEstimate(
            flops=8 * heads * length * length * HD,
            bytes_accessed=length * wide * 14,
            transcendentals=heads * length * length // 2,
        ),
        name="attend",
    )(qkvT, kv, qkvT)


def attend_back_kernel(lk, lv, blk, *refs):
    qT_ref, k_ref, kT_ref, v_ref, do_ref, oT_ref, lse_ref = refs[:7]
    dT_ref, dsend_ref, dk_acc, dv_acc = refs[-4:]
    length = qT_ref.shape[1]
    per = do_ref.shape[3]
    sc = HD**-0.5
    c = sc * LOG2E
    rows = lax.broadcasted_iota(jnp.int32, (blk, blk), 0)
    cols = lax.broadcasted_iota(jnp.int32, (blk, blk), 1)
    keep = rows <= cols
    n = length // blk
    for i in reversed(range(n)):
        x0, x1 = i * blk, (i + 1) * blk
        d, off = x0 // per, x0 % per
        q = qT_ref[:, x0:x1]
        do = do_ref[d, 0, :, off : off + blk]
        lse = lse_ref[0, :, x0:x1]
        delta = jnp.sum(do.astype(f32) * oT_ref[:, x0:x1], axis=0, keepdims=True)
        dq = None
        for a, b, diag in ([(0, x0, False)] if i else []) + [(x0, x1, True)]:
            s = dg(k_ref[a:b, lk : lk + HD], q, 1, 0)
            p = jnp.exp2(s * c - lse)
            if diag:
                p = jnp.where(keep, p, 0.0)
            dp = dg(v_ref[a:b, lv : lv + HD], do, 1, 0)
            ds = (p * (dp - delta)).astype(bf16)
            dvn = dg(do, p.astype(bf16), 1, 1)
            dkn = dg(q, ds, 1, 1)
            if i == n - 1:
                dv_acc[:, a:b] = dvn
                dk_acc[:, a:b] = dkn
            else:
                dv_acc[:, a:b] += dvn
                dk_acc[:, a:b] += dkn
            t = dg(kT_ref[:, a:b], ds, 1, 0)
            dq = t if dq is None else dq + t
        dq = (dq * sc).astype(bf16)
        dT_ref[0, :, x0:x1] = dq
        dsend_ref[d, 0, :, off : off + blk] = dq
    for d in range(dsend_ref.shape[0]):
        at_d = slice(d * per, (d + 1) * per)
        dk = (dk_acc[:, at_d] * sc).astype(bf16)
        dv = dv_acc[:, at_d].astype(bf16)
        dT_ref[1, :, at_d] = dk
        dT_ref[2, :, at_d] = dv
        dsend_ref[d, 1] = dk
        dsend_ref[d, 2] = dv


def attend_back(qkvT, kv, do, slot, oT, lse, h, so_far):
    length = kv.shape[0]
    n = qkvT.shape[0] // (3 * HD)
    dests, _, _, per = do.shape
    hv = n + h
    blk = min(256, per)
    args = [qkvT, kv, qkvT, kv, do, oT, lse]
    specs = [
        pl.BlockSpec((HD, length), lambda i: (h, 0)),
        pl.BlockSpec((length, 2 * HD), lambda i: (0, h // 2)),
        pl.BlockSpec((HD, length), lambda i: (n + h, 0)),
        pl.BlockSpec((length, 2 * HD), lambda i: (0, hv // 2)),
        pl.BlockSpec((dests, 1, HD, per), lambda i: (0, slot, 0, 0)),
        pl.BlockSpec((HD, length), lambda i: (h, 0)),
        pl.BlockSpec((1, 1, length), lambda i: (h, 0, 0)),
    ]
    alias = {}
    if so_far is not None:
        alias = {len(args): 0, len(args) + 1: 1}
        args += list(so_far)
        specs += [pl.BlockSpec(memory_space=pl.ANY)] * 2
    return pl.pallas_call(
        functools.partial(attend_back_kernel, (h % 2) * HD, (hv % 2) * HD, blk),
        out_shape=(
            jax.ShapeDtypeStruct((3, n * HD, length), bf16),
            jax.ShapeDtypeStruct((dests, 3, n * HD, per), bf16),
        ),
        grid=(1,),
        in_specs=specs,
        out_specs=(
            pl.BlockSpec((3, HD, length), lambda i: (0, h, 0)),
            pl.BlockSpec((dests, 3, HD, per), lambda i: (0, 0, h, 0)),
        ),
        scratch_shapes=[pltpu.VMEM((HD, length), f32)] * 2,
        input_output_aliases=alias,
        compiler_params=pltpu.CompilerParams(vmem_limit_bytes=VMEM),
        cost_estimate=pl.CostEstimate(
            flops=20 * length * length * HD, bytes_accessed=length * HD * 24, transcendentals=length * length // 2
        ),
        name=f"attend_back_head{h}",
    )(*args)


def middle_kernel(me_ref, att_ref, tok_ref, w_ref, gain_ref, slot_ref, middle_ref, second_ref, packed_ref):
    v = tok_ref[...].astype(f32) + dg(att_ref[...], w_ref[...], 0, 0)
    middle_ref[...] = v
    centred = v - jnp.mean(v, axis=1, keepdims=True)
    rstd = lax.rsqrt(jnp.mean(centred * centred, axis=1, keepdims=True) + norm_eps)
    second = (centred * rstd * gain_ref[...]).astype(bf16)
    second_ref[...] = second
    spread = one_hot_slots(slot_ref[...], packed_ref.shape[0] * packed_ref.shape[1])
    packed_ref[...] = dg(spread, second, 1, 0).astype(bf16).reshape(packed_ref.shape)


def middle_step(attT, tok, w, gain, slot, sources, cap):
    rows = tok.shape[0]
    outs = (((rows, D), f32), ((rows, D), bf16), ((sources, cap, D), bf16))
    return one_step(
        middle_kernel,
        "middle_step",
        outs,
        (jnp.zeros((1,), jnp.int32), attT, tok, w, gain, slot),
        [],
        2 * rows * D * (D + sources * cap),
    )


def up_kernel(pick_ref, dy_ref, wo_ref, u_ref):
    u_ref[...] = dg(dy_ref[...], wo_ref[0], 1, 1).astype(bf16)


def expert_up(pick, dy, w_out, fc=768):
    rows = dy.shape[0]
    ff = w_out.shape[1]
    return pl.pallas_call(
        up_kernel,
        out_shape=jax.ShapeDtypeStruct((rows, ff), bf16),
        grid_spec=pltpu.PrefetchScalarGridSpec(
            num_scalar_prefetch=1,
            grid=(ff // fc,),
            in_specs=[
                pl.BlockSpec((rows, D), lambda f, p: (0, 0)),
                pl.BlockSpec((1, fc, D), lambda f, p: (p[0], f, 0)),
            ],
            out_specs=pl.BlockSpec((rows, fc), lambda f, p: (0, f)),
        ),
        compiler_params=pltpu.CompilerParams(vmem_limit_bytes=VMEM),
        cost_estimate=pl.CostEstimate(
            flops=2 * rows * D * ff, bytes_accessed=2 * (rows * D + ff * D + rows * ff), transcendentals=0
        ),
        name="expert_up",
    )(pick, dy, w_out)


def mid_kernel(
    mean, pick_ref, x_ref, u_ref, wi_ref, wr_ref, count_ref, act_ref, gh_ref, rows_ref, router_ref, gate_ref, acc, gg, gate
):
    f = pl.program_id(0)
    n = pl.num_programs(0)

    @pl.when(f == 0)
    def _():
        logit = jnp.sum(x_ref[...].astype(f32) * wr_ref[...], axis=1, keepdims=True)
        gate[...] = jnp.broadcast_to(jax.nn.sigmoid(logit), gate.shape)
        acc[...] = jnp.zeros_like(acc)
        gg[...] = jnp.zeros_like(gg)

    step = 256
    for r in range(0, x_ref.shape[0], step):
        rs = slice(r, r + step)
        for c in range(0, wi_ref.shape[2], step):
            cs = slice(c, c + step)
            h = dg(x_ref[rs], wi_ref[0, :, cs], 1, 0)
            h2 = h * h
            t = jnp.tanh(h * (GELU_A + (GELU_A * GELU_B) * h2))
            hp = 0.5 + 0.5 * t
            dgelu = hp + (h * (hp - hp * hp)) * (2.0 * GELU_A + (6.0 * GELU_A * GELU_B) * h2)
            u = u_ref[rs, cs].astype(f32)
            active = h * hp
            act_ref[rs, cs] = active.astype(bf16)
            au = active * u
            lanes = au[:, :128]
            for j in range(128, step, 128):
                lanes = lanes + au[:, j : j + 128]
            gg[rs] += lanes
            gh = (gate[rs, :1] * (u * dgelu)).astype(bf16)
            gh_ref[rs, cs] = gh
            acc[rs] += dg(gh, wi_ref[0, :, cs], 1, 1)

    @pl.when(f == n - 1)
    def _():
        g = gate[:, :1]
        got = jnp.sum(gg[...], axis=1, keepdims=True)
        lane = lax.broadcasted_iota(jnp.int32, count_ref.shape, 1)
        count = jnp.sum(jnp.where(lane == pick_ref[2], count_ref[...], 0.0), axis=1, keepdims=True)
        load = balance_weight * (count - mean) / (mean * mean)
        sel = (g * (1.0 - g) * (got + load)).astype(bf16).astype(f32)
        rows_ref[...] = (acc[...] + sel * wr_ref[...]).astype(bf16)
        router_ref[...] = jnp.sum(x_ref[...].astype(f32) * sel, axis=0, keepdims=True)
        gate_ref[...] = gate[...]


def expert_mid(pick, x, u, w_in, wr, counts, mean, fc=768):
    rows = x.shape[0]
    ff = w_in.shape[2]

    def full(s):
        return pl.BlockSpec(s, lambda f, p: (0, 0))

    wide = pl.BlockSpec((rows, fc), lambda f, p: (0, f))
    return pl.pallas_call(
        functools.partial(mid_kernel, mean),
        out_shape=(
            jax.ShapeDtypeStruct((rows, ff), bf16),
            jax.ShapeDtypeStruct((rows, ff), bf16),
            jax.ShapeDtypeStruct((rows, D), bf16),
            jax.ShapeDtypeStruct((1, D), f32),
            jax.ShapeDtypeStruct((rows, 128), f32),
        ),
        grid_spec=pltpu.PrefetchScalarGridSpec(
            num_scalar_prefetch=1,
            grid=(ff // fc,),
            in_specs=[
                full((rows, D)),
                wide,
                pl.BlockSpec((1, D, fc), lambda f, p: (p[0], 0, f)),
                full((1, D)),
                full((1, 128)),
            ],
            out_specs=(wide, wide, full((rows, D)), full((1, D)), full((rows, 128))),
            scratch_shapes=[
                pltpu.VMEM((rows, D), f32),
                pltpu.VMEM((rows, 128), f32),
                pltpu.VMEM((rows, 128), f32),
            ],
        ),
        compiler_params=pltpu.CompilerParams(vmem_limit_bytes=VMEM),
        cost_estimate=pl.CostEstimate(
            flops=4 * rows * D * ff,
            bytes_accessed=2 * (3 * rows * D + ff * D + 3 * rows * ff),
            transcendentals=rows * ff,
        ),
        name="expert_mid",
    )(pick, x, u, w_in, wr, counts)


def grads_kernel(
    pick_ref, x_ref, dy_ref, gate_ref, act_ref, gh_ref, keep_ref, send_ref, go, gi, gexp
):
    f = pl.program_id(0)

    @pl.when(f == 0)
    def _():
        gexp[...] = (dy_ref[...].astype(f32) * gate_ref[:, :1]).astype(bf16)

    go[...] = dg(act_ref[...], gexp[...], 0, 0).astype(bf16)
    gi[...] = dg(gh_ref[...], x_ref[...], 0, 0).astype(bf16)
    w = keep_ref.shape[3]
    me = pick_ref[1]
    for xx in range(keep_ref.shape[2]):
        a = pl.multiple_of((2 * xx + me) * w, w)
        b = pl.multiple_of((2 * xx + 1 - me) * w, w)
        keep_ref[0, 0, xx] = gi[pl.ds(a, w)]
        keep_ref[0, 1, xx] = go[pl.ds(a, w)]
        send_ref[0, 0, xx] = gi[pl.ds(b, w)]
        send_ref[0, 1, xx] = go[pl.ds(b, w)]


def expert_grads(pick, x, dy, gate, act, gh, dp, nx):
    rows = x.shape[0]
    ff = act.shape[1]
    fc = ff // dp
    w = fc // (2 * nx)

    def full(s):
        return pl.BlockSpec(s, lambda f, p: (0, 0))

    wide = pl.BlockSpec((rows, fc), lambda f, p: (0, f))
    part = jax.ShapeDtypeStruct((dp, 2, nx, w, D), bf16)
    part_spec = pl.BlockSpec((1, 2, nx, w, D), lambda f, p: (f, 0, 0, 0, 0))
    return pl.pallas_call(
        grads_kernel,
        out_shape=(part, part),
        grid_spec=pltpu.PrefetchScalarGridSpec(
            num_scalar_prefetch=1,
            grid=(dp,),
            in_specs=[full((rows, D)), full((rows, D)), full((rows, 128)), wide, wide],
            out_specs=(part_spec, part_spec),
            scratch_shapes=[
                pltpu.VMEM((fc, D), bf16),
                pltpu.VMEM((fc, D), bf16),
                pltpu.VMEM((rows, D), bf16),
            ],
        ),
        compiler_params=pltpu.CompilerParams(vmem_limit_bytes=VMEM),
        cost_estimate=pl.CostEstimate(
            flops=4 * rows * D * ff,
            bytes_accessed=2 * (2 * rows * D + 2 * ff * D + 2 * rows * ff),
            transcendentals=0,
        ),
        name="expert_grads",
    )(pick, x, dy, gate, act, gh)


def out_kernel(pick_ref, act_ref, wo_ref, out_ref, acc):
    f = pl.program_id(0)
    part = dg(act_ref[...], wo_ref[0], 1, 0)

    @pl.when(f == 0)
    def _():
        acc[...] = part

    @pl.when(f > 0)
    def _():
        acc[...] += part

    @pl.when(f == pl.num_programs(0) - 1)
    def _():
        out_ref[...] = acc[...].astype(bf16)


def expert_out(pick, act, w_out, fc=768):
    rows, ff = act.shape
    return pl.pallas_call(
        out_kernel,
        out_shape=jax.ShapeDtypeStruct((rows, D), bf16),
        grid_spec=pltpu.PrefetchScalarGridSpec(
            num_scalar_prefetch=1,
            grid=(ff // fc,),
            in_specs=[
                pl.BlockSpec((rows, fc), lambda f, p: (0, f)),
                pl.BlockSpec((1, fc, D), lambda f, p: (p[0], f, 0)),
            ],
            out_specs=pl.BlockSpec((rows, D), lambda f, p: (0, 0)),
            scratch_shapes=[pltpu.VMEM((rows, D), f32)],
        ),
        compiler_params=pltpu.CompilerParams(vmem_limit_bytes=VMEM),
        cost_estimate=pl.CostEstimate(
            flops=2 * rows * D * ff, bytes_accessed=2 * (rows * D + ff * D + rows * ff), transcendentals=0
        ),
        name="expert_out",
    )(pick, act, w_out)


def one_hot_slots(slot, slots):
    return (lax.broadcasted_iota(jnp.int32, (slots, slot.shape[1]), 0) == slot).astype(f32).astype(bf16)


def halves_of(v):
    high = v.astype(bf16)
    return jnp.concatenate([high, (v - high.astype(f32)).astype(bf16)], axis=0)


def sum_halves(v):
    v = v.astype(f32)
    n = v.shape[0] // 2
    return v[:n] + v[n:]


def branch_kernel(
    norm_row,
    me_ref,
    back_ref,
    slot_ref,
    dy_ref,
    middle_ref,
    gain_ref,
    w_ref,
    att_ref,
    early_ref,
    grad_ref,
    heads_ref,
    keep_ref,
    send_ref,
    small_ref,
    acc,
):
    g = dg(one_hot_slots(slot_ref[...], back_ref.shape[0]), back_ref[...], 0, 0)
    v = middle_ref[...]
    centred = v - jnp.mean(v, axis=1, keepdims=True)
    rstd = lax.rsqrt(jnp.mean(centred * centred, axis=1, keepdims=True) + norm_eps)
    xh = centred * rstd
    dn = g * gain_ref[...]
    grad = rstd * (dn - jnp.mean(dn, axis=1, keepdims=True) - xh * jnp.mean(dn * xh, axis=1, keepdims=True))
    grad = dy_ref[...].astype(f32) + grad
    grad_ref[...] = grad
    low = grad.astype(bf16)
    heads_ref[...] = dg(w_ref[...], low, 1, 1).astype(bf16).reshape(heads_ref.shape)
    row = lax.broadcasted_iota(jnp.int32, small_ref.shape, 0)
    small = early_ref[...] + jnp.where(row == norm_row, jnp.sum(g * xh, axis=0, keepdims=True), 0.0)
    small_ref[...] = small
    acc[...] = dg(att_ref[...], low, 1, 0)
    nx, w, _ = keep_ref.shape
    for x in range(nx):
        keep_ref[x] = acc[pl.ds(pl.multiple_of((2 * x + me_ref[0]) * w, w), w)]
        send_ref[x * w : (x + 1) * w] = acc[pl.ds(pl.multiple_of((2 * x + 1 - me_ref[0]) * w, w), w)].astype(bf16)
    send_ref[nx * w :] = halves_of(small)


def whole_block(shape):
    return pl.BlockSpec(shape, lambda i, p: (0,) * len(shape))


def one_step(kernel, name, outs, args, scratch, flops):
    return pl.pallas_call(
        kernel,
        out_shape=tuple(jax.ShapeDtypeStruct(shape, dtype) for shape, dtype in outs),
        grid_spec=pltpu.PrefetchScalarGridSpec(
            num_scalar_prefetch=1,
            grid=(1,),
            in_specs=[whole_block(a.shape) for a in args[1:]],
            out_specs=tuple(whole_block(shape) for shape, _ in outs),
            scratch_shapes=scratch,
        ),
        compiler_params=pltpu.CompilerParams(vmem_limit_bytes=VMEM),
        cost_estimate=pl.CostEstimate(
            flops=flops, bytes_accessed=4 * sum(a.size for a in args), transcendentals=0
        ),
        name=name,
    )(*args)


def branch_back(ci, back, slot, dy, middle, gain, w, attT, early, norm_row, ctx):
    rows = dy.shape[0]
    mine = D // ctx
    outs = (
        ((rows, D), f32),
        ((ctx, HEADS // ctx, HD, rows), bf16),
        ((ctx // 2, mine, D), f32),
        ((ctx // 2 * mine + 2 * early.shape[0], D), bf16),
        (early.shape, f32),
    )
    return one_step(
        functools.partial(branch_kernel, norm_row),
        "branch_back",
        outs,
        (ci, back, slot, dy, middle, gain, w, attT, early),
        [pltpu.VMEM((D, D), f32)],
        2 * rows * D * (back.shape[0] + 2 * D),
    )


def go_kernel(me_ref, keep_ref, got_ref, small_ref, own_ref, send_ref, sum_ref, acc):
    nx, w, _ = keep_ref.shape
    for x in range(nx):
        acc[x] = keep_ref[x] + got_ref[x * w : (x + 1) * w].astype(f32)
    small = small_ref[...] + sum_halves(got_ref[nx * w :])
    sum_ref[...] = small
    own_ref[...] = acc[me_ref[0]]
    send_ref[:w] = acc[1 - me_ref[0]].astype(bf16)
    send_ref[w:] = halves_of(small)


def go_step(xi, keep, got, small):
    w = keep.shape[1]
    outs = (((w, D), f32), ((w + 2 * small.shape[0], D), bf16), (small.shape, f32))
    return one_step(go_kernel, "go_step", outs, (xi, keep, got, small), [pltpu.VMEM(keep.shape, f32)], 0)


def weight_rows_kernel(half_ref, dT_ref, normed_ref, go_ref, got_ref, early_ref, keep_ref, send_ref, small_ref, acc):
    n = dT_ref.shape[0]
    w = go_ref.shape[0]
    half = keep_ref.shape[0]
    acc[:n] = dg(dT_ref[...], normed_ref[...], 1, 0)
    acc[n:] = go_ref[...] + got_ref[:w].astype(f32)
    small = early_ref[...] + sum_halves(got_ref[w:])
    small_ref[...] = small
    a = pl.multiple_of(half_ref[0] * half, half)
    b = pl.multiple_of((1 - half_ref[0]) * half, half)
    keep_ref[...] = acc[pl.ds(a, half)]
    send_ref[:half] = acc[pl.ds(b, half)].astype(bf16)
    send_ref[half:] = halves_of(small)


def weight_rows(half, dT, normed, go, got, small):
    rows = dT.shape[0] + go.shape[0]
    outs = (((rows // 2, D), f32), ((rows // 2 + 2 * small.shape[0], D), bf16), (small.shape, f32))
    return one_step(
        weight_rows_kernel,
        "weight_rows",
        outs,
        (half, dT, normed, go, got, small),
        [pltpu.VMEM((rows, D), f32)],
        2 * dT.size * D,
    )


def share_kernel(me_ref, half_ref, got_ref, early_ref, own_ref, *refs):
    dp = len(refs) - 1
    sends, small_ref, acc = refs[: dp - 1], refs[dp - 1], refs[dp]
    half = half_ref.shape[0]
    w = half // dp
    acc[...] = half_ref[...] + got_ref[:half].astype(f32)
    small = early_ref[...] + sum_halves(got_ref[half:])
    small_ref[...] = small

    def share(step):
        return acc[pl.ds(pl.multiple_of(lax.rem(me_ref[0] + step, dp) * w, w), w)]

    own_ref[...] = share(0)
    for step in range(1, dp):
        sends[step - 1][:w] = share(step).astype(bf16)
        sends[step - 1][w:] = halves_of(small)


def share_step(zi, half, got, small, dp):
    w = half.shape[0] // dp
    outs = (((w, D), f32),) + (((w + 2 * small.shape[0], D), bf16),) * (dp - 1) + ((small.shape, f32),)
    return one_step(
        functools.partial(share_kernel),
        "share_step",
        outs,
        (zi, half, got, small),
        [pltpu.VMEM(half.shape, f32)],
        0,
    )


NEAR = ((0, 0, 0), (0, 1, 0), (1, 0, 0), (1, 1, 0))
FAR = ((0, 0, 0), (0, 1, 0), (0, 1, 2), (1, 0, 0), (1, 1, 0), (1, 1, 2))


def finish_kernel(dp, side, me_ref, *refs):
    layout = FAR if side else NEAR
    n = len(layout)
    pieces, weights, scale_ref, before_ref = refs[:n], refs[n : n + 3], refs[n + 3], refs[n + 4]
    outs, row_ref = refs[-11:-7], refs[-7]
    got, wide, held, in_sem, out_sem, w_sem = refs[-6:]
    mine = D // 4
    rows = 2 * mine // dp
    copies = []
    for k, (core, over, begin) in enumerate(layout):
        first = (over ^ me_ref[1]) * (2 * mine) + (core ^ me_ref[2]) * mine
        for i in range(pieces[k].shape[0] // rows):
            row = lax.rem(me_ref[0] + dp - begin - i, dp) * rows
            copy = pltpu.make_async_copy(
                pieces[k].at[pl.ds(i * rows, rows)],
                got.at[lax.div(row, mine), pl.ds(pl.multiple_of(first + lax.rem(row, mine), rows), rows)],
                in_sem.at[k, i],
            )
            copy.start()
            copies.append(copy)

    def put(pair):
        loads = [pltpu.make_async_copy(weights[p], held.at[k], w_sem.at[k]) for k, p in enumerate(pair) if p < 3]
        for copy in loads:
            copy.start()
        for copy in copies + loads:
            copy.wait()
        total = jnp.zeros((D, 1), f32)
        backs = []
        for k in (1, 0):
            if pair[k] < 3:
                g = got[k].T.astype(f32)
                total = total + jnp.sum(g * held[k].astype(f32), axis=1, keepdims=True)
            else:
                g = got[k].astype(f32)
            wide[k] = g
            back = pltpu.make_async_copy(wide.at[k], outs[pair[k]], out_sem.at[k])
            back.start()
            backs.append(back)
        row = jnp.broadcast_to(total, (D, 128)).T[:1]
        row_ref[...] = ((before_ref[...] + row) / scale_ref[...])[0] if side else row
        for back in backs:
            back.wait()

    y = lax.rem(me_ref[3] + side, 2)

    @pl.when(y == 0)
    def _():
        put((0, 1))

    @pl.when(y == 1)
    def _():
        put((2, 3))


def finish(me, pieces, weights, scale, side, so_far, dp):
    whole = jax.ShapeDtypeStruct((D, D), f32)
    anywhere = pl.BlockSpec(memory_space=pl.ANY)
    row = pl.BlockSpec((1, D), lambda i, p: (0, 0))
    args = [*pieces, *weights, scale, so_far[4] if side else scale]
    specs = [anywhere] * (len(args) - 2) + [row, row]
    alias = {}
    if side:
        alias = {1 + len(args) + p: p for p in range(4)}
        args += list(so_far[:4])
        specs += [anywhere] * 4
    return pl.pallas_call(
        functools.partial(finish_kernel, dp, side),
        out_shape=(whole,) * 4 + (jax.ShapeDtypeStruct((D,) if side else (1, D), f32),),
        grid_spec=pltpu.PrefetchScalarGridSpec(
            num_scalar_prefetch=1,
            grid=(1,),
            in_specs=specs,
            out_specs=(anywhere,) * 4 + (pl.BlockSpec((D,), lambda i, p: (0,)) if side else row,),
            scratch_shapes=[
                pltpu.VMEM((2, D, D), bf16),
                pltpu.VMEM((2, D, D), f32),
                pltpu.VMEM((2, D, D), bf16),
                pltpu.SemaphoreType.DMA((len(pieces), dp)),
                pltpu.SemaphoreType.DMA((2,)),
                pltpu.SemaphoreType.DMA((2,)),
            ],
        ),
        input_output_aliases=alias,
        compiler_params=pltpu.CompilerParams(vmem_limit_bytes=VMEM),
        cost_estimate=pl.CostEstimate(flops=4 * D * D, bytes_accessed=16 * D * D, transcendentals=0),
        name=f"finish{side}",
    )(me, *args)


def swap(v, axis):
    return lax.ppermute(v, axis, [(0, 1), (1, 0)])


def shift(v, axis, step):
    n = lax.axis_size(axis)
    return lax.ppermute(v, axis, [(i, (i + step) % n) for i in range(n)])


def at(v, index):
    return lax.dynamic_index_in_dim(v, index, 0, keepdims=False)


def one(v):
    v = v.astype(f32)
    n = v.shape[0] // 2
    return v[:n] + v[n:]


def add_pair(v):
    return v + (swap(v, "expert") if lax.axis_size("expert") == 2 else lax.psum(v, "expert") - v)


def add_shifts(v):
    out = v
    for s in range(1, lax.axis_size("dp")):
        out = out + shift(v, "dp", s)
    return out


def index(i):
    return i.astype(jnp.int32).reshape(1)


def tie(*arrays):
    return lax.optimization_barrier(arrays)


def normal_form(v):
    centred = v - jnp.mean(v, axis=-1, keepdims=True)
    rstd = lax.rsqrt(jnp.mean(centred * centred, axis=-1, keepdims=True) + norm_eps)
    return centred * rstd, rstd


def norm_back(dn, xh, rstd):
    return rstd * (dn - jnp.mean(dn, axis=-1, keepdims=True) - xh * jnp.mean(dn * xh, axis=-1, keepdims=True))


def per_device(
    tokens,
    cotangent,
    routes,
    norm1_gain,
    w_query,
    w_key,
    w_value,
    w_output,
    norm2_gain,
    w_router,
    w_in,
    w_out,
):
    rows = tokens.shape[1]
    nx, owners, dp = lax.axis_size("x"), lax.axis_size("expert"), lax.axis_size("dp")
    xi, ci, ei = lax.axis_index("x"), lax.axis_index("core"), lax.axis_index("expert")
    ctx = 2 * nx
    ctx_i = xi * 2 + ci
    length = ctx * rows
    experts = w_router.shape[1]
    cap = 2 * rows // experts
    mine = D // ctx
    heads = mine // HD
    expert_id = ei * nx + xi
    pick = jnp.stack([xi, ci, expert_id]).astype(jnp.int32)

    tok = tokens.reshape(rows, D)
    flat = tok.astype(f32)
    other = swap(tok, "x")
    near = swap(tok, "core")

    route = routes.reshape(rows)
    hot = (route[:, None] == jnp.arange(128, dtype=jnp.int32)[None, :]).astype(f32)
    lower = jnp.arange(rows)[:, None] >= jnp.arange(rows)[None, :]
    before = dg(lower.astype(bf16), hot.astype(bf16), 1, 0)
    rank = (jnp.sum(before * hot, axis=1) - 1.0).astype(jnp.int32)
    slot = ((route % nx) * owners + route // nx) * cap + rank
    spread = (jnp.arange(experts * cap, dtype=jnp.int32)[:, None] == slot[None, :]).astype(bf16)

    def pack(v):
        return dg(spread, v, 1, 0).astype(bf16).reshape(nx * owners, cap, D)

    def trade(v):
        v = lax.all_to_all(v.reshape(nx * owners, cap, D), ("x", "expert"), split_axis=0, concat_axis=0, tiled=True)
        return v.reshape(-1, D)

    def turn(v):
        return lax.all_to_all(v, ("x", "core"), split_axis=0, concat_axis=0, tiled=True)

    def cut(w):
        return lax.dynamic_slice(w, (0, ctx_i * mine), (D, mine))

    w_own = jnp.concatenate([cut(w_query), cut(w_key), cut(w_value)], axis=1)
    gain1 = norm1_gain.reshape(1, D)
    dy_low = cotangent.reshape(rows, D)
    dy = dy_low.astype(f32)
    wr = lax.dynamic_slice(w_router, (0, expert_id), (D, 1)).astype(f32).reshape(1, D)
    counts = jnp.sum(hot, axis=0, keepdims=True)
    counts = counts + swap(counts, "core")
    counts = add_pair(counts)
    so_far = project([ctx_i], [tok], gain1, w_own, ctx, None)
    counts, dy_packed, *so_far = tie(counts, pack(dy_low), *so_far)
    so_far = project([ctx_i ^ 1], [near], gain1, w_own, ctx, so_far)
    other, dy_packed, *so_far = tie(other, dy_packed, *so_far)
    far = swap(other, "core")
    dy_rows = trade(dy_packed)
    normed_all, qkvT, kv = project([ctx_i ^ 2, ctx_i ^ 3], [other, far], gain1, w_own, ctx, so_far)
    oT, osend, lse = attend(qkvT, kv, ctx)
    osend, dy_rows, counts = tie(osend, dy_rows, counts)
    attT = turn(osend)
    counts = add_shifts(counts)
    attT, counts = tie(attT, counts)
    counts = counts + swap(counts, "x")
    attT = attT.reshape(D, rows)
    mean_load = rows * ctx * dp * owners / experts
    gain2 = norm2_gain.reshape(1, D)
    middle, second, packed = middle_step(attT, tok, w_output, gain2, slot[None], nx * owners, cap)
    gating = jax.nn.sigmoid(jnp.sum(hot[:, :experts] * dg(second, w_router, 1, 0), axis=1))

    up = expert_up(pick, dy_rows, w_out)
    sig = jnp.pad(jnp.sum(hot[:, :experts] * gating[:, None], axis=0), (0, D - experts))
    counts, packed = tie(counts, packed)
    x_rows = trade(packed)
    x_rows, gating, sig, slot, gain2 = tie(x_rows, gating, sig, slot[None], gain2)
    active, grad_hidden, back_rows, router_row, gate = expert_mid(pick, x_rows, up, w_in, wr, counts, mean_load)
    returned = trade(back_rows)
    keep, send = expert_grads(pick, x_rows, dy_rows, gate, active, grad_hidden, dp, nx)
    produced = expert_out(pick, tie(active, keep)[0], w_out)
    returned, keep, send, produced = tie(returned, keep, send, produced)
    taken = swap(send, "core")
    zi = lax.axis_index("dp")

    def chunk(i):
        return at(keep, (i + dp) % dp).astype(f32) + at(taken, (i + dp) % dp).astype(f32)

    def ring(moving, step):
        return (shift(moving, "dp", 1).astype(f32) + chunk(zi - 2 - step)).astype(bf16)

    def side(v, x):
        return lax.dynamic_index_in_dim(v, x, 1, keepdims=False)

    router_rows = (jnp.arange(experts) == expert_id).astype(f32)[:, None] * router_row
    small = jnp.concatenate([router_rows, jnp.zeros((1, D), f32), sig[None]], axis=0)
    small = jnp.pad(small, ((0, -small.shape[0] % 8), (0, 0)))
    grad_middle, heads_grad, go, go_send, small = branch_back(
        index(ci), returned, slot, dy_low, middle, gain2, w_output, attT, small, experts, ctx
    )
    do = turn(heads_grad)

    moving = ring(chunk(zi - 1).astype(bf16), 0)
    go_got = swap(go_send, "core")
    go, go_send, small = go_step(index(xi), go, go_got, small)
    do, go_send = tie(do, go_send)
    go_got = swap(go_send, "x")

    so_far = attend_back(qkvT, kv, do, 0, oT, lse, 0, None)
    produced, go_got, *so_far = tie(produced, go_got, *so_far)
    went_back = trade(produced)
    so_far = attend_back(qkvT, kv, do, 1, oT, lse, 1, so_far)
    moving, *so_far = tie(moving, *so_far)
    moving = ring(moving, 1)
    for h in range(2, heads):
        so_far = attend_back(qkvT, kv, do, h, oT, lse, h, so_far)
    went_back, dT, dsend = tie(went_back, *so_far)
    output = (middle + gating[:, None] * dg(spread, went_back, 0, 0)).astype(bf16)

    ei2 = ei if owners == 2 else jnp.zeros_like(ei)
    half, send, small = weight_rows(index(ei2), dT.reshape(3 * mine, length), normed_all, go, go_got, small)
    dsend, send = tie(dsend, send)
    got = turn(dsend)
    if owners == 2:
        gift = swap(send, "expert")
        gift, moving = tie(gift, moving)
        halves = [(half, gift)]
    else:
        cut_at = half.shape[0]
        small = lax.psum(small, "expert")
        nothing = jnp.zeros_like(send)
        halves = [(lax.psum(half, "expert"), nothing), (lax.psum(send[:cut_at].astype(f32), "expert"), nothing)]
    pieces = []
    for part, gift in halves:
        share, *gifts, more = share_step(index(zi), part, gift, small, dp)
        gifts = [shift(gift, "dp", step + 1) for step, gift in enumerate(gifts)]
        for gift in gifts:
            more = more + one(gift[share.shape[0] :])
            share = share + gift[: share.shape[0]].astype(f32)
        share = share.astype(bf16)
        pieces.append(jnp.concatenate([share] + [shift(share, "dp", step) for step in range(1, dp)], axis=0))
    small = more
    output, keep, taken = tie(output, keep, taken)
    crossed = swap(side(chunk(zi), 1 - xi).astype(bf16), "x")
    for step in range(2, dp - 2):
        moving = ring(moving, step)
    moving, crossed, *pieces = tie(moving, crossed, *pieces)
    own = shift(side(moving, xi), "dp", 1)
    route_on = [(z * nx + x, (z + 1) % dp * nx + 1 - x) for z in range(dp) for x in range(nx)]
    theirs = side(moving, 1 - xi)

    grad_normed = 0.0
    for p, w in enumerate((w_query, w_key, w_value)):
        grad_normed = grad_normed + dg(got[:, p].reshape(D, rows), w, 0, 1)
    xh1, rstd1 = normal_form(flat)
    grad_tokens = grad_middle + norm_back(grad_normed * norm1_gain, xh1, rstd1)

    if owners == 2:
        pieces.append(swap(pieces[0], "expert"))
    beyond = swap(pieces[0], "x")
    me = jnp.stack([zi, xi, ci, ei2]).astype(jnp.int32)
    projections = (w_query, w_key, w_value)
    near_pieces = [pieces[0], beyond]
    near_pieces += [swap(piece, "core") for piece in near_pieces]
    pieces[1], beyond, theirs, grad_tokens = tie(pieces[1], beyond, theirs, grad_tokens)
    theirs, *near_pieces = tie(theirs, *near_pieces)
    moved = lax.ppermute(theirs, ("dp", "x"), route_on)
    rest = pieces[0].shape[0] // 2
    if owners == 2:
        corner = [swap(pieces[1][:rest], "x"), swap(beyond[rest:], "expert")]
    else:
        corner = [swap(pieces[1][:rest], "x"), swap(pieces[1][rest:], "x")]
    placed = finish(me, near_pieces, projections, gain1, 0, None, dp)
    own, *corner = tie(own, *corner, *placed)
    corner, placed = corner[:2], corner[2:]
    far_pieces = [pieces[1], *corner]
    far_pieces += [swap(piece, "core") for piece in far_pieces]
    *grads, grad_norm1 = finish(me, far_pieces, projections, gain1, 1, placed, dp)

    own = own.astype(f32) + side(chunk(zi), xi)
    moved = moved.astype(f32) + crossed.astype(f32)
    first, latter = jnp.where(xi == 0, own, moved), jnp.where(xi == 0, moved, own)
    both = jnp.stack([first, latter], axis=1)
    grad_in = jnp.swapaxes(both[0], 1, 2)
    grad_out = both[1]

    grad_router = jnp.transpose(small[:experts])
    grad_norm2 = small[experts]
    total_sig = small[experts + 1, :experts]
    counts = counts[0, :experts]
    balance = balance_weight * jnp.sum((counts - mean_load) / mean_load * total_sig) / mean_load

    return (
        output.reshape(1, rows, D),
        grad_tokens.reshape(1, rows, D),
        grad_norm1,
        grads[0],
        grads[1],
        grads[2],
        grads[3],
        grad_norm2,
        grad_router,
        grad_in,
        grad_out,
        balance,
    )


def solution(mesh):
    dp, ctx, owners = mesh.shape["dp"], mesh.shape["ctx"], mesh.shape["expert"]
    split = Mesh(mesh.devices.reshape(dp, ctx // 2, 2, owners), ("dp", "x", "core", "expert"))
    token = P(("dp", "expert"), ("x", "core"), None)
    return jax.shard_map(
        per_device,
        mesh=split,
        in_specs=(token, token, token, P(), P(), P(), P(), P(), P(), P(), P("expert"), P("expert")),
        out_specs=(
            token,
            token,
            P(),
            P(),
            P(),
            P(),
            P(),
            P(),
            P(),
            P("expert", None, ("dp", "x", "core")),
            P("expert", ("dp", "x", "core"), None),
            P(),
        ),
        check_vma=False,
    )
```

```python
import functools

import jax
import jax.numpy as jnp
from jax import lax
from jax.experimental import pallas as pl
from jax.experimental.pallas import tpu as pltpu
from jax.sharding import Mesh
from jax.sharding import PartitionSpec as P

D = 768
HEADS = 12
HD = 64
norm_eps = 1e-05
balance_weight = 1.0
LOG2E = 1.4426950408889634
MASKED = -1e30
GELU_A = 0.7978845608028654
GELU_B = 0.044715
VMEM = 56 * 1024 * 1024
f32 = jnp.float32
bf16 = jnp.bfloat16


def dg(a, b, ca, cb):
    return lax.dot_general(a, b, (((ca,), (cb,)), ((), ())), preferred_element_type=f32)


def project_kernel(place_ref, *refs):
    normed_ref, qkvT_ref, kv_ref = refs[-3:]
    blocks = place_ref.shape[0]
    gain_ref, w_ref = refs[blocks : blocks + 2]

    def work(tok_ref):
        x = tok_ref[...].astype(f32)
        centred = x - jnp.mean(x, axis=1, keepdims=True)
        rstd = lax.rsqrt(jnp.mean(centred * centred, axis=1, keepdims=True) + norm_eps)
        normed = (centred * rstd * gain_ref[...]).astype(bf16)
        normed_ref[...] = normed
        qkv = dg(normed, w_ref[...], 1, 0).astype(bf16)
        kv_ref[...] = qkv[:, qkv.shape[1] - kv_ref.shape[1] :]
        qkvT_ref[...] = qkv.T

    for k in range(blocks):

        @pl.when(pl.program_id(0) == k)
        def _():
            work(refs[k])


def project(places, toks, gain, w, ctx, so_far):
    rows = toks[0].shape[0]
    wide = w.shape[1]
    args = [*toks, gain, w]
    specs = [pl.BlockSpec(a.shape, lambda i, p: (0, 0)) for a in args]
    alias = {}
    if so_far is not None:
        alias = {1 + len(args) + k: k for k in range(3)}
        args += list(so_far)
        specs += [pl.BlockSpec(memory_space=pl.ANY)] * 3
    return pl.pallas_call(
        project_kernel,
        out_shape=(
            jax.ShapeDtypeStruct((ctx * rows, D), bf16),
            jax.ShapeDtypeStruct((wide, ctx * rows), bf16),
            jax.ShapeDtypeStruct((ctx * rows, 2 * wide // 3), bf16),
        ),
        grid_spec=pltpu.PrefetchScalarGridSpec(
            num_scalar_prefetch=1,
            grid=(len(toks),),
            in_specs=specs,
            out_specs=(
                pl.BlockSpec((rows, D), lambda i, p: (p[i], 0)),
                pl.BlockSpec((wide, rows), lambda i, p: (0, p[i])),
                pl.BlockSpec((rows, 2 * wide // 3), lambda i, p: (p[i], 0)),
            ),
        ),
        input_output_aliases=alias,
        compiler_params=pltpu.CompilerParams(vmem_limit_bytes=VMEM),
        cost_estimate=pl.CostEstimate(
            flops=4 * len(toks) * rows * D * wide, bytes_accessed=4 * rows * D + 8 * rows * wide, transcendentals=0
        ),
        name="project",
    )(jnp.stack(places).astype(jnp.int32), *args)


def attend_kernel(heads, blk, qT_ref, k_ref, vT_ref, oT_ref, osend_ref, lse_ref):
    length = qT_ref.shape[1]
    per = osend_ref.shape[3]
    c = (HD**-0.5) * LOG2E
    rows = lax.broadcasted_iota(jnp.int32, (blk, blk), 0)
    cols = lax.broadcasted_iota(jnp.int32, (blk, blk), 1)
    keep = rows <= cols
    for h in range(heads):
        hs = slice(h * HD, (h + 1) * HD)
        for i in range(length // blk):
            a, b = i * blk, (i + 1) * blk
            q = qT_ref[hs, a:b]
            sd = dg(k_ref[a:b, hs], q, 1, 0)
            sd = jnp.where(keep, sd, MASKED)
            m = jnp.max(sd, axis=0, keepdims=True)
            if i:
                s = dg(k_ref[:a, hs], q, 1, 0)
                m = jnp.maximum(m, jnp.max(s, axis=0, keepdims=True))
            mc = m * c
            pd = jnp.exp2(sd * c - mc)
            total = jnp.sum(pd, axis=0, keepdims=True)
            o = dg(vT_ref[hs, a:b], pd.astype(bf16), 1, 0)
            if i:
                p = jnp.exp2(s * c - mc)
                total = total + jnp.sum(p, axis=0, keepdims=True)
                o = o + dg(vT_ref[hs, :a], p.astype(bf16), 1, 0)
            o = o / total
            oT_ref[hs, a:b] = o
            d, off = a // per, a % per
            osend_ref[d, h, :, off : off + blk] = o.astype(bf16)
            lse_ref[h, :, a:b] = mc + jnp.log2(total)


def attend(qkvT, kv, dests):
    length = kv.shape[0]
    heads = qkvT.shape[0] // (3 * HD)
    wide = heads * HD
    per = length // dests
    return pl.pallas_call(
        functools.partial(attend_kernel, heads, per),
        out_shape=(
            jax.ShapeDtypeStruct((wide, length), f32),
            jax.ShapeDtypeStruct((dests, heads, HD, per), bf16),
            jax.ShapeDtypeStruct((heads, 1, length), f32),
        ),
        grid=(1,),
        in_specs=[
            pl.BlockSpec((wide, length), lambda i: (0, 0)),
            pl.BlockSpec(kv.shape, lambda i: (0, 0)),
            pl.BlockSpec((wide, length), lambda i: (2, 0)),
        ],
        out_specs=(
            pl.BlockSpec((wide, length), lambda i: (0, 0)),
            pl.BlockSpec((dests, heads, HD, per), lambda i: (0, 0, 0, 0)),
            pl.BlockSpec((heads, 1, length), lambda i: (0, 0, 0)),
        ),
        compiler_params=pltpu.CompilerParams(vmem_limit_bytes=VMEM),
        cost_estimate=pl.CostEstimate(
            flops=8 * heads * length * length * HD,
            bytes_accessed=length * wide * 14,
            transcendentals=heads * length * length // 2,
        ),
        name="attend",
    )(qkvT, kv, qkvT)


def attend_back_kernel(lk, lv, blk, *refs):
    qT_ref, k_ref, kT_ref, v_ref, do_ref, oT_ref, lse_ref = refs[:7]
    dT_ref, dsend_ref, dk_acc, dv_acc = refs[-4:]
    length = qT_ref.shape[1]
    per = do_ref.shape[3]
    sc = HD**-0.5
    c = sc * LOG2E
    rows = lax.broadcasted_iota(jnp.int32, (blk, blk), 0)
    cols = lax.broadcasted_iota(jnp.int32, (blk, blk), 1)
    keep = rows <= cols
    n = length // blk
    for i in reversed(range(n)):
        x0, x1 = i * blk, (i + 1) * blk
        d, off = x0 // per, x0 % per
        q = qT_ref[:, x0:x1]
        do = do_ref[d, 0, :, off : off + blk]
        lse = lse_ref[0, :, x0:x1]
        delta = jnp.sum(do.astype(f32) * oT_ref[:, x0:x1], axis=0, keepdims=True)
        dq = None
        for a, b, diag in ([(0, x0, False)] if i else []) + [(x0, x1, True)]:
            s = dg(k_ref[a:b, lk : lk + HD], q, 1, 0)
            p = jnp.exp2(s * c - lse)
            if diag:
                p = jnp.where(keep, p, 0.0)
            dp = dg(v_ref[a:b, lv : lv + HD], do, 1, 0)
            ds = (p * (dp - delta)).astype(bf16)
            dvn = dg(do, p.astype(bf16), 1, 1)
            dkn = dg(q, ds, 1, 1)
            if i == n - 1:
                dv_acc[:, a:b] = dvn
                dk_acc[:, a:b] = dkn
            else:
                dv_acc[:, a:b] += dvn
                dk_acc[:, a:b] += dkn
            t = dg(kT_ref[:, a:b], ds, 1, 0)
            dq = t if dq is None else dq + t
        dq = (dq * sc).astype(bf16)
        dT_ref[0, :, x0:x1] = dq
        dsend_ref[d, 0, :, off : off + blk] = dq
    for d in range(dsend_ref.shape[0]):
        at_d = slice(d * per, (d + 1) * per)
        dk = (dk_acc[:, at_d] * sc).astype(bf16)
        dv = dv_acc[:, at_d].astype(bf16)
        dT_ref[1, :, at_d] = dk
        dT_ref[2, :, at_d] = dv
        dsend_ref[d, 1] = dk
        dsend_ref[d, 2] = dv


def attend_back(qkvT, kv, do, slot, oT, lse, h, so_far):
    length = kv.shape[0]
    n = qkvT.shape[0] // (3 * HD)
    dests, _, _, per = do.shape
    hv = n + h
    blk = min(256, per)
    args = [qkvT, kv, qkvT, kv, do, oT, lse]
    specs = [
        pl.BlockSpec((HD, length), lambda i: (h, 0)),
        pl.BlockSpec((length, 2 * HD), lambda i: (0, h // 2)),
        pl.BlockSpec((HD, length), lambda i: (n + h, 0)),
        pl.BlockSpec((length, 2 * HD), lambda i: (0, hv // 2)),
        pl.BlockSpec((dests, 1, HD, per), lambda i: (0, slot, 0, 0)),
        pl.BlockSpec((HD, length), lambda i: (h, 0)),
        pl.BlockSpec((1, 1, length), lambda i: (h, 0, 0)),
    ]
    alias = {}
    if so_far is not None:
        alias = {len(args): 0, len(args) + 1: 1}
        args += list(so_far)
        specs += [pl.BlockSpec(memory_space=pl.ANY)] * 2
    return pl.pallas_call(
        functools.partial(attend_back_kernel, (h % 2) * HD, (hv % 2) * HD, blk),
        out_shape=(
            jax.ShapeDtypeStruct((3, n * HD, length), bf16),
            jax.ShapeDtypeStruct((dests, 3, n * HD, per), bf16),
        ),
        grid=(1,),
        in_specs=specs,
        out_specs=(
            pl.BlockSpec((3, HD, length), lambda i: (0, h, 0)),
            pl.BlockSpec((dests, 3, HD, per), lambda i: (0, 0, h, 0)),
        ),
        scratch_shapes=[pltpu.VMEM((HD, length), f32)] * 2,
        input_output_aliases=alias,
        compiler_params=pltpu.CompilerParams(vmem_limit_bytes=VMEM),
        cost_estimate=pl.CostEstimate(
            flops=20 * length * length * HD, bytes_accessed=length * HD * 24, transcendentals=length * length // 2
        ),
        name=f"attend_back_head{h}",
    )(*args)


def middle_kernel(me_ref, att_ref, tok_ref, w_ref, gain_ref, slot_ref, middle_ref, second_ref, packed_ref):
    v = tok_ref[...].astype(f32) + dg(att_ref[...], w_ref[...], 0, 0)
    middle_ref[...] = v
    centred = v - jnp.mean(v, axis=1, keepdims=True)
    rstd = lax.rsqrt(jnp.mean(centred * centred, axis=1, keepdims=True) + norm_eps)
    second = (centred * rstd * gain_ref[...]).astype(bf16)
    second_ref[...] = second
    spread = one_hot_slots(slot_ref[...], packed_ref.shape[0] * packed_ref.shape[1])
    packed_ref[...] = dg(spread, second, 1, 0).astype(bf16).reshape(packed_ref.shape)


def middle_step(attT, tok, w, gain, slot, sources, cap):
    rows = tok.shape[0]
    outs = (((rows, D), f32), ((rows, D), bf16), ((sources, cap, D), bf16))
    return one_step(
        middle_kernel,
        "middle_step",
        outs,
        (jnp.zeros((1,), jnp.int32), attT, tok, w, gain, slot),
        [],
        2 * rows * D * (D + sources * cap),
    )


def up_kernel(pick_ref, dy_ref, wo_ref, u_ref):
    u_ref[...] = dg(dy_ref[...], wo_ref[0], 1, 1).astype(bf16)


def expert_up(pick, dy, w_out, fc=768):
    rows = dy.shape[0]
    ff = w_out.shape[1]
    return pl.pallas_call(
        up_kernel,
        out_shape=jax.ShapeDtypeStruct((rows, ff), bf16),
        grid_spec=pltpu.PrefetchScalarGridSpec(
            num_scalar_prefetch=1,
            grid=(ff // fc,),
            in_specs=[
                pl.BlockSpec((rows, D), lambda f, p: (0, 0)),
                pl.BlockSpec((1, fc, D), lambda f, p: (p[0], f, 0)),
            ],
            out_specs=pl.BlockSpec((rows, fc), lambda f, p: (0, f)),
        ),
        compiler_params=pltpu.CompilerParams(vmem_limit_bytes=VMEM),
        cost_estimate=pl.CostEstimate(
            flops=2 * rows * D * ff, bytes_accessed=2 * (rows * D + ff * D + rows * ff), transcendentals=0
        ),
        name="expert_up",
    )(pick, dy, w_out)


def mid_kernel(
    mean, pick_ref, x_ref, u_ref, wi_ref, wr_ref, count_ref, act_ref, gh_ref, rows_ref, router_ref, gate_ref, acc, gg, gate
):
    f = pl.program_id(0)
    n = pl.num_programs(0)

    @pl.when(f == 0)
    def _():
        logit = jnp.sum(x_ref[...].astype(f32) * wr_ref[...], axis=1, keepdims=True)
        gate[...] = jnp.broadcast_to(jax.nn.sigmoid(logit), gate.shape)
        acc[...] = jnp.zeros_like(acc)
        gg[...] = jnp.zeros_like(gg)

    step = 256
    for r in range(0, x_ref.shape[0], step):
        rs = slice(r, r + step)
        for c in range(0, wi_ref.shape[2], step):
            cs = slice(c, c + step)
            h = dg(x_ref[rs], wi_ref[0, :, cs], 1, 0)
            h2 = h * h
            t = jnp.tanh(h * (GELU_A + (GELU_A * GELU_B) * h2))
            hp = 0.5 + 0.5 * t
            dgelu = hp + (h * (hp - hp * hp)) * (2.0 * GELU_A + (6.0 * GELU_A * GELU_B) * h2)
            u = u_ref[rs, cs].astype(f32)
            active = h * hp
            act_ref[rs, cs] = active.astype(bf16)
            au = active * u
            lanes = au[:, :128]
            for j in range(128, step, 128):
                lanes = lanes + au[:, j : j + 128]
            gg[rs] += lanes
            gh = (gate[rs, :1] * (u * dgelu)).astype(bf16)
            gh_ref[rs, cs] = gh
            acc[rs] += dg(gh, wi_ref[0, :, cs], 1, 1)

    @pl.when(f == n - 1)
    def _():
        g = gate[:, :1]
        got = jnp.sum(gg[...], axis=1, keepdims=True)
        lane = lax.broadcasted_iota(jnp.int32, count_ref.shape, 1)
        count = jnp.sum(jnp.where(lane == pick_ref[2], count_ref[...], 0.0), axis=1, keepdims=True)
        load = balance_weight * (count - mean) / (mean * mean)
        sel = (g * (1.0 - g) * (got + load)).astype(bf16).astype(f32)
        rows_ref[...] = (acc[...] + sel * wr_ref[...]).astype(bf16)
        router_ref[...] = jnp.sum(x_ref[...].astype(f32) * sel, axis=0, keepdims=True)
        gate_ref[...] = gate[...]


def expert_mid(pick, x, u, w_in, wr, counts, mean, fc=768):
    rows = x.shape[0]
    ff = w_in.shape[2]

    def full(s):
        return pl.BlockSpec(s, lambda f, p: (0, 0))

    wide = pl.BlockSpec((rows, fc), lambda f, p: (0, f))
    return pl.pallas_call(
        functools.partial(mid_kernel, mean),
        out_shape=(
            jax.ShapeDtypeStruct((rows, ff), bf16),
            jax.ShapeDtypeStruct((rows, ff), bf16),
            jax.ShapeDtypeStruct((rows, D), bf16),
            jax.ShapeDtypeStruct((1, D), f32),
            jax.ShapeDtypeStruct((rows, 128), f32),
        ),
        grid_spec=pltpu.PrefetchScalarGridSpec(
            num_scalar_prefetch=1,
            grid=(ff // fc,),
            in_specs=[
                full((rows, D)),
                wide,
                pl.BlockSpec((1, D, fc), lambda f, p: (p[0], 0, f)),
                full((1, D)),
                full((1, 128)),
            ],
            out_specs=(wide, wide, full((rows, D)), full((1, D)), full((rows, 128))),
            scratch_shapes=[
                pltpu.VMEM((rows, D), f32),
                pltpu.VMEM((rows, 128), f32),
                pltpu.VMEM((rows, 128), f32),
            ],
        ),
        compiler_params=pltpu.CompilerParams(vmem_limit_bytes=VMEM),
        cost_estimate=pl.CostEstimate(
            flops=4 * rows * D * ff,
            bytes_accessed=2 * (3 * rows * D + ff * D + 3 * rows * ff),
            transcendentals=rows * ff,
        ),
        name="expert_mid",
    )(pick, x, u, w_in, wr, counts)


def grads_kernel(
    pick_ref, x_ref, dy_ref, gate_ref, act_ref, gh_ref, wo_ref, keep_ref, send_ref, prod_ref, acc, go, gi, gexp
):
    f = pl.program_id(0)
    n = pl.num_programs(0)

    @pl.when(f == 0)
    def _():
        gexp[...] = (dy_ref[...].astype(f32) * gate_ref[:, :1]).astype(bf16)

    go[...] = dg(act_ref[...], gexp[...], 0, 0).astype(bf16)
    gi[...] = dg(gh_ref[...], x_ref[...], 0, 0).astype(bf16)
    part = dg(act_ref[...], wo_ref[0], 1, 0)

    @pl.when(f == 0)
    def _():
        acc[...] = part

    @pl.when(f > 0)
    def _():
        acc[...] += part

    w = keep_ref.shape[3]
    me = pick_ref[1]
    for xx in range(keep_ref.shape[2]):
        a = pl.multiple_of((2 * xx + me) * w, w)
        b = pl.multiple_of((2 * xx + 1 - me) * w, w)
        keep_ref[0, 0, xx] = gi[pl.ds(a, w)]
        keep_ref[0, 1, xx] = go[pl.ds(a, w)]
        send_ref[0, 0, xx] = gi[pl.ds(b, w)]
        send_ref[0, 1, xx] = go[pl.ds(b, w)]

    @pl.when(f == n - 1)
    def _():
        prod_ref[...] = acc[...].astype(bf16)


def expert_grads(pick, x, dy, gate, act, gh, w_out, dp, nx):
    rows = x.shape[0]
    ff = w_out.shape[1]
    fc = ff // dp
    w = fc // (2 * nx)

    def full(s):
        return pl.BlockSpec(s, lambda f, p: (0, 0))

    wide = pl.BlockSpec((rows, fc), lambda f, p: (0, f))
    part = jax.ShapeDtypeStruct((dp, 2, nx, w, D), bf16)
    part_spec = pl.BlockSpec((1, 2, nx, w, D), lambda f, p: (f, 0, 0, 0, 0))
    return pl.pallas_call(
        grads_kernel,
        out_shape=(part, part, jax.ShapeDtypeStruct((rows, D), bf16)),
        grid_spec=pltpu.PrefetchScalarGridSpec(
            num_scalar_prefetch=1,
            grid=(dp,),
            in_specs=[
                full((rows, D)),
                full((rows, D)),
                full((rows, 128)),
                wide,
                wide,
                pl.BlockSpec((1, fc, D), lambda f, p: (p[0], f, 0)),
            ],
            out_specs=(part_spec, part_spec, full((rows, D))),
            scratch_shapes=[
                pltpu.VMEM((rows, D), f32),
                pltpu.VMEM((fc, D), bf16),
                pltpu.VMEM((fc, D), bf16),
                pltpu.VMEM((rows, D), bf16),
            ],
        ),
        compiler_params=pltpu.CompilerParams(vmem_limit_bytes=VMEM),
        cost_estimate=pl.CostEstimate(
            flops=6 * rows * D * ff,
            bytes_accessed=2 * (3 * rows * D + 3 * ff * D + 2 * rows * ff),
            transcendentals=0,
        ),
        name="expert_grads",
    )(pick, x, dy, gate, act, gh, w_out)


def one_hot_slots(slot, slots):
    return (lax.broadcasted_iota(jnp.int32, (slots, slot.shape[1]), 0) == slot).astype(f32).astype(bf16)


def halves_of(v):
    high = v.astype(bf16)
    return jnp.concatenate([high, (v - high.astype(f32)).astype(bf16)], axis=0)


def sum_halves(v):
    v = v.astype(f32)
    n = v.shape[0] // 2
    return v[:n] + v[n:]


def branch_kernel(
    norm_row,
    me_ref,
    back_ref,
    slot_ref,
    dy_ref,
    middle_ref,
    gain_ref,
    w_ref,
    att_ref,
    early_ref,
    grad_ref,
    heads_ref,
    keep_ref,
    send_ref,
    small_ref,
    acc,
):
    g = dg(one_hot_slots(slot_ref[...], back_ref.shape[0]), back_ref[...], 0, 0)
    v = middle_ref[...]
    centred = v - jnp.mean(v, axis=1, keepdims=True)
    rstd = lax.rsqrt(jnp.mean(centred * centred, axis=1, keepdims=True) + norm_eps)
    xh = centred * rstd
    dn = g * gain_ref[...]
    grad = rstd * (dn - jnp.mean(dn, axis=1, keepdims=True) - xh * jnp.mean(dn * xh, axis=1, keepdims=True))
    grad = dy_ref[...].astype(f32) + grad
    grad_ref[...] = grad
    low = grad.astype(bf16)
    heads_ref[...] = dg(w_ref[...], low, 1, 1).astype(bf16).reshape(heads_ref.shape)
    row = lax.broadcasted_iota(jnp.int32, small_ref.shape, 0)
    small = early_ref[...] + jnp.where(row == norm_row, jnp.sum(g * xh, axis=0, keepdims=True), 0.0)
    small_ref[...] = small
    acc[...] = dg(att_ref[...], low, 1, 0)
    nx, w, _ = keep_ref.shape
    for x in range(nx):
        keep_ref[x] = acc[pl.ds(pl.multiple_of((2 * x + me_ref[0]) * w, w), w)]
        send_ref[x * w : (x + 1) * w] = acc[pl.ds(pl.multiple_of((2 * x + 1 - me_ref[0]) * w, w), w)].astype(bf16)
    send_ref[nx * w :] = halves_of(small)


def whole_block(shape):
    return pl.BlockSpec(shape, lambda i, p: (0,) * len(shape))


def one_step(kernel, name, outs, args, scratch, flops):
    return pl.pallas_call(
        kernel,
        out_shape=tuple(jax.ShapeDtypeStruct(shape, dtype) for shape, dtype in outs),
        grid_spec=pltpu.PrefetchScalarGridSpec(
            num_scalar_prefetch=1,
            grid=(1,),
            in_specs=[whole_block(a.shape) for a in args[1:]],
            out_specs=tuple(whole_block(shape) for shape, _ in outs),
            scratch_shapes=scratch,
        ),
        compiler_params=pltpu.CompilerParams(vmem_limit_bytes=VMEM),
        cost_estimate=pl.CostEstimate(
            flops=flops, bytes_accessed=4 * sum(a.size for a in args), transcendentals=0
        ),
        name=name,
    )(*args)


def branch_back(ci, back, slot, dy, middle, gain, w, attT, early, norm_row, ctx):
    rows = dy.shape[0]
    mine = D // ctx
    outs = (
        ((rows, D), f32),
        ((ctx, HEADS // ctx, HD, rows), bf16),
        ((ctx // 2, mine, D), f32),
        ((ctx // 2 * mine + 2 * early.shape[0], D), bf16),
        (early.shape, f32),
    )
    return one_step(
        functools.partial(branch_kernel, norm_row),
        "branch_back",
        outs,
        (ci, back, slot, dy, middle, gain, w, attT, early),
        [pltpu.VMEM((D, D), f32)],
        2 * rows * D * (back.shape[0] + 2 * D),
    )


def go_kernel(me_ref, keep_ref, got_ref, small_ref, own_ref, send_ref, sum_ref, acc):
    nx, w, _ = keep_ref.shape
    for x in range(nx):
        acc[x] = keep_ref[x] + got_ref[x * w : (x + 1) * w].astype(f32)
    small = small_ref[...] + sum_halves(got_ref[nx * w :])
    sum_ref[...] = small
    own_ref[...] = acc[me_ref[0]]
    send_ref[:w] = acc[1 - me_ref[0]].astype(bf16)
    send_ref[w:] = halves_of(small)


def go_step(xi, keep, got, small):
    w = keep.shape[1]
    outs = (((w, D), f32), ((w + 2 * small.shape[0], D), bf16), (small.shape, f32))
    return one_step(go_kernel, "go_step", outs, (xi, keep, got, small), [pltpu.VMEM(keep.shape, f32)], 0)


def weight_rows_kernel(half_ref, dT_ref, normed_ref, go_ref, got_ref, early_ref, keep_ref, send_ref, small_ref, acc):
    n = dT_ref.shape[0]
    w = go_ref.shape[0]
    half = keep_ref.shape[0]
    acc[:n] = dg(dT_ref[...], normed_ref[...], 1, 0)
    acc[n:] = go_ref[...] + got_ref[:w].astype(f32)
    small = early_ref[...] + sum_halves(got_ref[w:])
    small_ref[...] = small
    a = pl.multiple_of(half_ref[0] * half, half)
    b = pl.multiple_of((1 - half_ref[0]) * half, half)
    keep_ref[...] = acc[pl.ds(a, half)]
    send_ref[:half] = acc[pl.ds(b, half)].astype(bf16)
    send_ref[half:] = halves_of(small)


def weight_rows(half, dT, normed, go, got, small):
    rows = dT.shape[0] + go.shape[0]
    outs = (((rows // 2, D), f32), ((rows // 2 + 2 * small.shape[0], D), bf16), (small.shape, f32))
    return one_step(
        weight_rows_kernel,
        "weight_rows",
        outs,
        (half, dT, normed, go, got, small),
        [pltpu.VMEM((rows, D), f32)],
        2 * dT.size * D,
    )


def share_kernel(me_ref, half_ref, got_ref, early_ref, own_ref, *refs):
    dp = len(refs) - 1
    sends, small_ref, acc = refs[: dp - 1], refs[dp - 1], refs[dp]
    half = half_ref.shape[0]
    w = half // dp
    acc[...] = half_ref[...] + got_ref[:half].astype(f32)
    small = early_ref[...] + sum_halves(got_ref[half:])
    small_ref[...] = small

    def share(step):
        return acc[pl.ds(pl.multiple_of(lax.rem(me_ref[0] + step, dp) * w, w), w)]

    own_ref[...] = share(0)
    for step in range(1, dp):
        sends[step - 1][:w] = share(step).astype(bf16)
        sends[step - 1][w:] = halves_of(small)


def share_step(zi, half, got, small, dp):
    w = half.shape[0] // dp
    outs = (((w, D), f32),) + (((w + 2 * small.shape[0], D), bf16),) * (dp - 1) + ((small.shape, f32),)
    return one_step(
        functools.partial(share_kernel),
        "share_step",
        outs,
        (zi, half, got, small),
        [pltpu.VMEM(half.shape, f32)],
        0,
    )


SIDE = tuple((core, over, begin) for core in range(2) for over in range(2) for begin in range(2))


def finish_kernel(dp, side, me_ref, *refs):
    layout = SIDE
    n = len(layout)
    pieces, weights, scale_ref, before_ref = refs[:n], refs[n : n + 3], refs[n + 3], refs[n + 4]
    outs, row_ref = refs[-11:-7], refs[-7]
    got, wide, held, in_sem, out_sem, w_sem = refs[-6:]
    mine = D // 4
    rows = 2 * mine // dp
    copies = []
    for k, (core, over, begin) in enumerate(layout):
        first = (over ^ me_ref[1]) * (2 * mine) + (core ^ me_ref[2]) * mine
        for i in range(pieces[k].shape[0] // rows):
            row = lax.rem(me_ref[0] + dp - begin * (dp // 2) - i, dp) * rows
            copy = pltpu.make_async_copy(
                pieces[k].at[pl.ds(i * rows, rows)],
                got.at[lax.div(row, mine), pl.ds(pl.multiple_of(first + lax.rem(row, mine), rows), rows)],
                in_sem.at[k, i],
            )
            copy.start()
            copies.append(copy)

    def put(pair):
        loads = [pltpu.make_async_copy(weights[p], held.at[k], w_sem.at[k]) for k, p in enumerate(pair) if p < 3]
        for copy in loads:
            copy.start()
        for copy in copies + loads:
            copy.wait()
        total = jnp.zeros((D, 1), f32)
        backs = []
        for k in (1, 0):
            if pair[k] < 3:
                g = got[k].T.astype(f32)
                total = total + jnp.sum(g * held[k].astype(f32), axis=1, keepdims=True)
            else:
                g = got[k].astype(f32)
            wide[k] = g
            back = pltpu.make_async_copy(wide.at[k], outs[pair[k]], out_sem.at[k])
            back.start()
            backs.append(back)
        row = jnp.broadcast_to(total, (D, 128)).T[:1]
        row_ref[...] = ((before_ref[...] + row) / scale_ref[...])[0] if side else row
        for back in backs:
            back.wait()

    y = lax.rem(me_ref[3] + side, 2)

    @pl.when(y == 0)
    def _():
        put((0, 1))

    @pl.when(y == 1)
    def _():
        put((2, 3))


def finish(me, pieces, weights, scale, side, so_far, dp):
    whole = jax.ShapeDtypeStruct((D, D), f32)
    anywhere = pl.BlockSpec(memory_space=pl.ANY)
    row = pl.BlockSpec((1, D), lambda i, p: (0, 0))
    args = [*pieces, *weights, scale, so_far[4] if side else scale]
    specs = [anywhere] * (len(args) - 2) + [row, row]
    alias = {}
    if side:
        alias = {1 + len(args) + p: p for p in range(4)}
        args += list(so_far[:4])
        specs += [anywhere] * 4
    return pl.pallas_call(
        functools.partial(finish_kernel, dp, side),
        out_shape=(whole,) * 4 + (jax.ShapeDtypeStruct((D,) if side else (1, D), f32),),
        grid_spec=pltpu.PrefetchScalarGridSpec(
            num_scalar_prefetch=1,
            grid=(1,),
            in_specs=specs,
            out_specs=(anywhere,) * 4 + (pl.BlockSpec((D,), lambda i, p: (0,)) if side else row,),
            scratch_shapes=[
                pltpu.VMEM((2, D, D), bf16),
                pltpu.VMEM((2, D, D), f32),
                pltpu.VMEM((2, D, D), bf16),
                pltpu.SemaphoreType.DMA((len(pieces), dp)),
                pltpu.SemaphoreType.DMA((2,)),
                pltpu.SemaphoreType.DMA((2,)),
            ],
        ),
        input_output_aliases=alias,
        compiler_params=pltpu.CompilerParams(vmem_limit_bytes=VMEM),
        cost_estimate=pl.CostEstimate(flops=4 * D * D, bytes_accessed=16 * D * D, transcendentals=0),
        name=f"finish{side}",
    )(me, *args)


def swap(v, axis):
    return lax.ppermute(v, axis, [(0, 1), (1, 0)])


def shift(v, axis, step):
    n = lax.axis_size(axis)
    return lax.ppermute(v, axis, [(i, (i + step) % n) for i in range(n)])


def at(v, index):
    return lax.dynamic_index_in_dim(v, index, 0, keepdims=False)


def one(v):
    v = v.astype(f32)
    n = v.shape[0] // 2
    return v[:n] + v[n:]


def add_pair(v):
    return v + (swap(v, "expert") if lax.axis_size("expert") == 2 else lax.psum(v, "expert") - v)


def add_shifts(v):
    out = v
    for s in range(1, lax.axis_size("dp")):
        out = out + shift(v, "dp", s)
    return out


def index(i):
    return i.astype(jnp.int32).reshape(1)


def tie(*arrays):
    return lax.optimization_barrier(arrays)


def normal_form(v):
    centred = v - jnp.mean(v, axis=-1, keepdims=True)
    rstd = lax.rsqrt(jnp.mean(centred * centred, axis=-1, keepdims=True) + norm_eps)
    return centred * rstd, rstd


def norm_back(dn, xh, rstd):
    return rstd * (dn - jnp.mean(dn, axis=-1, keepdims=True) - xh * jnp.mean(dn * xh, axis=-1, keepdims=True))


def per_device(
    tokens,
    cotangent,
    routes,
    norm1_gain,
    w_query,
    w_key,
    w_value,
    w_output,
    norm2_gain,
    w_router,
    w_in,
    w_out,
):
    rows = tokens.shape[1]
    nx, owners, dp = lax.axis_size("x"), lax.axis_size("expert"), lax.axis_size("dp")
    xi, ci, ei = lax.axis_index("x"), lax.axis_index("core"), lax.axis_index("expert")
    ctx = 2 * nx
    ctx_i = xi * 2 + ci
    length = ctx * rows
    experts = w_router.shape[1]
    cap = 2 * rows // experts
    mine = D // ctx
    heads = mine // HD
    expert_id = ei * nx + xi
    pick = jnp.stack([xi, ci, expert_id]).astype(jnp.int32)

    tok = tokens.reshape(rows, D)
    flat = tok.astype(f32)
    other = swap(tok, "x")
    near = swap(tok, "core")

    route = routes.reshape(rows)
    hot = (route[:, None] == jnp.arange(128, dtype=jnp.int32)[None, :]).astype(f32)
    lower = jnp.arange(rows)[:, None] >= jnp.arange(rows)[None, :]
    before = dg(lower.astype(bf16), hot.astype(bf16), 1, 0)
    rank = (jnp.sum(before * hot, axis=1) - 1.0).astype(jnp.int32)
    slot = ((route % nx) * owners + route // nx) * cap + rank
    spread = (jnp.arange(experts * cap, dtype=jnp.int32)[:, None] == slot[None, :]).astype(bf16)

    def pack(v):
        return dg(spread, v, 1, 0).astype(bf16).reshape(nx * owners, cap, D)

    def trade(v):
        v = lax.all_to_all(v.reshape(nx * owners, cap, D), ("x", "expert"), split_axis=0, concat_axis=0, tiled=True)
        return v.reshape(-1, D)

    def turn(v):
        return lax.all_to_all(v, ("x", "core"), split_axis=0, concat_axis=0, tiled=True)

    def cut(w):
        return lax.dynamic_slice(w, (0, ctx_i * mine), (D, mine))

    w_own = jnp.concatenate([cut(w_query), cut(w_key), cut(w_value)], axis=1)
    gain1 = norm1_gain.reshape(1, D)
    dy_low = cotangent.reshape(rows, D)
    dy = dy_low.astype(f32)
    wr = lax.dynamic_slice(w_router, (0, expert_id), (D, 1)).astype(f32).reshape(1, D)
    counts = jnp.sum(hot, axis=0, keepdims=True)
    counts = counts + swap(counts, "core")
    counts = add_pair(counts)
    so_far = project([ctx_i], [tok], gain1, w_own, ctx, None)
    counts, dy_packed, *so_far = tie(counts, pack(dy_low), *so_far)
    so_far = project([ctx_i ^ 1], [near], gain1, w_own, ctx, so_far)
    other, dy_packed, *so_far = tie(other, dy_packed, *so_far)
    far = swap(other, "core")
    dy_rows = trade(dy_packed)
    normed_all, qkvT, kv = project([ctx_i ^ 2, ctx_i ^ 3], [other, far], gain1, w_own, ctx, so_far)
    oT, osend, lse = attend(qkvT, kv, ctx)
    osend, dy_rows, counts = tie(osend, dy_rows, counts)
    attT = turn(osend)
    counts = add_shifts(counts)
    attT, counts = tie(attT, counts)
    counts = counts + swap(counts, "x")
    attT = attT.reshape(D, rows)
    mean_load = rows * ctx * dp * owners / experts
    gain2 = norm2_gain.reshape(1, D)
    middle, second, packed = middle_step(attT, tok, w_output, gain2, slot[None], nx * owners, cap)
    gating = jax.nn.sigmoid(jnp.sum(hot[:, :experts] * dg(second, w_router, 1, 0), axis=1))

    up = expert_up(pick, dy_rows, w_out)
    sig = jnp.pad(jnp.sum(hot[:, :experts] * gating[:, None], axis=0), (0, D - experts))
    counts, packed = tie(counts, packed)
    x_rows = trade(packed)
    x_rows, gating, sig, slot, gain2 = tie(x_rows, gating, sig, slot[None], gain2)
    active, grad_hidden, back_rows, router_row, gate = expert_mid(pick, x_rows, up, w_in, wr, counts, mean_load)
    returned = trade(back_rows)
    keep, send, produced = expert_grads(pick, x_rows, dy_rows, gate, active, grad_hidden, w_out, dp, nx)
    returned, keep, send, produced = tie(returned, keep, send, produced)
    taken = swap(send, "core")
    zi = lax.axis_index("dp")

    def chunk(i):
        return at(keep, (i + dp) % dp).astype(f32) + at(taken, (i + dp) % dp).astype(f32)

    def ring(moving, step):
        return (shift(moving, "dp", 1).astype(f32) + chunk(zi - 2 - step)).astype(bf16)

    def side(v, x):
        return lax.dynamic_index_in_dim(v, x, 1, keepdims=False)

    router_rows = (jnp.arange(experts) == expert_id).astype(f32)[:, None] * router_row
    small = jnp.concatenate([router_rows, jnp.zeros((1, D), f32), sig[None]], axis=0)
    small = jnp.pad(small, ((0, -small.shape[0] % 8), (0, 0)))
    grad_middle, heads_grad, go, go_send, small = branch_back(
        index(ci), returned, slot, dy_low, middle, gain2, w_output, attT, small, experts, ctx
    )
    do = turn(heads_grad)

    moving = ring(chunk(zi - 1).astype(bf16), 0)
    go_got = swap(go_send, "core")
    go, go_send, small = go_step(index(xi), go, go_got, small)
    do, go_send = tie(do, go_send)
    go_got = swap(go_send, "x")

    so_far = attend_back(qkvT, kv, do, 0, oT, lse, 0, None)
    produced, go_got, *so_far = tie(produced, go_got, *so_far)
    went_back = trade(produced)
    so_far = attend_back(qkvT, kv, do, 1, oT, lse, 1, so_far)
    moving, *so_far = tie(moving, *so_far)
    moving = ring(moving, 1)
    for h in range(2, heads):
        so_far = attend_back(qkvT, kv, do, h, oT, lse, h, so_far)
    went_back, dT, dsend = tie(went_back, *so_far)
    output = (middle + gating[:, None] * dg(spread, went_back, 0, 0)).astype(bf16)

    ei2 = ei if owners == 2 else jnp.zeros_like(ei)
    half, send, small = weight_rows(index(ei2), dT.reshape(3 * mine, length), normed_all, go, go_got, small)
    dsend, send = tie(dsend, send)
    got = turn(dsend)
    if owners == 2:
        gift = swap(send, "expert")
        gift, moving = tie(gift, moving)
        halves = [(half, gift)]
    else:
        cut_at = half.shape[0]
        small = lax.psum(small, "expert")
        nothing = jnp.zeros_like(send)
        halves = [(lax.psum(half, "expert"), nothing), (lax.psum(send[:cut_at].astype(f32), "expert"), nothing)]
    pieces = []
    for part, gift in halves:
        share, *gifts, more = share_step(index(zi), part, gift, small, dp)
        gifts = [shift(gift, "dp", step + 1) for step, gift in enumerate(gifts)]
        for gift in gifts:
            more = more + one(gift[share.shape[0] :])
            share = share + gift[: share.shape[0]].astype(f32)
        share = share.astype(bf16)
        shares = [share] + [shift(share, "dp", step) for step in range(1, dp)]
        pieces.append([jnp.concatenate(shares[k : k + dp // 2], axis=0) for k in range(0, dp, dp // 2)])
    small = more
    output, keep, taken = tie(output, keep, taken)
    crossed = swap(side(chunk(zi), 1 - xi).astype(bf16), "x")
    for step in range(2, dp - 2):
        moving = ring(moving, step)
    moving, crossed, *pieces = tie(moving, crossed, *pieces)
    own = shift(side(moving, xi), "dp", 1)
    route_on = [(z * nx + x, (z + 1) % dp * nx + 1 - x) for z in range(dp) for x in range(nx)]
    theirs = side(moving, 1 - xi)

    grad_normed = 0.0
    for p, w in enumerate((w_query, w_key, w_value)):
        grad_normed = grad_normed + dg(got[:, p].reshape(D, rows), w, 0, 1)
    xh1, rstd1 = normal_form(flat)
    grad_tokens = grad_middle + norm_back(grad_normed * norm1_gain, xh1, rstd1)

    near_pieces = pieces[0]
    if owners == 2:
        across = [swap(near_pieces[0], "expert"), None]
        beyond = [None, swap(near_pieces[1], "x")]
        across[1] = swap(near_pieces[1], "expert")
        beyond[0] = swap(near_pieces[0], "x")
        corner = [swap(across[0], "x"), swap(beyond[1], "expert")]
    else:
        across = pieces[1]
        beyond = [swap(piece, "x") for piece in near_pieces]
        corner = [swap(piece, "x") for piece in across]
    me = jnp.stack([zi, xi, ci, ei2]).astype(jnp.int32)
    projections = (w_query, w_key, w_value)
    near_pieces = near_pieces + beyond
    near_pieces += [swap(piece, "core") for piece in near_pieces]
    placed = finish(me, near_pieces, projections, gain1, 0, None, dp)
    own, theirs, *corner = tie(own, theirs, *corner, *placed)
    corner, placed = corner[:2], corner[2:]
    moved = lax.ppermute(theirs, ("dp", "x"), route_on)
    far_pieces = across + corner
    far_pieces += [swap(piece, "core") for piece in far_pieces]
    *grads, grad_norm1 = finish(me, far_pieces, projections, gain1, 1, placed, dp)

    own = own.astype(f32) + side(chunk(zi), xi)
    moved = moved.astype(f32) + crossed.astype(f32)
    first, latter = jnp.where(xi == 0, own, moved), jnp.where(xi == 0, moved, own)
    both = jnp.stack([first, latter], axis=1)
    grad_in = jnp.swapaxes(both[0], 1, 2)
    grad_out = both[1]

    grad_router = jnp.transpose(small[:experts])
    grad_norm2 = small[experts]
    total_sig = small[experts + 1, :experts]
    counts = counts[0, :experts]
    balance = balance_weight * jnp.sum((counts - mean_load) / mean_load * total_sig) / mean_load

    return (
        output.reshape(1, rows, D),
        grad_tokens.reshape(1, rows, D),
        grad_norm1,
        grads[0],
        grads[1],
        grads[2],
        grads[3],
        grad_norm2,
        grad_router,
        grad_in,
        grad_out,
        balance,
    )


def solution(mesh):
    dp, ctx, owners = mesh.shape["dp"], mesh.shape["ctx"], mesh.shape["expert"]
    split = Mesh(mesh.devices.reshape(dp, ctx // 2, 2, owners), ("dp", "x", "core", "expert"))
    token = P(("dp", "expert"), ("x", "core"), None)
    return jax.shard_map(
        per_device,
        mesh=split,
        in_specs=(token, token, token, P(), P(), P(), P(), P(), P(), P(), P("expert"), P("expert")),
        out_specs=(
            token,
            token,
            P(),
            P(),
            P(),
            P(),
            P(),
            P(),
            P(),
            P("expert", None, ("dp", "x", "core")),
            P("expert", ("dp", "x", "core"), None),
            P(),
        ),
        check_vma=False,
    )
```

```python
import functools

import jax
import jax.numpy as jnp
from jax import lax
from jax.experimental import pallas as pl
from jax.experimental.pallas import tpu as pltpu
from jax.sharding import Mesh
from jax.sharding import PartitionSpec as P

D = 768
HEADS = 12
HD = 64
norm_eps = 1e-05
balance_weight = 1.0
LOG2E = 1.4426950408889634
MASKED = -1e30
GELU_A = 0.7978845608028654
GELU_B = 0.044715
VMEM = 56 * 1024 * 1024
f32 = jnp.float32
bf16 = jnp.bfloat16


def dg(a, b, ca, cb):
    return lax.dot_general(a, b, (((ca,), (cb,)), ((), ())), preferred_element_type=f32)


def project_kernel(place_ref, *refs):
    normed_ref, qkvT_ref, kv_ref = refs[-3:]
    blocks = place_ref.shape[0]
    gain_ref, w_ref = refs[blocks : blocks + 2]

    def work(tok_ref):
        x = tok_ref[...].astype(f32)
        centred = x - jnp.mean(x, axis=1, keepdims=True)
        rstd = lax.rsqrt(jnp.mean(centred * centred, axis=1, keepdims=True) + norm_eps)
        normed = (centred * rstd * gain_ref[...]).astype(bf16)
        normed_ref[...] = normed
        qkv = dg(normed, w_ref[...], 1, 0).astype(bf16)
        kv_ref[...] = qkv[:, qkv.shape[1] - kv_ref.shape[1] :]
        qkvT_ref[...] = qkv.T

    for k in range(blocks):

        @pl.when(pl.program_id(0) == k)
        def _():
            work(refs[k])


def project(places, toks, gain, w, ctx, so_far):
    rows = toks[0].shape[0]
    wide = w.shape[1]
    args = [*toks, gain, w]
    specs = [pl.BlockSpec(a.shape, lambda i, p: (0, 0)) for a in args]
    alias = {}
    if so_far is not None:
        alias = {1 + len(args) + k: k for k in range(3)}
        args += list(so_far)
        specs += [pl.BlockSpec(memory_space=pl.ANY)] * 3
    return pl.pallas_call(
        project_kernel,
        out_shape=(
            jax.ShapeDtypeStruct((ctx * rows, D), bf16),
            jax.ShapeDtypeStruct((wide, ctx * rows), bf16),
            jax.ShapeDtypeStruct((ctx * rows, 2 * wide // 3), bf16),
        ),
        grid_spec=pltpu.PrefetchScalarGridSpec(
            num_scalar_prefetch=1,
            grid=(len(toks),),
            in_specs=specs,
            out_specs=(
                pl.BlockSpec((rows, D), lambda i, p: (p[i], 0)),
                pl.BlockSpec((wide, rows), lambda i, p: (0, p[i])),
                pl.BlockSpec((rows, 2 * wide // 3), lambda i, p: (p[i], 0)),
            ),
        ),
        input_output_aliases=alias,
        compiler_params=pltpu.CompilerParams(vmem_limit_bytes=VMEM),
        cost_estimate=pl.CostEstimate(
            flops=4 * len(toks) * rows * D * wide, bytes_accessed=4 * rows * D + 8 * rows * wide, transcendentals=0
        ),
        name="project",
    )(jnp.stack(places).astype(jnp.int32), *args)


def attend_kernel(heads, blk, qT_ref, k_ref, vT_ref, oT_ref, osend_ref, lse_ref):
    length = qT_ref.shape[1]
    per = osend_ref.shape[3]
    c = (HD**-0.5) * LOG2E
    rows = lax.broadcasted_iota(jnp.int32, (blk, blk), 0)
    cols = lax.broadcasted_iota(jnp.int32, (blk, blk), 1)
    keep = rows <= cols
    for h in range(heads):
        hs = slice(h * HD, (h + 1) * HD)
        for i in range(length // blk):
            a, b = i * blk, (i + 1) * blk
            q = qT_ref[hs, a:b]
            sd = dg(k_ref[a:b, hs], q, 1, 0)
            sd = jnp.where(keep, sd, MASKED)
            m = jnp.max(sd, axis=0, keepdims=True)
            if i:
                s = dg(k_ref[:a, hs], q, 1, 0)
                m = jnp.maximum(m, jnp.max(s, axis=0, keepdims=True))
            mc = m * c
            pd = jnp.exp2(sd * c - mc)
            total = jnp.sum(pd, axis=0, keepdims=True)
            o = dg(vT_ref[hs, a:b], pd.astype(bf16), 1, 0)
            if i:
                p = jnp.exp2(s * c - mc)
                total = total + jnp.sum(p, axis=0, keepdims=True)
                o = o + dg(vT_ref[hs, :a], p.astype(bf16), 1, 0)
            o = o / total
            oT_ref[hs, a:b] = o
            d, off = a // per, a % per
            osend_ref[d, h, :, off : off + blk] = o.astype(bf16)
            lse_ref[h, :, a:b] = mc + jnp.log2(total)


def attend(qkvT, kv, dests):
    length = kv.shape[0]
    heads = qkvT.shape[0] // (3 * HD)
    wide = heads * HD
    per = length // dests
    return pl.pallas_call(
        functools.partial(attend_kernel, heads, per),
        out_shape=(
            jax.ShapeDtypeStruct((wide, length), f32),
            jax.ShapeDtypeStruct((dests, heads, HD, per), bf16),
            jax.ShapeDtypeStruct((heads, 1, length), f32),
        ),
        grid=(1,),
        in_specs=[
            pl.BlockSpec((wide, length), lambda i: (0, 0)),
            pl.BlockSpec(kv.shape, lambda i: (0, 0)),
            pl.BlockSpec((wide, length), lambda i: (2, 0)),
        ],
        out_specs=(
            pl.BlockSpec((wide, length), lambda i: (0, 0)),
            pl.BlockSpec((dests, heads, HD, per), lambda i: (0, 0, 0, 0)),
            pl.BlockSpec((heads, 1, length), lambda i: (0, 0, 0)),
        ),
        compiler_params=pltpu.CompilerParams(vmem_limit_bytes=VMEM),
        cost_estimate=pl.CostEstimate(
            flops=8 * heads * length * length * HD,
            bytes_accessed=length * wide * 14,
            transcendentals=heads * length * length // 2,
        ),
        name="attend",
    )(qkvT, kv, qkvT)


def attend_back_kernel(lk, lv, blk, *refs):
    qT_ref, k_ref, kT_ref, v_ref, do_ref, oT_ref, lse_ref = refs[:7]
    dT_ref, dsend_ref, dk_acc, dv_acc = refs[-4:]
    length = qT_ref.shape[1]
    per = do_ref.shape[3]
    sc = HD**-0.5
    c = sc * LOG2E
    rows = lax.broadcasted_iota(jnp.int32, (blk, blk), 0)
    cols = lax.broadcasted_iota(jnp.int32, (blk, blk), 1)
    keep = rows <= cols
    n = length // blk
    for i in reversed(range(n)):
        x0, x1 = i * blk, (i + 1) * blk
        d, off = x0 // per, x0 % per
        q = qT_ref[:, x0:x1]
        do = do_ref[d, 0, :, off : off + blk]
        lse = lse_ref[0, :, x0:x1]
        delta = jnp.sum(do.astype(f32) * oT_ref[:, x0:x1], axis=0, keepdims=True)
        dq = None
        for a, b, diag in ([(0, x0, False)] if i else []) + [(x0, x1, True)]:
            s = dg(k_ref[a:b, lk : lk + HD], q, 1, 0)
            p = jnp.exp2(s * c - lse)
            if diag:
                p = jnp.where(keep, p, 0.0)
            dp = dg(v_ref[a:b, lv : lv + HD], do, 1, 0)
            ds = (p * (dp - delta)).astype(bf16)
            dvn = dg(do, p.astype(bf16), 1, 1)
            dkn = dg(q, ds, 1, 1)
            if i == n - 1:
                dv_acc[:, a:b] = dvn
                dk_acc[:, a:b] = dkn
            else:
                dv_acc[:, a:b] += dvn
                dk_acc[:, a:b] += dkn
            t = dg(kT_ref[:, a:b], ds, 1, 0)
            dq = t if dq is None else dq + t
        dq = (dq * sc).astype(bf16)
        dT_ref[0, :, x0:x1] = dq
        dsend_ref[d, 0, :, off : off + blk] = dq
    for d in range(dsend_ref.shape[0]):
        at_d = slice(d * per, (d + 1) * per)
        dk = (dk_acc[:, at_d] * sc).astype(bf16)
        dv = dv_acc[:, at_d].astype(bf16)
        dT_ref[1, :, at_d] = dk
        dT_ref[2, :, at_d] = dv
        dsend_ref[d, 1] = dk
        dsend_ref[d, 2] = dv


def attend_back(qkvT, kv, do, slot, oT, lse, h, so_far):
    length = kv.shape[0]
    n = qkvT.shape[0] // (3 * HD)
    dests, _, _, per = do.shape
    hv = n + h
    blk = min(256, per)
    args = [qkvT, kv, qkvT, kv, do, oT, lse]
    specs = [
        pl.BlockSpec((HD, length), lambda i: (h, 0)),
        pl.BlockSpec((length, 2 * HD), lambda i: (0, h // 2)),
        pl.BlockSpec((HD, length), lambda i: (n + h, 0)),
        pl.BlockSpec((length, 2 * HD), lambda i: (0, hv // 2)),
        pl.BlockSpec((dests, 1, HD, per), lambda i: (0, slot, 0, 0)),
        pl.BlockSpec((HD, length), lambda i: (h, 0)),
        pl.BlockSpec((1, 1, length), lambda i: (h, 0, 0)),
    ]
    alias = {}
    if so_far is not None:
        alias = {len(args): 0, len(args) + 1: 1}
        args += list(so_far)
        specs += [pl.BlockSpec(memory_space=pl.ANY)] * 2
    return pl.pallas_call(
        functools.partial(attend_back_kernel, (h % 2) * HD, (hv % 2) * HD, blk),
        out_shape=(
            jax.ShapeDtypeStruct((3, n * HD, length), bf16),
            jax.ShapeDtypeStruct((dests, 3, n * HD, per), bf16),
        ),
        grid=(1,),
        in_specs=specs,
        out_specs=(
            pl.BlockSpec((3, HD, length), lambda i: (0, h, 0)),
            pl.BlockSpec((dests, 3, HD, per), lambda i: (0, 0, h, 0)),
        ),
        scratch_shapes=[pltpu.VMEM((HD, length), f32)] * 2,
        input_output_aliases=alias,
        compiler_params=pltpu.CompilerParams(vmem_limit_bytes=VMEM),
        cost_estimate=pl.CostEstimate(
            flops=20 * length * length * HD, bytes_accessed=length * HD * 24, transcendentals=length * length // 2
        ),
        name=f"attend_back_head{h}",
    )(*args)


def middle_kernel(me_ref, att_ref, tok_ref, w_ref, gain_ref, slot_ref, middle_ref, second_ref, packed_ref):
    v = tok_ref[...].astype(f32) + dg(att_ref[...], w_ref[...], 0, 0)
    middle_ref[...] = v
    centred = v - jnp.mean(v, axis=1, keepdims=True)
    rstd = lax.rsqrt(jnp.mean(centred * centred, axis=1, keepdims=True) + norm_eps)
    second = (centred * rstd * gain_ref[...]).astype(bf16)
    second_ref[...] = second
    spread = one_hot_slots(slot_ref[...], packed_ref.shape[0] * packed_ref.shape[1])
    packed_ref[...] = dg(spread, second, 1, 0).astype(bf16).reshape(packed_ref.shape)


def middle_step(attT, tok, w, gain, slot, sources, cap):
    rows = tok.shape[0]
    outs = (((rows, D), f32), ((rows, D), bf16), ((sources, cap, D), bf16))
    return one_step(
        middle_kernel,
        "middle_step",
        outs,
        (jnp.zeros((1,), jnp.int32), attT, tok, w, gain, slot),
        [],
        2 * rows * D * (D + sources * cap),
    )


def up_kernel(pick_ref, dy_ref, wo_ref, u_ref):
    u_ref[...] = dg(dy_ref[...], wo_ref[0], 1, 1).astype(bf16)


def expert_up(pick, dy, w_out, fc=768):
    rows = dy.shape[0]
    ff = w_out.shape[1]
    return pl.pallas_call(
        up_kernel,
        out_shape=jax.ShapeDtypeStruct((rows, ff), bf16),
        grid_spec=pltpu.PrefetchScalarGridSpec(
            num_scalar_prefetch=1,
            grid=(ff // fc,),
            in_specs=[
                pl.BlockSpec((rows, D), lambda f, p: (0, 0)),
                pl.BlockSpec((1, fc, D), lambda f, p: (p[0], f, 0)),
            ],
            out_specs=pl.BlockSpec((rows, fc), lambda f, p: (0, f)),
        ),
        compiler_params=pltpu.CompilerParams(vmem_limit_bytes=VMEM),
        cost_estimate=pl.CostEstimate(
            flops=2 * rows * D * ff, bytes_accessed=2 * (rows * D + ff * D + rows * ff), transcendentals=0
        ),
        name="expert_up",
    )(pick, dy, w_out)


def mid_kernel(
    mean, pick_ref, x_ref, u_ref, wi_ref, wr_ref, count_ref, act_ref, gh_ref, rows_ref, router_ref, gate_ref, acc, gg, gate
):
    f = pl.program_id(0)
    n = pl.num_programs(0)

    @pl.when(f == 0)
    def _():
        logit = jnp.sum(x_ref[...].astype(f32) * wr_ref[...], axis=1, keepdims=True)
        gate[...] = jnp.broadcast_to(jax.nn.sigmoid(logit), gate.shape)
        acc[...] = jnp.zeros_like(acc)
        gg[...] = jnp.zeros_like(gg)

    step = 256
    for r in range(0, x_ref.shape[0], step):
        rs = slice(r, r + step)
        for c in range(0, wi_ref.shape[2], step):
            cs = slice(c, c + step)
            h = dg(x_ref[rs], wi_ref[0, :, cs], 1, 0)
            h2 = h * h
            t = jnp.tanh(h * (GELU_A + (GELU_A * GELU_B) * h2))
            hp = 0.5 + 0.5 * t
            dgelu = hp + (h * (hp - hp * hp)) * (2.0 * GELU_A + (6.0 * GELU_A * GELU_B) * h2)
            u = u_ref[rs, cs].astype(f32)
            active = h * hp
            act_ref[rs, cs] = active.astype(bf16)
            au = active * u
            lanes = au[:, :128]
            for j in range(128, step, 128):
                lanes = lanes + au[:, j : j + 128]
            gg[rs] += lanes
            gh = (gate[rs, :1] * (u * dgelu)).astype(bf16)
            gh_ref[rs, cs] = gh
            acc[rs] += dg(gh, wi_ref[0, :, cs], 1, 1)

    @pl.when(f == n - 1)
    def _():
        g = gate[:, :1]
        got = jnp.sum(gg[...], axis=1, keepdims=True)
        lane = lax.broadcasted_iota(jnp.int32, count_ref.shape, 1)
        count = jnp.sum(jnp.where(lane == pick_ref[2], count_ref[...], 0.0), axis=1, keepdims=True)
        load = balance_weight * (count - mean) / (mean * mean)
        sel = (g * (1.0 - g) * (got + load)).astype(bf16).astype(f32)
        rows_ref[...] = (acc[...] + sel * wr_ref[...]).astype(bf16)
        router_ref[...] = jnp.sum(x_ref[...].astype(f32) * sel, axis=0, keepdims=True)
        gate_ref[...] = gate[...]


def expert_mid(pick, x, u, w_in, wr, counts, mean, fc=768):
    rows = x.shape[0]
    ff = w_in.shape[2]

    def full(s):
        return pl.BlockSpec(s, lambda f, p: (0, 0))

    wide = pl.BlockSpec((rows, fc), lambda f, p: (0, f))
    return pl.pallas_call(
        functools.partial(mid_kernel, mean),
        out_shape=(
            jax.ShapeDtypeStruct((rows, ff), bf16),
            jax.ShapeDtypeStruct((rows, ff), bf16),
            jax.ShapeDtypeStruct((rows, D), bf16),
            jax.ShapeDtypeStruct((1, D), f32),
            jax.ShapeDtypeStruct((rows, 128), f32),
        ),
        grid_spec=pltpu.PrefetchScalarGridSpec(
            num_scalar_prefetch=1,
            grid=(ff // fc,),
            in_specs=[
                full((rows, D)),
                wide,
                pl.BlockSpec((1, D, fc), lambda f, p: (p[0], 0, f)),
                full((1, D)),
                full((1, 128)),
            ],
            out_specs=(wide, wide, full((rows, D)), full((1, D)), full((rows, 128))),
            scratch_shapes=[
                pltpu.VMEM((rows, D), f32),
                pltpu.VMEM((rows, 128), f32),
                pltpu.VMEM((rows, 128), f32),
            ],
        ),
        compiler_params=pltpu.CompilerParams(vmem_limit_bytes=VMEM),
        cost_estimate=pl.CostEstimate(
            flops=4 * rows * D * ff,
            bytes_accessed=2 * (3 * rows * D + ff * D + 3 * rows * ff),
            transcendentals=rows * ff,
        ),
        name="expert_mid",
    )(pick, x, u, w_in, wr, counts)


def grads_kernel(
    pick_ref, x_ref, dy_ref, gate_ref, act_ref, gh_ref, wo_ref, keep_ref, send_ref, prod_ref, acc, go, gi, gexp
):
    f = pl.program_id(0)
    n = pl.num_programs(0)

    @pl.when(f == 0)
    def _():
        gexp[...] = (dy_ref[...].astype(f32) * gate_ref[:, :1]).astype(bf16)

    go[...] = dg(act_ref[...], gexp[...], 0, 0).astype(bf16)
    gi[...] = dg(gh_ref[...], x_ref[...], 0, 0).astype(bf16)
    part = dg(act_ref[...], wo_ref[0], 1, 0)

    @pl.when(f == 0)
    def _():
        acc[...] = part

    @pl.when(f > 0)
    def _():
        acc[...] += part

    w = keep_ref.shape[3]
    me = pick_ref[1]
    for xx in range(keep_ref.shape[2]):
        a = pl.multiple_of((2 * xx + me) * w, w)
        b = pl.multiple_of((2 * xx + 1 - me) * w, w)
        keep_ref[0, 0, xx] = gi[pl.ds(a, w)]
        keep_ref[0, 1, xx] = go[pl.ds(a, w)]
        send_ref[0, 0, xx] = gi[pl.ds(b, w)]
        send_ref[0, 1, xx] = go[pl.ds(b, w)]

    @pl.when(f == n - 1)
    def _():
        prod_ref[...] = acc[...].astype(bf16)


def expert_grads(pick, x, dy, gate, act, gh, w_out, dp, nx):
    rows = x.shape[0]
    ff = w_out.shape[1]
    fc = ff // dp
    w = fc // (2 * nx)

    def full(s):
        return pl.BlockSpec(s, lambda f, p: (0, 0))

    wide = pl.BlockSpec((rows, fc), lambda f, p: (0, f))
    part = jax.ShapeDtypeStruct((dp, 2, nx, w, D), bf16)
    part_spec = pl.BlockSpec((1, 2, nx, w, D), lambda f, p: (f, 0, 0, 0, 0))
    return pl.pallas_call(
        grads_kernel,
        out_shape=(part, part, jax.ShapeDtypeStruct((rows, D), bf16)),
        grid_spec=pltpu.PrefetchScalarGridSpec(
            num_scalar_prefetch=1,
            grid=(dp,),
            in_specs=[
                full((rows, D)),
                full((rows, D)),
                full((rows, 128)),
                wide,
                wide,
                pl.BlockSpec((1, fc, D), lambda f, p: (p[0], f, 0)),
            ],
            out_specs=(part_spec, part_spec, full((rows, D))),
            scratch_shapes=[
                pltpu.VMEM((rows, D), f32),
                pltpu.VMEM((fc, D), bf16),
                pltpu.VMEM((fc, D), bf16),
                pltpu.VMEM((rows, D), bf16),
            ],
        ),
        compiler_params=pltpu.CompilerParams(vmem_limit_bytes=VMEM),
        cost_estimate=pl.CostEstimate(
            flops=6 * rows * D * ff,
            bytes_accessed=2 * (3 * rows * D + 3 * ff * D + 2 * rows * ff),
            transcendentals=0,
        ),
        name="expert_grads",
    )(pick, x, dy, gate, act, gh, w_out)


def one_hot_slots(slot, slots):
    return (lax.broadcasted_iota(jnp.int32, (slots, slot.shape[1]), 0) == slot).astype(f32).astype(bf16)


def halves_of(v):
    high = v.astype(bf16)
    return jnp.concatenate([high, (v - high.astype(f32)).astype(bf16)], axis=0)


def sum_halves(v):
    v = v.astype(f32)
    n = v.shape[0] // 2
    return v[:n] + v[n:]


def branch_kernel(
    norm_row,
    me_ref,
    back_ref,
    slot_ref,
    dy_ref,
    middle_ref,
    gain_ref,
    w_ref,
    att_ref,
    early_ref,
    grad_ref,
    heads_ref,
    keep_ref,
    send_ref,
    small_ref,
    acc,
):
    g = dg(one_hot_slots(slot_ref[...], back_ref.shape[0]), back_ref[...], 0, 0)
    v = middle_ref[...]
    centred = v - jnp.mean(v, axis=1, keepdims=True)
    rstd = lax.rsqrt(jnp.mean(centred * centred, axis=1, keepdims=True) + norm_eps)
    xh = centred * rstd
    dn = g * gain_ref[...]
    grad = rstd * (dn - jnp.mean(dn, axis=1, keepdims=True) - xh * jnp.mean(dn * xh, axis=1, keepdims=True))
    grad = dy_ref[...].astype(f32) + grad
    grad_ref[...] = grad
    low = grad.astype(bf16)
    heads_ref[...] = dg(w_ref[...], low, 1, 1).astype(bf16).reshape(heads_ref.shape)
    row = lax.broadcasted_iota(jnp.int32, small_ref.shape, 0)
    small = early_ref[...] + jnp.where(row == norm_row, jnp.sum(g * xh, axis=0, keepdims=True), 0.0)
    small_ref[...] = small
    acc[...] = dg(att_ref[...], low, 1, 0)
    nx, w, _ = keep_ref.shape
    for x in range(nx):
        keep_ref[x] = acc[pl.ds(pl.multiple_of((2 * x + me_ref[0]) * w, w), w)]
        send_ref[x * w : (x + 1) * w] = acc[pl.ds(pl.multiple_of((2 * x + 1 - me_ref[0]) * w, w), w)].astype(bf16)
    send_ref[nx * w :] = halves_of(small)


def whole_block(shape):
    return pl.BlockSpec(shape, lambda i, p: (0,) * len(shape))


def one_step(kernel, name, outs, args, scratch, flops):
    return pl.pallas_call(
        kernel,
        out_shape=tuple(jax.ShapeDtypeStruct(shape, dtype) for shape, dtype in outs),
        grid_spec=pltpu.PrefetchScalarGridSpec(
            num_scalar_prefetch=1,
            grid=(1,),
            in_specs=[whole_block(a.shape) for a in args[1:]],
            out_specs=tuple(whole_block(shape) for shape, _ in outs),
            scratch_shapes=scratch,
        ),
        compiler_params=pltpu.CompilerParams(vmem_limit_bytes=VMEM),
        cost_estimate=pl.CostEstimate(
            flops=flops, bytes_accessed=4 * sum(a.size for a in args), transcendentals=0
        ),
        name=name,
    )(*args)


def branch_back(ci, back, slot, dy, middle, gain, w, attT, early, norm_row, ctx):
    rows = dy.shape[0]
    mine = D // ctx
    outs = (
        ((rows, D), f32),
        ((ctx, HEADS // ctx, HD, rows), bf16),
        ((ctx // 2, mine, D), f32),
        ((ctx // 2 * mine + 2 * early.shape[0], D), bf16),
        (early.shape, f32),
    )
    return one_step(
        functools.partial(branch_kernel, norm_row),
        "branch_back",
        outs,
        (ci, back, slot, dy, middle, gain, w, attT, early),
        [pltpu.VMEM((D, D), f32)],
        2 * rows * D * (back.shape[0] + 2 * D),
    )


def go_kernel(me_ref, keep_ref, got_ref, small_ref, own_ref, send_ref, sum_ref, acc):
    nx, w, _ = keep_ref.shape
    for x in range(nx):
        acc[x] = keep_ref[x] + got_ref[x * w : (x + 1) * w].astype(f32)
    small = small_ref[...] + sum_halves(got_ref[nx * w :])
    sum_ref[...] = small
    own_ref[...] = acc[me_ref[0]]
    send_ref[:w] = acc[1 - me_ref[0]].astype(bf16)
    send_ref[w:] = halves_of(small)


def go_step(xi, keep, got, small):
    w = keep.shape[1]
    outs = (((w, D), f32), ((w + 2 * small.shape[0], D), bf16), (small.shape, f32))
    return one_step(go_kernel, "go_step", outs, (xi, keep, got, small), [pltpu.VMEM(keep.shape, f32)], 0)


def weight_rows_kernel(half_ref, dT_ref, normed_ref, go_ref, got_ref, early_ref, keep_ref, send_ref, small_ref, acc):
    n = dT_ref.shape[0]
    w = go_ref.shape[0]
    half = keep_ref.shape[0]
    acc[:n] = dg(dT_ref[...], normed_ref[...], 1, 0)
    acc[n:] = go_ref[...] + got_ref[:w].astype(f32)
    small = early_ref[...] + sum_halves(got_ref[w:])
    small_ref[...] = small
    a = pl.multiple_of(half_ref[0] * half, half)
    b = pl.multiple_of((1 - half_ref[0]) * half, half)
    keep_ref[...] = acc[pl.ds(a, half)]
    send_ref[:half] = acc[pl.ds(b, half)].astype(bf16)
    send_ref[half:] = halves_of(small)


def weight_rows(half, dT, normed, go, got, small):
    rows = dT.shape[0] + go.shape[0]
    outs = (((rows // 2, D), f32), ((rows // 2 + 2 * small.shape[0], D), bf16), (small.shape, f32))
    return one_step(
        weight_rows_kernel,
        "weight_rows",
        outs,
        (half, dT, normed, go, got, small),
        [pltpu.VMEM((rows, D), f32)],
        2 * dT.size * D,
    )


def share_kernel(me_ref, half_ref, got_ref, early_ref, own_ref, *refs):
    dp = len(refs) - 1
    sends, small_ref, acc = refs[: dp - 1], refs[dp - 1], refs[dp]
    half = half_ref.shape[0]
    w = half // dp
    acc[...] = half_ref[...] + got_ref[:half].astype(f32)
    small = early_ref[...] + sum_halves(got_ref[half:])
    small_ref[...] = small

    def share(step):
        return acc[pl.ds(pl.multiple_of(lax.rem(me_ref[0] + step, dp) * w, w), w)]

    own_ref[...] = share(0)
    for step in range(1, dp):
        sends[step - 1][:w] = share(step).astype(bf16)
        sends[step - 1][w:] = halves_of(small)


def share_step(zi, half, got, small, dp):
    w = half.shape[0] // dp
    outs = (((w, D), f32),) + (((w + 2 * small.shape[0], D), bf16),) * (dp - 1) + ((small.shape, f32),)
    return one_step(
        functools.partial(share_kernel),
        "share_step",
        outs,
        (zi, half, got, small),
        [pltpu.VMEM(half.shape, f32)],
        0,
    )


SIDE = tuple((core, over, begin) for core in range(2) for over in range(2) for begin in range(2))


def finish_kernel(dp, side, me_ref, *refs):
    layout = SIDE
    n = len(layout)
    pieces, weights, scale_ref, before_ref = refs[:n], refs[n : n + 3], refs[n + 3], refs[n + 4]
    outs, row_ref = refs[-11:-7], refs[-7]
    got, wide, held, in_sem, out_sem, w_sem = refs[-6:]
    mine = D // 4
    rows = 2 * mine // dp
    copies = []
    for k, (core, over, begin) in enumerate(layout):
        first = (over ^ me_ref[1]) * (2 * mine) + (core ^ me_ref[2]) * mine
        for i in range(pieces[k].shape[0] // rows):
            row = lax.rem(me_ref[0] + dp - begin * (dp // 2) - i, dp) * rows
            copy = pltpu.make_async_copy(
                pieces[k].at[pl.ds(i * rows, rows)],
                got.at[lax.div(row, mine), pl.ds(pl.multiple_of(first + lax.rem(row, mine), rows), rows)],
                in_sem.at[k, i],
            )
            copy.start()
            copies.append(copy)

    def put(pair):
        loads = [pltpu.make_async_copy(weights[p], held.at[k], w_sem.at[k]) for k, p in enumerate(pair) if p < 3]
        for copy in loads:
            copy.start()
        for copy in copies + loads:
            copy.wait()
        total = jnp.zeros((D, 1), f32)
        backs = []
        for k in (1, 0):
            if pair[k] < 3:
                g = got[k].T.astype(f32)
                total = total + jnp.sum(g * held[k].astype(f32), axis=1, keepdims=True)
            else:
                g = got[k].astype(f32)
            wide[k] = g
            back = pltpu.make_async_copy(wide.at[k], outs[pair[k]], out_sem.at[k])
            back.start()
            backs.append(back)
        row = jnp.broadcast_to(total, (D, 128)).T[:1]
        row_ref[...] = ((before_ref[...] + row) / scale_ref[...])[0] if side else row
        for back in backs:
            back.wait()

    y = lax.rem(me_ref[3] + side, 2)

    @pl.when(y == 0)
    def _():
        put((0, 1))

    @pl.when(y == 1)
    def _():
        put((2, 3))


def finish(me, pieces, weights, scale, side, so_far, dp):
    whole = jax.ShapeDtypeStruct((D, D), f32)
    anywhere = pl.BlockSpec(memory_space=pl.ANY)
    row = pl.BlockSpec((1, D), lambda i, p: (0, 0))
    args = [*pieces, *weights, scale, so_far[4] if side else scale]
    specs = [anywhere] * (len(args) - 2) + [row, row]
    alias = {}
    if side:
        alias = {1 + len(args) + p: p for p in range(4)}
        args += list(so_far[:4])
        specs += [anywhere] * 4
    return pl.pallas_call(
        functools.partial(finish_kernel, dp, side),
        out_shape=(whole,) * 4 + (jax.ShapeDtypeStruct((D,) if side else (1, D), f32),),
        grid_spec=pltpu.PrefetchScalarGridSpec(
            num_scalar_prefetch=1,
            grid=(1,),
            in_specs=specs,
            out_specs=(anywhere,) * 4 + (pl.BlockSpec((D,), lambda i, p: (0,)) if side else row,),
            scratch_shapes=[
                pltpu.VMEM((2, D, D), bf16),
                pltpu.VMEM((2, D, D), f32),
                pltpu.VMEM((2, D, D), bf16),
                pltpu.SemaphoreType.DMA((len(pieces), dp)),
                pltpu.SemaphoreType.DMA((2,)),
                pltpu.SemaphoreType.DMA((2,)),
            ],
        ),
        input_output_aliases=alias,
        compiler_params=pltpu.CompilerParams(vmem_limit_bytes=VMEM),
        cost_estimate=pl.CostEstimate(flops=4 * D * D, bytes_accessed=16 * D * D, transcendentals=0),
        name=f"finish{side}",
    )(me, *args)


def swap(v, axis):
    return lax.ppermute(v, axis, [(0, 1), (1, 0)])


def shift(v, axis, step):
    n = lax.axis_size(axis)
    return lax.ppermute(v, axis, [(i, (i + step) % n) for i in range(n)])


def at(v, index):
    return lax.dynamic_index_in_dim(v, index, 0, keepdims=False)


def one(v):
    v = v.astype(f32)
    n = v.shape[0] // 2
    return v[:n] + v[n:]


def add_pair(v):
    return v + (swap(v, "expert") if lax.axis_size("expert") == 2 else lax.psum(v, "expert") - v)


def add_shifts(v):
    out = v
    for s in range(1, lax.axis_size("dp")):
        out = out + shift(v, "dp", s)
    return out


def index(i):
    return i.astype(jnp.int32).reshape(1)


def tie(*arrays):
    return lax.optimization_barrier(arrays)


def normal_form(v):
    centred = v - jnp.mean(v, axis=-1, keepdims=True)
    rstd = lax.rsqrt(jnp.mean(centred * centred, axis=-1, keepdims=True) + norm_eps)
    return centred * rstd, rstd


def norm_back(dn, xh, rstd):
    return rstd * (dn - jnp.mean(dn, axis=-1, keepdims=True) - xh * jnp.mean(dn * xh, axis=-1, keepdims=True))


def per_device(
    tokens,
    cotangent,
    routes,
    norm1_gain,
    w_query,
    w_key,
    w_value,
    w_output,
    norm2_gain,
    w_router,
    w_in,
    w_out,
):
    rows = tokens.shape[1]
    nx, owners, dp = lax.axis_size("x"), lax.axis_size("expert"), lax.axis_size("dp")
    xi, ci, ei = lax.axis_index("x"), lax.axis_index("core"), lax.axis_index("expert")
    ctx = 2 * nx
    ctx_i = xi * 2 + ci
    length = ctx * rows
    experts = w_router.shape[1]
    cap = 2 * rows // experts
    mine = D // ctx
    heads = mine // HD
    expert_id = ei * nx + xi
    pick = jnp.stack([xi, ci, expert_id]).astype(jnp.int32)

    tok = tokens.reshape(rows, D)
    flat = tok.astype(f32)
    other = swap(tok, "x")
    near = swap(tok, "core")

    route = routes.reshape(rows)
    hot = (route[:, None] == jnp.arange(128, dtype=jnp.int32)[None, :]).astype(f32)
    lower = jnp.arange(rows)[:, None] >= jnp.arange(rows)[None, :]
    before = dg(lower.astype(bf16), hot.astype(bf16), 1, 0)
    rank = (jnp.sum(before * hot, axis=1) - 1.0).astype(jnp.int32)
    slot = ((route % nx) * owners + route // nx) * cap + rank
    spread = (jnp.arange(experts * cap, dtype=jnp.int32)[:, None] == slot[None, :]).astype(bf16)

    def pack(v):
        return dg(spread, v, 1, 0).astype(bf16).reshape(nx * owners, cap, D)

    def trade(v):
        v = lax.all_to_all(v.reshape(nx * owners, cap, D), ("x", "expert"), split_axis=0, concat_axis=0, tiled=True)
        return v.reshape(-1, D)

    def turn(v):
        return lax.all_to_all(v, ("x", "core"), split_axis=0, concat_axis=0, tiled=True)

    def cut(w):
        return lax.dynamic_slice(w, (0, ctx_i * mine), (D, mine))

    w_own = jnp.concatenate([cut(w_query), cut(w_key), cut(w_value)], axis=1)
    gain1 = norm1_gain.reshape(1, D)
    dy_low = cotangent.reshape(rows, D)
    dy = dy_low.astype(f32)
    wr = lax.dynamic_slice(w_router, (0, expert_id), (D, 1)).astype(f32).reshape(1, D)
    counts = jnp.sum(hot, axis=0, keepdims=True)
    counts = counts + swap(counts, "core")
    counts = add_pair(counts)
    so_far = project([ctx_i], [tok], gain1, w_own, ctx, None)
    counts, dy_packed, *so_far = tie(counts, pack(dy_low), *so_far)
    so_far = project([ctx_i ^ 1], [near], gain1, w_own, ctx, so_far)
    other, dy_packed, *so_far = tie(other, dy_packed, *so_far)
    far = swap(other, "core")
    dy_rows = trade(dy_packed)
    normed_all, qkvT, kv = project([ctx_i ^ 2, ctx_i ^ 3], [other, far], gain1, w_own, ctx, so_far)
    oT, osend, lse = attend(qkvT, kv, ctx)
    osend, dy_rows, counts = tie(osend, dy_rows, counts)
    attT = turn(osend)
    counts = add_shifts(counts)
    attT, counts = tie(attT, counts)
    counts = counts + swap(counts, "x")
    attT = attT.reshape(D, rows)
    mean_load = rows * ctx * dp * owners / experts
    gain2 = norm2_gain.reshape(1, D)
    middle, second, packed = middle_step(attT, tok, w_output, gain2, slot[None], nx * owners, cap)
    gating = jax.nn.sigmoid(jnp.sum(hot[:, :experts] * dg(second, w_router, 1, 0), axis=1))

    up = expert_up(pick, dy_rows, w_out)
    sig = jnp.pad(jnp.sum(hot[:, :experts] * gating[:, None], axis=0), (0, D - experts))
    counts, packed = tie(counts, packed)
    x_rows = trade(packed)
    x_rows, gating, sig, slot, gain2 = tie(x_rows, gating, sig, slot[None], gain2)
    active, grad_hidden, back_rows, router_row, gate = expert_mid(pick, x_rows, up, w_in, wr, counts, mean_load)
    returned = trade(back_rows)
    keep, send, produced = expert_grads(pick, x_rows, dy_rows, gate, active, grad_hidden, w_out, dp, nx)
    returned, keep, send, produced = tie(returned, keep, send, produced)
    taken = swap(send, "core")
    zi = lax.axis_index("dp")

    def chunk(i):
        return at(keep, (i + dp) % dp).astype(f32) + at(taken, (i + dp) % dp).astype(f32)

    def ring(moving, step):
        return (shift(moving, "dp", 1).astype(f32) + chunk(zi - 2 - step)).astype(bf16)

    def side(v, x):
        return lax.dynamic_index_in_dim(v, x, 1, keepdims=False)

    router_rows = (jnp.arange(experts) == expert_id).astype(f32)[:, None] * router_row
    small = jnp.concatenate([router_rows, jnp.zeros((1, D), f32), sig[None]], axis=0)
    small = jnp.pad(small, ((0, -small.shape[0] % 8), (0, 0)))
    grad_middle, heads_grad, go, go_send, small = branch_back(
        index(ci), returned, slot, dy_low, middle, gain2, w_output, attT, small, experts, ctx
    )
    do = turn(heads_grad)

    moving = ring(chunk(zi - 1).astype(bf16), 0)
    go_got = swap(go_send, "core")
    go, go_send, small = go_step(index(xi), go, go_got, small)
    do, go_send = tie(do, go_send)
    go_got = swap(go_send, "x")

    so_far = attend_back(qkvT, kv, do, 0, oT, lse, 0, None)
    produced, go_got, *so_far = tie(produced, go_got, *so_far)
    went_back = trade(produced)
    so_far = attend_back(qkvT, kv, do, 1, oT, lse, 1, so_far)
    moving, *so_far = tie(moving, *so_far)
    moving = ring(moving, 1)
    for h in range(2, heads):
        so_far = attend_back(qkvT, kv, do, h, oT, lse, h, so_far)
    went_back, dT, dsend = tie(went_back, *so_far)
    output = (middle + gating[:, None] * dg(spread, went_back, 0, 0)).astype(bf16)

    ei2 = ei if owners == 2 else jnp.zeros_like(ei)
    half, send, small = weight_rows(index(ei2), dT.reshape(3 * mine, length), normed_all, go, go_got, small)
    dsend, send = tie(dsend, send)
    got = turn(dsend)
    if owners == 2:
        gift = swap(send, "expert")
        gift, moving = tie(gift, moving)
        halves = [(half, gift)]
    else:
        cut_at = half.shape[0]
        small = lax.psum(small, "expert")
        nothing = jnp.zeros_like(send)
        halves = [(lax.psum(half, "expert"), nothing), (lax.psum(send[:cut_at].astype(f32), "expert"), nothing)]
    pieces = []
    for part, gift in halves:
        share, *gifts, more = share_step(index(zi), part, gift, small, dp)
        gifts = [shift(gift, "dp", step + 1) for step, gift in enumerate(gifts)]
        for gift in gifts:
            more = more + one(gift[share.shape[0] :])
            share = share + gift[: share.shape[0]].astype(f32)
        share = share.astype(bf16)
        shares = [share] + [shift(share, "dp", step) for step in range(1, dp)]
        pieces.append([jnp.concatenate(shares[k : k + dp // 2], axis=0) for k in range(0, dp, dp // 2)])
    small = more
    output, keep, taken = tie(output, keep, taken)
    crossed = swap(side(chunk(zi), 1 - xi).astype(bf16), "x")
    for step in range(2, dp - 2):
        moving = ring(moving, step)
    moving, crossed, *pieces = tie(moving, crossed, *pieces)
    own = shift(side(moving, xi), "dp", 1)
    route_on = [(z * nx + x, (z + 1) % dp * nx + 1 - x) for z in range(dp) for x in range(nx)]
    theirs = side(moving, 1 - xi)

    grad_normed = 0.0
    for p, w in enumerate((w_query, w_key, w_value)):
        grad_normed = grad_normed + dg(got[:, p].reshape(D, rows), w, 0, 1)
    xh1, rstd1 = normal_form(flat)
    grad_tokens = grad_middle + norm_back(grad_normed * norm1_gain, xh1, rstd1)

    near_pieces = pieces[0]
    beyond = [swap(piece, "x") for piece in near_pieces]
    if owners == 2:
        across = [swap(piece, "expert") for piece in near_pieces]
    else:
        across = list(pieces[1])
    theirs, *rest = tie(theirs, *beyond, *across)
    beyond, across = rest[:2], rest[2:]
    moved = lax.ppermute(theirs, ("dp", "x"), route_on)
    if owners == 2:
        corner = [swap(piece, "expert") for piece in beyond]
    else:
        corner = [swap(piece, "x") for piece in across]
    me = jnp.stack([zi, xi, ci, ei2]).astype(jnp.int32)
    projections = (w_query, w_key, w_value)
    near_pieces = near_pieces + beyond
    near_pieces += [swap(piece, "core") for piece in near_pieces]
    placed = finish(me, near_pieces, projections, gain1, 0, None, dp)
    own, grad_tokens, *corner = tie(own, grad_tokens, *corner, *placed)
    corner, placed = corner[:2], corner[2:]
    far_pieces = across + corner
    far_pieces += [swap(piece, "core") for piece in far_pieces]
    *grads, grad_norm1 = finish(me, far_pieces, projections, gain1, 1, placed, dp)
    moved, grad_norm1 = tie(moved, grad_norm1)

    own = own.astype(f32) + side(chunk(zi), xi)
    moved = moved.astype(f32) + crossed.astype(f32)
    first, latter = jnp.where(xi == 0, own, moved), jnp.where(xi == 0, moved, own)
    both = jnp.stack([first, latter], axis=1)
    grad_in = jnp.swapaxes(both[0], 1, 2)
    grad_out = both[1]

    grad_router = jnp.transpose(small[:experts])
    grad_norm2 = small[experts]
    total_sig = small[experts + 1, :experts]
    counts = counts[0, :experts]
    balance = balance_weight * jnp.sum((counts - mean_load) / mean_load * total_sig) / mean_load

    return (
        output.reshape(1, rows, D),
        grad_tokens.reshape(1, rows, D),
        grad_norm1,
        grads[0],
        grads[1],
        grads[2],
        grads[3],
        grad_norm2,
        grad_router,
        grad_in,
        grad_out,
        balance,
    )


def solution(mesh):
    dp, ctx, owners = mesh.shape["dp"], mesh.shape["ctx"], mesh.shape["expert"]
    split = Mesh(mesh.devices.reshape(dp, ctx // 2, 2, owners), ("dp", "x", "core", "expert"))
    token = P(("dp", "expert"), ("x", "core"), None)
    return jax.shard_map(
        per_device,
        mesh=split,
        in_specs=(token, token, token, P(), P(), P(), P(), P(), P(), P(), P("expert"), P("expert")),
        out_specs=(
            token,
            token,
            P(),
            P(),
            P(),
            P(),
            P(),
            P(),
            P(),
            P("expert", None, ("dp", "x", "core")),
            P("expert", ("dp", "x", "core"), None),
            P(),
        ),
        check_vma=False,
    )
```

```python
import functools

import jax
import jax.numpy as jnp
from jax import lax
from jax.experimental import pallas as pl
from jax.experimental.pallas import tpu as pltpu
from jax.sharding import Mesh
from jax.sharding import PartitionSpec as P

D = 768
HEADS = 12
HD = 64
norm_eps = 1e-05
balance_weight = 1.0
LOG2E = 1.4426950408889634
MASKED = -1e30
GELU_A = 0.7978845608028654
GELU_B = 0.044715
VMEM = 56 * 1024 * 1024
f32 = jnp.float32
bf16 = jnp.bfloat16


def dg(a, b, ca, cb):
    return lax.dot_general(a, b, (((ca,), (cb,)), ((), ())), preferred_element_type=f32)


def project_kernel(place_ref, *refs):
    normed_ref, qkvT_ref, kv_ref = refs[-3:]
    blocks = place_ref.shape[0]
    gain_ref, w_ref = refs[blocks : blocks + 2]

    def work(tok_ref):
        x = tok_ref[...].astype(f32)
        centred = x - jnp.mean(x, axis=1, keepdims=True)
        rstd = lax.rsqrt(jnp.mean(centred * centred, axis=1, keepdims=True) + norm_eps)
        normed = (centred * rstd * gain_ref[...]).astype(bf16)
        normed_ref[...] = normed
        qkv = dg(normed, w_ref[...], 1, 0).astype(bf16)
        kv_ref[...] = qkv[:, qkv.shape[1] - kv_ref.shape[1] :]
        qkvT_ref[...] = qkv.T

    for k in range(blocks):

        @pl.when(pl.program_id(0) == k)
        def _():
            work(refs[k])


def project(places, toks, gain, w, ctx, so_far):
    rows = toks[0].shape[0]
    wide = w.shape[1]
    args = [*toks, gain, w]
    specs = [pl.BlockSpec(a.shape, lambda i, p: (0, 0)) for a in args]
    alias = {}
    if so_far is not None:
        alias = {1 + len(args) + k: k for k in range(3)}
        args += list(so_far)
        specs += [pl.BlockSpec(memory_space=pl.ANY)] * 3
    return pl.pallas_call(
        project_kernel,
        out_shape=(
            jax.ShapeDtypeStruct((ctx * rows, D), bf16),
            jax.ShapeDtypeStruct((wide, ctx * rows), bf16),
            jax.ShapeDtypeStruct((ctx * rows, 2 * wide // 3), bf16),
        ),
        grid_spec=pltpu.PrefetchScalarGridSpec(
            num_scalar_prefetch=1,
            grid=(len(toks),),
            in_specs=specs,
            out_specs=(
                pl.BlockSpec((rows, D), lambda i, p: (p[i], 0)),
                pl.BlockSpec((wide, rows), lambda i, p: (0, p[i])),
                pl.BlockSpec((rows, 2 * wide // 3), lambda i, p: (p[i], 0)),
            ),
        ),
        input_output_aliases=alias,
        compiler_params=pltpu.CompilerParams(vmem_limit_bytes=VMEM),
        cost_estimate=pl.CostEstimate(
            flops=4 * len(toks) * rows * D * wide, bytes_accessed=4 * rows * D + 8 * rows * wide, transcendentals=0
        ),
        name="project",
    )(jnp.stack(places).astype(jnp.int32), *args)


def attend_kernel(heads, blk, qT_ref, k_ref, vT_ref, oT_ref, osend_ref, lse_ref):
    length = qT_ref.shape[1]
    per = osend_ref.shape[3]
    c = (HD**-0.5) * LOG2E
    rows = lax.broadcasted_iota(jnp.int32, (blk, blk), 0)
    cols = lax.broadcasted_iota(jnp.int32, (blk, blk), 1)
    keep = rows <= cols
    for h in range(heads):
        hs = slice(h * HD, (h + 1) * HD)
        for i in range(length // blk):
            a, b = i * blk, (i + 1) * blk
            q = qT_ref[hs, a:b]
            sd = dg(k_ref[a:b, hs], q, 1, 0)
            sd = jnp.where(keep, sd, MASKED)
            m = jnp.max(sd, axis=0, keepdims=True)
            if i:
                s = dg(k_ref[:a, hs], q, 1, 0)
                m = jnp.maximum(m, jnp.max(s, axis=0, keepdims=True))
            mc = m * c
            pd = jnp.exp2(sd * c - mc)
            total = jnp.sum(pd, axis=0, keepdims=True)
            o = dg(vT_ref[hs, a:b], pd.astype(bf16), 1, 0)
            if i:
                p = jnp.exp2(s * c - mc)
                total = total + jnp.sum(p, axis=0, keepdims=True)
                o = o + dg(vT_ref[hs, :a], p.astype(bf16), 1, 0)
            o = o / total
            oT_ref[hs, a:b] = o
            d, off = a // per, a % per
            osend_ref[d, h, :, off : off + blk] = o.astype(bf16)
            lse_ref[h, :, a:b] = mc + jnp.log2(total)


def attend(qkvT, kv, dests):
    length = kv.shape[0]
    heads = qkvT.shape[0] // (3 * HD)
    wide = heads * HD
    per = length // dests
    return pl.pallas_call(
        functools.partial(attend_kernel, heads, per),
        out_shape=(
            jax.ShapeDtypeStruct((wide, length), f32),
            jax.ShapeDtypeStruct((dests, heads, HD, per), bf16),
            jax.ShapeDtypeStruct((heads, 1, length), f32),
        ),
        grid=(1,),
        in_specs=[
            pl.BlockSpec((wide, length), lambda i: (0, 0)),
            pl.BlockSpec(kv.shape, lambda i: (0, 0)),
            pl.BlockSpec((wide, length), lambda i: (2, 0)),
        ],
        out_specs=(
            pl.BlockSpec((wide, length), lambda i: (0, 0)),
            pl.BlockSpec((dests, heads, HD, per), lambda i: (0, 0, 0, 0)),
            pl.BlockSpec((heads, 1, length), lambda i: (0, 0, 0)),
        ),
        compiler_params=pltpu.CompilerParams(vmem_limit_bytes=VMEM),
        cost_estimate=pl.CostEstimate(
            flops=8 * heads * length * length * HD,
            bytes_accessed=length * wide * 14,
            transcendentals=heads * length * length // 2,
        ),
        name="attend",
    )(qkvT, kv, qkvT)


def attend_back_kernel(lk, lv, blk, *refs):
    qT_ref, k_ref, kT_ref, v_ref, do_ref, oT_ref, lse_ref = refs[:7]
    dT_ref, dsend_ref, dk_acc, dv_acc = refs[-4:]
    length = qT_ref.shape[1]
    per = do_ref.shape[3]
    sc = HD**-0.5
    c = sc * LOG2E
    rows = lax.broadcasted_iota(jnp.int32, (blk, blk), 0)
    cols = lax.broadcasted_iota(jnp.int32, (blk, blk), 1)
    keep = rows <= cols
    n = length // blk
    for i in reversed(range(n)):
        x0, x1 = i * blk, (i + 1) * blk
        d, off = x0 // per, x0 % per
        q = qT_ref[:, x0:x1]
        do = do_ref[d, 0, :, off : off + blk]
        lse = lse_ref[0, :, x0:x1]
        delta = jnp.sum(do.astype(f32) * oT_ref[:, x0:x1], axis=0, keepdims=True)
        dq = None
        for a, b, diag in ([(0, x0, False)] if i else []) + [(x0, x1, True)]:
            s = dg(k_ref[a:b, lk : lk + HD], q, 1, 0)
            p = jnp.exp2(s * c - lse)
            if diag:
                p = jnp.where(keep, p, 0.0)
            dp = dg(v_ref[a:b, lv : lv + HD], do, 1, 0)
            ds = (p * (dp - delta)).astype(bf16)
            dvn = dg(do, p.astype(bf16), 1, 1)
            dkn = dg(q, ds, 1, 1)
            if i == n - 1:
                dv_acc[:, a:b] = dvn
                dk_acc[:, a:b] = dkn
            else:
                dv_acc[:, a:b] += dvn
                dk_acc[:, a:b] += dkn
            t = dg(kT_ref[:, a:b], ds, 1, 0)
            dq = t if dq is None else dq + t
        dq = (dq * sc).astype(bf16)
        dT_ref[0, :, x0:x1] = dq
        dsend_ref[d, 0, :, off : off + blk] = dq
    for d in range(dsend_ref.shape[0]):
        at_d = slice(d * per, (d + 1) * per)
        dk = (dk_acc[:, at_d] * sc).astype(bf16)
        dv = dv_acc[:, at_d].astype(bf16)
        dT_ref[1, :, at_d] = dk
        dT_ref[2, :, at_d] = dv
        dsend_ref[d, 1] = dk
        dsend_ref[d, 2] = dv


def attend_back(qkvT, kv, do, slot, oT, lse, h, so_far):
    length = kv.shape[0]
    n = qkvT.shape[0] // (3 * HD)
    dests, _, _, per = do.shape
    hv = n + h
    blk = min(256, per)
    args = [qkvT, kv, qkvT, kv, do, oT, lse]
    specs = [
        pl.BlockSpec((HD, length), lambda i: (h, 0)),
        pl.BlockSpec((length, 2 * HD), lambda i: (0, h // 2)),
        pl.BlockSpec((HD, length), lambda i: (n + h, 0)),
        pl.BlockSpec((length, 2 * HD), lambda i: (0, hv // 2)),
        pl.BlockSpec((dests, 1, HD, per), lambda i: (0, slot, 0, 0)),
        pl.BlockSpec((HD, length), lambda i: (h, 0)),
        pl.BlockSpec((1, 1, length), lambda i: (h, 0, 0)),
    ]
    alias = {}
    if so_far is not None:
        alias = {len(args): 0, len(args) + 1: 1}
        args += list(so_far)
        specs += [pl.BlockSpec(memory_space=pl.ANY)] * 2
    return pl.pallas_call(
        functools.partial(attend_back_kernel, (h % 2) * HD, (hv % 2) * HD, blk),
        out_shape=(
            jax.ShapeDtypeStruct((3, n * HD, length), bf16),
            jax.ShapeDtypeStruct((dests, 3, n * HD, per), bf16),
        ),
        grid=(1,),
        in_specs=specs,
        out_specs=(
            pl.BlockSpec((3, HD, length), lambda i: (0, h, 0)),
            pl.BlockSpec((dests, 3, HD, per), lambda i: (0, 0, h, 0)),
        ),
        scratch_shapes=[pltpu.VMEM((HD, length), f32)] * 2,
        input_output_aliases=alias,
        compiler_params=pltpu.CompilerParams(vmem_limit_bytes=VMEM),
        cost_estimate=pl.CostEstimate(
            flops=20 * length * length * HD, bytes_accessed=length * HD * 24, transcendentals=length * length // 2
        ),
        name=f"attend_back_head{h}",
    )(*args)


def middle_kernel(me_ref, att_ref, tok_ref, w_ref, gain_ref, slot_ref, middle_ref, second_ref, packed_ref):
    v = tok_ref[...].astype(f32) + dg(att_ref[...], w_ref[...], 0, 0)
    middle_ref[...] = v
    centred = v - jnp.mean(v, axis=1, keepdims=True)
    rstd = lax.rsqrt(jnp.mean(centred * centred, axis=1, keepdims=True) + norm_eps)
    second = (centred * rstd * gain_ref[...]).astype(bf16)
    second_ref[...] = second
    spread = one_hot_slots(slot_ref[...], packed_ref.shape[0] * packed_ref.shape[1])
    packed_ref[...] = dg(spread, second, 1, 0).astype(bf16).reshape(packed_ref.shape)


def middle_step(attT, tok, w, gain, slot, sources, cap):
    rows = tok.shape[0]
    outs = (((rows, D), f32), ((rows, D), bf16), ((sources, cap, D), bf16))
    return one_step(
        middle_kernel,
        "middle_step",
        outs,
        (jnp.zeros((1,), jnp.int32), attT, tok, w, gain, slot),
        [],
        2 * rows * D * (D + sources * cap),
    )


def up_kernel(pick_ref, dy_ref, wo_ref, u_ref):
    u_ref[...] = dg(dy_ref[...], wo_ref[0], 1, 1).astype(bf16)


def expert_up(pick, dy, w_out, fc=768):
    rows = dy.shape[0]
    ff = w_out.shape[1]
    return pl.pallas_call(
        up_kernel,
        out_shape=jax.ShapeDtypeStruct((rows, ff), bf16),
        grid_spec=pltpu.PrefetchScalarGridSpec(
            num_scalar_prefetch=1,
            grid=(ff // fc,),
            in_specs=[
                pl.BlockSpec((rows, D), lambda f, p: (0, 0)),
                pl.BlockSpec((1, fc, D), lambda f, p: (p[0], f, 0)),
            ],
            out_specs=pl.BlockSpec((rows, fc), lambda f, p: (0, f)),
        ),
        compiler_params=pltpu.CompilerParams(vmem_limit_bytes=VMEM),
        cost_estimate=pl.CostEstimate(
            flops=2 * rows * D * ff, bytes_accessed=2 * (rows * D + ff * D + rows * ff), transcendentals=0
        ),
        name="expert_up",
    )(pick, dy, w_out)


def mid_kernel(
    mean, pick_ref, x_ref, u_ref, wi_ref, wr_ref, count_ref, act_ref, gh_ref, rows_ref, router_ref, gate_ref, acc, gg, gate
):
    f = pl.program_id(0)
    n = pl.num_programs(0)

    @pl.when(f == 0)
    def _():
        logit = jnp.sum(x_ref[...].astype(f32) * wr_ref[...], axis=1, keepdims=True)
        gate[...] = jnp.broadcast_to(jax.nn.sigmoid(logit), gate.shape)
        acc[...] = jnp.zeros_like(acc)
        gg[...] = jnp.zeros_like(gg)

    step = 256
    for r in range(0, x_ref.shape[0], step):
        rs = slice(r, r + step)
        for c in range(0, wi_ref.shape[2], step):
            cs = slice(c, c + step)
            h = dg(x_ref[rs], wi_ref[0, :, cs], 1, 0)
            h2 = h * h
            t = jnp.tanh(h * (GELU_A + (GELU_A * GELU_B) * h2))
            hp = 0.5 + 0.5 * t
            dgelu = hp + (h * (hp - hp * hp)) * (2.0 * GELU_A + (6.0 * GELU_A * GELU_B) * h2)
            u = u_ref[rs, cs].astype(f32)
            active = h * hp
            act_ref[rs, cs] = active.astype(bf16)
            au = active * u
            lanes = au[:, :128]
            for j in range(128, step, 128):
                lanes = lanes + au[:, j : j + 128]
            gg[rs] += lanes
            gh = (gate[rs, :1] * (u * dgelu)).astype(bf16)
            gh_ref[rs, cs] = gh
            acc[rs] += dg(gh, wi_ref[0, :, cs], 1, 1)

    @pl.when(f == n - 1)
    def _():
        g = gate[:, :1]
        got = jnp.sum(gg[...], axis=1, keepdims=True)
        lane = lax.broadcasted_iota(jnp.int32, count_ref.shape, 1)
        count = jnp.sum(jnp.where(lane == pick_ref[2], count_ref[...], 0.0), axis=1, keepdims=True)
        load = balance_weight * (count - mean) / (mean * mean)
        sel = (g * (1.0 - g) * (got + load)).astype(bf16).astype(f32)
        rows_ref[...] = (acc[...] + sel * wr_ref[...]).astype(bf16)
        router_ref[...] = jnp.sum(x_ref[...].astype(f32) * sel, axis=0, keepdims=True)
        gate_ref[...] = gate[...]


def expert_mid(pick, x, u, w_in, wr, counts, mean, fc=768):
    rows = x.shape[0]
    ff = w_in.shape[2]

    def full(s):
        return pl.BlockSpec(s, lambda f, p: (0, 0))

    wide = pl.BlockSpec((rows, fc), lambda f, p: (0, f))
    return pl.pallas_call(
        functools.partial(mid_kernel, mean),
        out_shape=(
            jax.ShapeDtypeStruct((rows, ff), bf16),
            jax.ShapeDtypeStruct((rows, ff), bf16),
            jax.ShapeDtypeStruct((rows, D), bf16),
            jax.ShapeDtypeStruct((1, D), f32),
            jax.ShapeDtypeStruct((rows, 128), f32),
        ),
        grid_spec=pltpu.PrefetchScalarGridSpec(
            num_scalar_prefetch=1,
            grid=(ff // fc,),
            in_specs=[
                full((rows, D)),
                wide,
                pl.BlockSpec((1, D, fc), lambda f, p: (p[0], 0, f)),
                full((1, D)),
                full((1, 128)),
            ],
            out_specs=(wide, wide, full((rows, D)), full((1, D)), full((rows, 128))),
            scratch_shapes=[
                pltpu.VMEM((rows, D), f32),
                pltpu.VMEM((rows, 128), f32),
                pltpu.VMEM((rows, 128), f32),
            ],
        ),
        compiler_params=pltpu.CompilerParams(vmem_limit_bytes=VMEM),
        cost_estimate=pl.CostEstimate(
            flops=4 * rows * D * ff,
            bytes_accessed=2 * (3 * rows * D + ff * D + 3 * rows * ff),
            transcendentals=rows * ff,
        ),
        name="expert_mid",
    )(pick, x, u, w_in, wr, counts)


def grads_kernel(
    pick_ref, x_ref, dy_ref, gate_ref, act_ref, gh_ref, wo_ref, keep_ref, send_ref, prod_ref, acc, go, gi, gexp
):
    f = pl.program_id(0)
    n = pl.num_programs(0)

    @pl.when(f == 0)
    def _():
        gexp[...] = (dy_ref[...].astype(f32) * gate_ref[:, :1]).astype(bf16)

    go[...] = dg(act_ref[...], gexp[...], 0, 0).astype(bf16)
    gi[...] = dg(gh_ref[...], x_ref[...], 0, 0).astype(bf16)
    part = dg(act_ref[...], wo_ref[0], 1, 0)

    @pl.when(f == 0)
    def _():
        acc[...] = part

    @pl.when(f > 0)
    def _():
        acc[...] += part

    w = keep_ref.shape[3]
    me = pick_ref[1]
    for xx in range(keep_ref.shape[2]):
        a = pl.multiple_of((2 * xx + me) * w, w)
        b = pl.multiple_of((2 * xx + 1 - me) * w, w)
        keep_ref[0, 0, xx] = gi[pl.ds(a, w)]
        keep_ref[0, 1, xx] = go[pl.ds(a, w)]
        send_ref[0, 0, xx] = gi[pl.ds(b, w)]
        send_ref[0, 1, xx] = go[pl.ds(b, w)]

    @pl.when(f == n - 1)
    def _():
        prod_ref[...] = acc[...].astype(bf16)


def expert_grads(pick, x, dy, gate, act, gh, w_out, dp, nx):
    rows = x.shape[0]
    ff = w_out.shape[1]
    fc = ff // dp
    w = fc // (2 * nx)

    def full(s):
        return pl.BlockSpec(s, lambda f, p: (0, 0))

    wide = pl.BlockSpec((rows, fc), lambda f, p: (0, f))
    part = jax.ShapeDtypeStruct((dp, 2, nx, w, D), bf16)
    part_spec = pl.BlockSpec((1, 2, nx, w, D), lambda f, p: (f, 0, 0, 0, 0))
    return pl.pallas_call(
        grads_kernel,
        out_shape=(part, part, jax.ShapeDtypeStruct((rows, D), bf16)),
        grid_spec=pltpu.PrefetchScalarGridSpec(
            num_scalar_prefetch=1,
            grid=(dp,),
            in_specs=[
                full((rows, D)),
                full((rows, D)),
                full((rows, 128)),
                wide,
                wide,
                pl.BlockSpec((1, fc, D), lambda f, p: (p[0], f, 0)),
            ],
            out_specs=(part_spec, part_spec, full((rows, D))),
            scratch_shapes=[
                pltpu.VMEM((rows, D), f32),
                pltpu.VMEM((fc, D), bf16),
                pltpu.VMEM((fc, D), bf16),
                pltpu.VMEM((rows, D), bf16),
            ],
        ),
        compiler_params=pltpu.CompilerParams(vmem_limit_bytes=VMEM),
        cost_estimate=pl.CostEstimate(
            flops=6 * rows * D * ff,
            bytes_accessed=2 * (3 * rows * D + 3 * ff * D + 2 * rows * ff),
            transcendentals=0,
        ),
        name="expert_grads",
    )(pick, x, dy, gate, act, gh, w_out)


def one_hot_slots(slot, slots):
    return (lax.broadcasted_iota(jnp.int32, (slots, slot.shape[1]), 0) == slot).astype(f32).astype(bf16)


def halves_of(v):
    high = v.astype(bf16)
    return jnp.concatenate([high, (v - high.astype(f32)).astype(bf16)], axis=0)


def sum_halves(v):
    v = v.astype(f32)
    n = v.shape[0] // 2
    return v[:n] + v[n:]


def branch_kernel(
    norm_row,
    me_ref,
    back_ref,
    slot_ref,
    dy_ref,
    middle_ref,
    gain_ref,
    w_ref,
    att_ref,
    early_ref,
    grad_ref,
    heads_ref,
    keep_ref,
    send_ref,
    small_ref,
    acc,
):
    g = dg(one_hot_slots(slot_ref[...], back_ref.shape[0]), back_ref[...], 0, 0)
    v = middle_ref[...]
    centred = v - jnp.mean(v, axis=1, keepdims=True)
    rstd = lax.rsqrt(jnp.mean(centred * centred, axis=1, keepdims=True) + norm_eps)
    xh = centred * rstd
    dn = g * gain_ref[...]
    grad = rstd * (dn - jnp.mean(dn, axis=1, keepdims=True) - xh * jnp.mean(dn * xh, axis=1, keepdims=True))
    grad = dy_ref[...].astype(f32) + grad
    grad_ref[...] = grad
    low = grad.astype(bf16)
    heads_ref[...] = dg(w_ref[...], low, 1, 1).astype(bf16).reshape(heads_ref.shape)
    row = lax.broadcasted_iota(jnp.int32, small_ref.shape, 0)
    small = early_ref[...] + jnp.where(row == norm_row, jnp.sum(g * xh, axis=0, keepdims=True), 0.0)
    small_ref[...] = small
    acc[...] = dg(att_ref[...], low, 1, 0)
    nx, w, _ = keep_ref.shape
    for x in range(nx):
        keep_ref[x] = acc[pl.ds(pl.multiple_of((2 * x + me_ref[0]) * w, w), w)]
        send_ref[x * w : (x + 1) * w] = acc[pl.ds(pl.multiple_of((2 * x + 1 - me_ref[0]) * w, w), w)].astype(bf16)
    send_ref[nx * w :] = halves_of(small)


def whole_block(shape):
    return pl.BlockSpec(shape, lambda i, p: (0,) * len(shape))


def one_step(kernel, name, outs, args, scratch, flops):
    return pl.pallas_call(
        kernel,
        out_shape=tuple(jax.ShapeDtypeStruct(shape, dtype) for shape, dtype in outs),
        grid_spec=pltpu.PrefetchScalarGridSpec(
            num_scalar_prefetch=1,
            grid=(1,),
            in_specs=[whole_block(a.shape) for a in args[1:]],
            out_specs=tuple(whole_block(shape) for shape, _ in outs),
            scratch_shapes=scratch,
        ),
        compiler_params=pltpu.CompilerParams(vmem_limit_bytes=VMEM),
        cost_estimate=pl.CostEstimate(
            flops=flops, bytes_accessed=4 * sum(a.size for a in args), transcendentals=0
        ),
        name=name,
    )(*args)


def branch_back(ci, back, slot, dy, middle, gain, w, attT, early, norm_row, ctx):
    rows = dy.shape[0]
    mine = D // ctx
    outs = (
        ((rows, D), f32),
        ((ctx, HEADS // ctx, HD, rows), bf16),
        ((ctx // 2, mine, D), f32),
        ((ctx // 2 * mine + 2 * early.shape[0], D), bf16),
        (early.shape, f32),
    )
    return one_step(
        functools.partial(branch_kernel, norm_row),
        "branch_back",
        outs,
        (ci, back, slot, dy, middle, gain, w, attT, early),
        [pltpu.VMEM((D, D), f32)],
        2 * rows * D * (back.shape[0] + 2 * D),
    )


def go_kernel(me_ref, keep_ref, got_ref, small_ref, own_ref, send_ref, sum_ref, acc):
    nx, w, _ = keep_ref.shape
    for x in range(nx):
        acc[x] = keep_ref[x] + got_ref[x * w : (x + 1) * w].astype(f32)
    small = small_ref[...] + sum_halves(got_ref[nx * w :])
    sum_ref[...] = small
    own_ref[...] = acc[me_ref[0]]
    send_ref[:w] = acc[1 - me_ref[0]].astype(bf16)
    send_ref[w:] = halves_of(small)


def go_step(xi, keep, got, small):
    w = keep.shape[1]
    outs = (((w, D), f32), ((w + 2 * small.shape[0], D), bf16), (small.shape, f32))
    return one_step(go_kernel, "go_step", outs, (xi, keep, got, small), [pltpu.VMEM(keep.shape, f32)], 0)


def weight_rows_kernel(half_ref, dT_ref, normed_ref, go_ref, got_ref, early_ref, keep_ref, send_ref, small_ref, acc):
    n = dT_ref.shape[0]
    w = go_ref.shape[0]
    half = keep_ref.shape[0]
    acc[:n] = dg(dT_ref[...], normed_ref[...], 1, 0)
    acc[n:] = go_ref[...] + got_ref[:w].astype(f32)
    small = early_ref[...] + sum_halves(got_ref[w:])
    small_ref[...] = small
    a = pl.multiple_of(half_ref[0] * half, half)
    b = pl.multiple_of((1 - half_ref[0]) * half, half)
    keep_ref[...] = acc[pl.ds(a, half)]
    send_ref[:half] = acc[pl.ds(b, half)].astype(bf16)
    send_ref[half:] = halves_of(small)


def weight_rows(half, dT, normed, go, got, small):
    rows = dT.shape[0] + go.shape[0]
    outs = (((rows // 2, D), f32), ((rows // 2 + 2 * small.shape[0], D), bf16), (small.shape, f32))
    return one_step(
        weight_rows_kernel,
        "weight_rows",
        outs,
        (half, dT, normed, go, got, small),
        [pltpu.VMEM((rows, D), f32)],
        2 * dT.size * D,
    )


def share_kernel(me_ref, half_ref, got_ref, early_ref, own_ref, *refs):
    dp = len(refs) - 1
    sends, small_ref, acc = refs[: dp - 1], refs[dp - 1], refs[dp]
    half = half_ref.shape[0]
    w = half // dp
    acc[...] = half_ref[...] + got_ref[:half].astype(f32)
    small = early_ref[...] + sum_halves(got_ref[half:])
    small_ref[...] = small

    def share(step):
        return acc[pl.ds(pl.multiple_of(lax.rem(me_ref[0] + step, dp) * w, w), w)]

    own_ref[...] = share(0)
    for step in range(1, dp):
        sends[step - 1][:w] = share(step).astype(bf16)
        sends[step - 1][w:] = halves_of(small)


def share_step(zi, half, got, small, dp):
    w = half.shape[0] // dp
    outs = (((w, D), f32),) + (((w + 2 * small.shape[0], D), bf16),) * (dp - 1) + ((small.shape, f32),)
    return one_step(
        functools.partial(share_kernel),
        "share_step",
        outs,
        (zi, half, got, small),
        [pltpu.VMEM(half.shape, f32)],
        0,
    )


SIDE = tuple((core, over, begin) for core in range(2) for over in range(2) for begin in range(2))


def finish_kernel(dp, side, me_ref, *refs):
    layout = SIDE
    n = len(layout)
    pieces, weights, scale_ref, before_ref = refs[:n], refs[n : n + 3], refs[n + 3], refs[n + 4]
    outs, row_ref = refs[-11:-7], refs[-7]
    got, wide, held, in_sem, out_sem, w_sem = refs[-6:]
    mine = D // 4
    rows = 2 * mine // dp
    copies = []
    for k, (core, over, begin) in enumerate(layout):
        first = (over ^ me_ref[1]) * (2 * mine) + (core ^ me_ref[2]) * mine
        for i in range(pieces[k].shape[0] // rows):
            row = lax.rem(me_ref[0] + dp - begin * (dp // 2) - i, dp) * rows
            copy = pltpu.make_async_copy(
                pieces[k].at[pl.ds(i * rows, rows)],
                got.at[lax.div(row, mine), pl.ds(pl.multiple_of(first + lax.rem(row, mine), rows), rows)],
                in_sem.at[k, i],
            )
            copy.start()
            copies.append(copy)

    def put(pair):
        loads = [pltpu.make_async_copy(weights[p], held.at[k], w_sem.at[k]) for k, p in enumerate(pair) if p < 3]
        for copy in loads:
            copy.start()
        for copy in copies + loads:
            copy.wait()
        total = jnp.zeros((D, 1), f32)
        backs = []
        for k in (1, 0):
            if pair[k] < 3:
                g = got[k].T.astype(f32)
                total = total + jnp.sum(g * held[k].astype(f32), axis=1, keepdims=True)
            else:
                g = got[k].astype(f32)
            wide[k] = g
            back = pltpu.make_async_copy(wide.at[k], outs[pair[k]], out_sem.at[k])
            back.start()
            backs.append(back)
        row = jnp.broadcast_to(total, (D, 128)).T[:1]
        row_ref[...] = ((before_ref[...] + row) / scale_ref[...])[0] if side else row
        for back in backs:
            back.wait()

    y = lax.rem(me_ref[3] + side, 2)

    @pl.when(y == 0)
    def _():
        put((0, 1))

    @pl.when(y == 1)
    def _():
        put((2, 3))


def finish(me, pieces, weights, scale, side, so_far, dp):
    whole = jax.ShapeDtypeStruct((D, D), f32)
    anywhere = pl.BlockSpec(memory_space=pl.ANY)
    row = pl.BlockSpec((1, D), lambda i, p: (0, 0))
    args = [*pieces, *weights, scale, so_far[4] if side else scale]
    specs = [anywhere] * (len(args) - 2) + [row, row]
    alias = {}
    if side:
        alias = {1 + len(args) + p: p for p in range(4)}
        args += list(so_far[:4])
        specs += [anywhere] * 4
    return pl.pallas_call(
        functools.partial(finish_kernel, dp, side),
        out_shape=(whole,) * 4 + (jax.ShapeDtypeStruct((D,) if side else (1, D), f32),),
        grid_spec=pltpu.PrefetchScalarGridSpec(
            num_scalar_prefetch=1,
            grid=(1,),
            in_specs=specs,
            out_specs=(anywhere,) * 4 + (pl.BlockSpec((D,), lambda i, p: (0,)) if side else row,),
            scratch_shapes=[
                pltpu.VMEM((2, D, D), bf16),
                pltpu.VMEM((2, D, D), f32),
                pltpu.VMEM((2, D, D), bf16),
                pltpu.SemaphoreType.DMA((len(pieces), dp)),
                pltpu.SemaphoreType.DMA((2,)),
                pltpu.SemaphoreType.DMA((2,)),
            ],
        ),
        input_output_aliases=alias,
        compiler_params=pltpu.CompilerParams(vmem_limit_bytes=VMEM),
        cost_estimate=pl.CostEstimate(flops=4 * D * D, bytes_accessed=16 * D * D, transcendentals=0),
        name=f"finish{side}",
    )(me, *args)


def swap(v, axis):
    return lax.ppermute(v, axis, [(0, 1), (1, 0)])


def shift(v, axis, step):
    n = lax.axis_size(axis)
    return lax.ppermute(v, axis, [(i, (i + step) % n) for i in range(n)])


def at(v, index):
    return lax.dynamic_index_in_dim(v, index, 0, keepdims=False)


def one(v):
    v = v.astype(f32)
    n = v.shape[0] // 2
    return v[:n] + v[n:]


def add_pair(v):
    return v + (swap(v, "expert") if lax.axis_size("expert") == 2 else lax.psum(v, "expert") - v)


def add_shifts(v):
    out = v
    for s in range(1, lax.axis_size("dp")):
        out = out + shift(v, "dp", s)
    return out


def index(i):
    return i.astype(jnp.int32).reshape(1)


def tie(*arrays):
    return lax.optimization_barrier(arrays)


def normal_form(v):
    centred = v - jnp.mean(v, axis=-1, keepdims=True)
    rstd = lax.rsqrt(jnp.mean(centred * centred, axis=-1, keepdims=True) + norm_eps)
    return centred * rstd, rstd


def norm_back(dn, xh, rstd):
    return rstd * (dn - jnp.mean(dn, axis=-1, keepdims=True) - xh * jnp.mean(dn * xh, axis=-1, keepdims=True))


def per_device(
    tokens,
    cotangent,
    routes,
    norm1_gain,
    w_query,
    w_key,
    w_value,
    w_output,
    norm2_gain,
    w_router,
    w_in,
    w_out,
):
    rows = tokens.shape[1]
    nx, owners, dp = lax.axis_size("x"), lax.axis_size("expert"), lax.axis_size("dp")
    xi, ci, ei = lax.axis_index("x"), lax.axis_index("core"), lax.axis_index("expert")
    ctx = 2 * nx
    ctx_i = xi * 2 + ci
    length = ctx * rows
    experts = w_router.shape[1]
    cap = 2 * rows // experts
    mine = D // ctx
    heads = mine // HD
    expert_id = ei * nx + xi
    pick = jnp.stack([xi, ci, expert_id]).astype(jnp.int32)

    tok = tokens.reshape(rows, D)
    flat = tok.astype(f32)
    other = swap(tok, "x")
    near = swap(tok, "core")

    route = routes.reshape(rows)
    hot = (route[:, None] == jnp.arange(128, dtype=jnp.int32)[None, :]).astype(f32)
    lower = jnp.arange(rows)[:, None] >= jnp.arange(rows)[None, :]
    before = dg(lower.astype(bf16), hot.astype(bf16), 1, 0)
    rank = (jnp.sum(before * hot, axis=1) - 1.0).astype(jnp.int32)
    slot = ((route % nx) * owners + route // nx) * cap + rank
    spread = (jnp.arange(experts * cap, dtype=jnp.int32)[:, None] == slot[None, :]).astype(bf16)

    def pack(v):
        return dg(spread, v, 1, 0).astype(bf16).reshape(nx * owners, cap, D)

    def trade(v):
        v = lax.all_to_all(v.reshape(nx * owners, cap, D), ("x", "expert"), split_axis=0, concat_axis=0, tiled=True)
        return v.reshape(-1, D)

    def turn(v):
        return lax.all_to_all(v, ("x", "core"), split_axis=0, concat_axis=0, tiled=True)

    def cut(w):
        return lax.dynamic_slice(w, (0, ctx_i * mine), (D, mine))

    w_own = jnp.concatenate([cut(w_query), cut(w_key), cut(w_value)], axis=1)
    gain1 = norm1_gain.reshape(1, D)
    dy_low = cotangent.reshape(rows, D)
    dy = dy_low.astype(f32)
    wr = lax.dynamic_slice(w_router, (0, expert_id), (D, 1)).astype(f32).reshape(1, D)
    counts = jnp.sum(hot, axis=0, keepdims=True)
    counts = counts + swap(counts, "core")
    counts = add_pair(counts)
    so_far = project([ctx_i], [tok], gain1, w_own, ctx, None)
    counts, dy_packed, *so_far = tie(counts, pack(dy_low), *so_far)
    so_far = project([ctx_i ^ 1], [near], gain1, w_own, ctx, so_far)
    other, dy_packed, *so_far = tie(other, dy_packed, *so_far)
    far = swap(other, "core")
    dy_rows = trade(dy_packed)
    normed_all, qkvT, kv = project([ctx_i ^ 2, ctx_i ^ 3], [other, far], gain1, w_own, ctx, so_far)
    oT, osend, lse = attend(qkvT, kv, ctx)
    osend, dy_rows, counts = tie(osend, dy_rows, counts)
    attT = turn(osend)
    counts = add_shifts(counts)
    attT, counts = tie(attT, counts)
    counts = counts + swap(counts, "x")
    attT = attT.reshape(D, rows)
    mean_load = rows * ctx * dp * owners / experts
    gain2 = norm2_gain.reshape(1, D)
    middle, second, packed = middle_step(attT, tok, w_output, gain2, slot[None], nx * owners, cap)
    gating = jax.nn.sigmoid(jnp.sum(hot[:, :experts] * dg(second, w_router, 1, 0), axis=1))

    up = expert_up(pick, dy_rows, w_out)
    sig = jnp.pad(jnp.sum(hot[:, :experts] * gating[:, None], axis=0), (0, D - experts))
    counts, packed = tie(counts, packed)
    x_rows = trade(packed)
    x_rows, gating, sig, slot, gain2 = tie(x_rows, gating, sig, slot[None], gain2)
    active, grad_hidden, back_rows, router_row, gate = expert_mid(pick, x_rows, up, w_in, wr, counts, mean_load)
    returned = trade(back_rows)
    keep, send, produced = expert_grads(pick, x_rows, dy_rows, gate, active, grad_hidden, w_out, dp, nx)
    returned, keep, send, produced = tie(returned, keep, send, produced)
    taken = swap(send, "core")
    zi = lax.axis_index("dp")

    def chunk(i):
        return at(keep, (i + dp) % dp).astype(f32) + at(taken, (i + dp) % dp).astype(f32)

    def ring(moving, step):
        return (shift(moving, "dp", 1).astype(f32) + chunk(zi - 2 - step)).astype(bf16)

    def side(v, x):
        return lax.dynamic_index_in_dim(v, x, 1, keepdims=False)

    router_rows = (jnp.arange(experts) == expert_id).astype(f32)[:, None] * router_row
    small = jnp.concatenate([router_rows, jnp.zeros((1, D), f32), sig[None]], axis=0)
    small = jnp.pad(small, ((0, -small.shape[0] % 8), (0, 0)))
    grad_middle, heads_grad, go, go_send, small = branch_back(
        index(ci), returned, slot, dy_low, middle, gain2, w_output, attT, small, experts, ctx
    )
    do = turn(heads_grad)

    moving = ring(chunk(zi - 1).astype(bf16), 0)
    go_got = swap(go_send, "core")
    go, go_send, small = go_step(index(xi), go, go_got, small)
    do, go_send = tie(do, go_send)
    go_got = swap(go_send, "x")

    so_far = attend_back(qkvT, kv, do, 0, oT, lse, 0, None)
    produced, go_got, *so_far = tie(produced, go_got, *so_far)
    went_back = trade(produced)
    so_far = attend_back(qkvT, kv, do, 1, oT, lse, 1, so_far)
    moving, *so_far = tie(moving, *so_far)
    moving = ring(moving, 1)
    for h in range(2, heads):
        so_far = attend_back(qkvT, kv, do, h, oT, lse, h, so_far)
    went_back, dT, dsend = tie(went_back, *so_far)
    output = (middle + gating[:, None] * dg(spread, went_back, 0, 0)).astype(bf16)

    ei2 = ei if owners == 2 else jnp.zeros_like(ei)
    half, send, small = weight_rows(index(ei2), dT.reshape(3 * mine, length), normed_all, go, go_got, small)
    dsend, send = tie(dsend, send)
    got = turn(dsend)
    if owners == 2:
        gift = swap(send, "expert")
        gift, moving = tie(gift, moving)
        halves = [(half, gift)]
    else:
        cut_at = half.shape[0]
        small = lax.psum(small, "expert")
        nothing = jnp.zeros_like(send)
        halves = [(lax.psum(half, "expert"), nothing), (lax.psum(send[:cut_at].astype(f32), "expert"), nothing)]
    pieces = []
    for part, gift in halves:
        share, *gifts, more = share_step(index(zi), part, gift, small, dp)
        gifts = [shift(gift, "dp", step + 1) for step, gift in enumerate(gifts)]
        for gift in gifts:
            more = more + one(gift[share.shape[0] :])
            share = share + gift[: share.shape[0]].astype(f32)
        share = share.astype(bf16)
        shares = [share] + [shift(share, "dp", step) for step in range(1, dp)]
        pieces.append([jnp.concatenate(shares[k : k + dp // 2], axis=0) for k in range(0, dp, dp // 2)])
    small = more
    output, keep, taken = tie(output, keep, taken)
    crossed = swap(side(chunk(zi), 1 - xi).astype(bf16), "x")
    for step in range(2, dp - 2):
        moving = ring(moving, step)
    moving, crossed, *pieces = tie(moving, crossed, *pieces)
    own = shift(side(moving, xi), "dp", 1)
    route_on = [(z * nx + x, (z + 1) % dp * nx + 1 - x) for z in range(dp) for x in range(nx)]
    theirs = side(moving, 1 - xi)

    grad_normed = 0.0
    for p, w in enumerate((w_query, w_key, w_value)):
        grad_normed = grad_normed + dg(got[:, p].reshape(D, rows), w, 0, 1)
    xh1, rstd1 = normal_form(flat)
    grad_tokens = grad_middle + norm_back(grad_normed * norm1_gain, xh1, rstd1)

    near_pieces = pieces[0]
    beyond = [swap(piece, "x") for piece in near_pieces]
    if owners == 2:
        across = [swap(piece, "expert") for piece in near_pieces]
    else:
        across = list(pieces[1])
    theirs, *rest = tie(theirs, *beyond, *across)
    beyond, across = rest[:2], rest[2:]
    moved = lax.ppermute(theirs, ("dp", "x"), route_on)
    if owners == 2:
        corner = [swap(piece, "expert") for piece in beyond]
    else:
        corner = [swap(piece, "x") for piece in across]
    me = jnp.stack([zi, xi, ci, ei2]).astype(jnp.int32)
    projections = (w_query, w_key, w_value)
    near_pieces = near_pieces + beyond
    near_pieces += [swap(piece, "core") for piece in near_pieces]
    placed = finish(me, near_pieces, projections, gain1, 0, None, dp)
    grad_tokens, *corner = tie(grad_tokens, *corner, *placed)
    corner, placed = corner[:2], corner[2:]
    far_pieces = across + corner
    far_pieces += [swap(piece, "core") for piece in far_pieces]
    *grads, grad_norm1 = finish(me, far_pieces, projections, gain1, 1, placed, dp)
    own, moved, grad_norm1 = tie(own, moved, grad_norm1)

    own = own.astype(f32) + side(chunk(zi), xi)
    moved = moved.astype(f32) + crossed.astype(f32)
    first, latter = jnp.where(xi == 0, own, moved), jnp.where(xi == 0, moved, own)
    both = jnp.stack([first, latter], axis=1)
    grad_in = jnp.swapaxes(both[0], 1, 2)
    grad_out = both[1]

    grad_router = jnp.transpose(small[:experts])
    grad_norm2 = small[experts]
    total_sig = small[experts + 1, :experts]
    counts = counts[0, :experts]
    balance = balance_weight * jnp.sum((counts - mean_load) / mean_load * total_sig) / mean_load

    return (
        output.reshape(1, rows, D),
        grad_tokens.reshape(1, rows, D),
        grad_norm1,
        grads[0],
        grads[1],
        grads[2],
        grads[3],
        grad_norm2,
        grad_router,
        grad_in,
        grad_out,
        balance,
    )


def solution(mesh):
    dp, ctx, owners = mesh.shape["dp"], mesh.shape["ctx"], mesh.shape["expert"]
    split = Mesh(mesh.devices.reshape(dp, ctx // 2, 2, owners), ("dp", "x", "core", "expert"))
    token = P(("dp", "expert"), ("x", "core"), None)
    return jax.shard_map(
        per_device,
        mesh=split,
        in_specs=(token, token, token, P(), P(), P(), P(), P(), P(), P(), P("expert"), P("expert")),
        out_specs=(
            token,
            token,
            P(),
            P(),
            P(),
            P(),
            P(),
            P(),
            P(),
            P("expert", None, ("dp", "x", "core")),
            P("expert", ("dp", "x", "core"), None),
            P(),
        ),
        check_vma=False,
    )
```
